32 devices in a mesh: seq: 16 (over z, y, x), rep: 2 (over core).
Axes of the slice: x: 2, y: 2, z: 4, core: 2. Of those that a mesh axis runs over, the one named last changes fastest.
Arguments:
- tokens: bfloat16 [16, 2, 1024, 768], P('rep', None, 'seq'), may hold values from -6 to 6
- mixer_gain: bfloat16 [768], P(('seq', 'rep')), may hold values from 0.5 to 1.5
- mixer_bias: bfloat16 [768], P(('seq', 'rep')), may hold values from -1.75 to 1.75
- key_blend: bfloat16 [768], P(('seq', 'rep')), may hold values from 0.019897461 to 0.3984375
- value_blend: bfloat16 [768], P(('seq', 'rep')), may hold values from 0.019897461 to 0.3984375
- gate_blend: bfloat16 [768], P(('seq', 'rep')), may hold values from 0.019897461 to 0.3984375
- time_decay: bfloat16 [768], P(('seq', 'rep')), may hold values from -10 to -2.796875
- time_first: bfloat16 [768], P(('seq', 'rep')), may hold values from -1 to 1
- key_weight: bfloat16 [768, 768], P(('seq', 'rep')), may hold values from -0.21875 to 0.21875
- value_weight: bfloat16 [768, 768], P(('seq', 'rep')), may hold values from -0.875 to 0.875
- gate_weight: bfloat16 [768, 768], P(('seq', 'rep')), may hold values from -0.21875 to 0.21875
- output_weight: bfloat16 [768, 768], P(('seq', 'rep')), may hold values from -0.875 to 0.875
- channel_gain: bfloat16 [768], P(('seq', 'rep')), may hold values from 0.5 to 1.5
- channel_bias: bfloat16 [768], P(('seq', 'rep')), may hold values from -1.75 to 1.75
- hidden_blend: bfloat16 [768], P(('seq', 'rep')), may hold values from 0.049804688 to 0.94921875
- screen_blend: bfloat16 [768], P(('seq', 'rep')), may hold values from 0.049804688 to 0.94921875
- hidden_weight: bfloat16 [768, 3072], P(('seq', 'rep')), may hold values from -0.21875 to 0.21875
- screen_weight: bfloat16 [768, 768], P(('seq', 'rep')), may hold values from -0.21875 to 0.21875
- return_weight: bfloat16 [3072, 768], P(('seq', 'rep')), may hold values from -0.109375 to 0.109375
- cotangent: bfloat16 [16, 2, 1024, 768], P('rep', None, 'seq'), may hold values from -6 to 6
Outputs:
- output: bfloat16 [16, 2, 1024, 768], P('rep', None, 'seq')
- input_grad: float32 [16, 2, 1024, 768], P('rep', None, 'seq')
- final_numerator: float32 [16, 768], P('rep', 'seq')
- final_denominator: float32 [16, 768], P('rep', 'seq')
- final_maximum: float32 [16, 768], P('rep', 'seq')
- mixer_gain_grad: float32 [768], P(('seq', 'rep'))
- mixer_bias_grad: float32 [768], P(('seq', 'rep'))
- key_blend_grad: float32 [768], P(('seq', 'rep'))
- value_blend_grad: float32 [768], P(('seq', 'rep'))
- gate_blend_grad: float32 [768], P(('seq', 'rep'))
- time_decay_grad: float32 [768], P(('seq', 'rep'))
- time_first_gradient: float32 [768], P(('seq', 'rep'))
- key_weight_grad: float32 [768, 768], P(('seq', 'rep'))
- value_weight_grad: float32 [768, 768], P(('seq', 'rep'))
- gate_weight_grad: float32 [768, 768], P(('seq', 'rep'))
- output_weight_grad: float32 [768, 768], P(('seq', 'rep'))
- channel_gain_grad: float32 [768], P(('seq', 'rep'))
- channel_bias_grad: float32 [768], P(('seq', 'rep'))
- hidden_blend_grad: float32 [768], P(('seq', 'rep'))
- screen_blend_grad: float32 [768], P(('seq', 'rep'))
- hidden_weight_grad: float32 [768, 3072], P(('seq', 'rep'))
- screen_weight_grad: float32 [768, 768], P(('seq', 'rep'))
- return_weight_grad: float32 [3072, 768], P(('seq', 'rep'))
The draws below stay inside these ranges and needn't reach their ends.
All inputs are finite; a program needn't handle non-finite values.
Results may differ from the reference program's by a relative error of at most 0.012.
Values may be sent and summed in bfloat16 or wider, within the bound.
A program may use at most 320 MiB of HBM per device.

```python
import jax
import jax.numpy as jnp
from jax import lax

D = 768
FF = 3072
STRETCHES = 2
STRETCH_LEN = 1024
SEQS = 16


def shard_levels(own_key, dims, pieces, least, largest):
    gain, own = 1.0, jax.random.fold_in(own_key, 6)
    for dim, blocks in pieces:
        steps = jnp.exp(jax.random.uniform(jax.random.fold_in(own, dim), (blocks,), jnp.float32, least / len(pieces), largest / len(pieces)))
        gain = gain * jnp.repeat(steps, dims[dim] // blocks).reshape([-1 if axis == dim else 1 for axis in range(len(dims))])
    return gain


def gaussian(key, shape, spread, most, shards=(), held_as=jnp.bfloat16):
    values = jax.random.normal(key, shape, jnp.float32) * spread
    if len(shards) > 0:
        values = shard_levels(key, shape, shards, -0.22, 0.18) * values
    return jnp.clip(values, min=-most, max=most).astype(held_as)


def setup_inputs(seed: int = 0) -> dict:
    splits = jax.random.split(jax.random.key(seed), 21)
    return {
        "tokens": gaussian(splits[0], (SEQS, STRETCHES, STRETCH_LEN, D), 1.0, 6.0, ((0, 2), (2, 16))),
        "mixer_gain": jnp.clip(1.0 + 0.1 * jax.random.normal(splits[1], (D,), jnp.float32), 0.5, 1.5).astype(jnp.bfloat16),
        "mixer_bias": gaussian(splits[2], (D,), 0.3, 1.75, ((0, 32),)),
        "key_blend": jnp.clip(0.019897461 + 0.37854004 * jax.random.uniform(splits[3], (D,), jnp.float32) ** shard_levels(splits[3], (D,), ((0, 32),), -0.2, 0.2), 0.019897461, 0.3984375).astype(jnp.bfloat16),
        "value_blend": jnp.clip(0.019897461 + 0.37854004 * jax.random.uniform(splits[4], (D,), jnp.float32) ** shard_levels(splits[4], (D,), ((0, 32),), -0.2, 0.2), 0.019897461, 0.3984375).astype(jnp.bfloat16),
        "gate_blend": jnp.clip(0.019897461 + 0.37854004 * jax.random.uniform(splits[5], (D,), jnp.float32) ** shard_levels(splits[5], (D,), ((0, 32),), -0.2, 0.2), 0.019897461, 0.3984375).astype(jnp.bfloat16),
        "time_decay": jnp.clip(-10.0 + 7.203125 * jax.random.uniform(splits[6], (D,), jnp.float32) ** shard_levels(splits[6], (D,), ((0, 32),), -0.2, 0.2), -10.0, -2.796875).astype(jnp.bfloat16),
        "time_first": jnp.clip(jax.random.uniform(splits[7], (D,), jnp.float32, -1.0, 1.0) * shard_levels(splits[7], (D,), ((0, 32),), -0.4, 0.0), -1.0, 1.0).astype(jnp.bfloat16),
        "key_weight": gaussian(splits[8], (D, D), D ** -0.5, 0.21875, ((0, 32),)),
        "value_weight": gaussian(splits[9], (D, D), (D // 16) ** -0.5, 0.875, ((0, 32),)),
        "gate_weight": gaussian(splits[10], (D, D), D ** -0.5, 0.21875, ((0, 32),)),
        "output_weight": gaussian(splits[11], (D, D), (D // 16) ** -0.5, 0.875, ((0, 32),)),
        "channel_gain": jnp.clip(1.0 + 0.1 * jax.random.normal(splits[12], (D,), jnp.float32), 0.5, 1.5).astype(jnp.bfloat16),
        "channel_bias": gaussian(splits[13], (D,), 0.3, 1.75, ((0, 32),)),
        "hidden_blend": jnp.clip(0.049804688 + 0.89941406 * jax.random.uniform(splits[14], (D,), jnp.float32) ** shard_levels(splits[14], (D,), ((0, 32),), -0.2, 0.2), 0.049804688, 0.94921875).astype(jnp.bfloat16),
        "screen_blend": jnp.clip(0.049804688 + 0.89941406 * jax.random.uniform(splits[15], (D,), jnp.float32) ** shard_levels(splits[15], (D,), ((0, 32),), -0.2, 0.2), 0.049804688, 0.94921875).astype(jnp.bfloat16),
        "hidden_weight": gaussian(splits[16], (D, FF), D ** -0.5, 0.21875, ((0, 32),)),
        "screen_weight": gaussian(splits[17], (D, D), D ** -0.5, 0.21875, ((0, 32),)),
        "return_weight": gaussian(splits[18], (FF, D), FF ** -0.5, 0.109375, ((0, 32),)),
        "cotangent": gaussian(splits[19], (SEQS, STRETCHES, STRETCH_LEN, D), 1.0, 6.0, ((0, 2), (2, 16))),
    }


@jax.custom_vjp
def low(v):
    return lax.optimization_barrier(v.astype(jnp.bfloat16)).astype(jnp.float32)

@jax.custom_vjp
def low_back(v):
    return v

def low_keep(v):
    return (low(v), None)

def low_pass(kept, grad):
    return (grad,)

def back_keep(v):
    return (v, None)

def back_low(kept, grad):
    return (low(grad),)
low.defvjp(low_keep, low_pass)
low_back.defvjp(back_keep, back_low)
highest = lax.Precision.HIGHEST
norm_eps = 1e-05

def product(operand, matrix):
    return jnp.dot(operand, matrix, precision=highest, preferred_element_type=jnp.float32)

def layer_norm(values, norm_gain, norm_bias):
    centred = values - lax.optimization_barrier(jnp.mean(values, -1, keepdims=True))
    inverse = lax.rsqrt(lax.optimization_barrier(jnp.mean(centred * centred, -1, keepdims=True)) + norm_eps)
    return centred * inverse * norm_gain + norm_bias

def blend(current_element, portion):
    before = jnp.concatenate([jnp.zeros_like(current_element[:1]), current_element[:-1]], 0)
    return before + (current_element - before) * portion

def sequential_sweep(address_matrix_tile, payload_matrix_tile, fading_multiplier, temporal_reward_exponent):
    retention = jnp.exp(-fading_multiplier)

    @jax.checkpoint
    def advance(running_state, step_input):
        dividend_sum, normalizer_sum = running_state
        address_current, payload_current = step_input
        reward_scaled_entry = jnp.exp(temporal_reward_exponent + address_current)
        blended_input = (dividend_sum + reward_scaled_entry * payload_current) / (normalizer_sum + reward_scaled_entry)
        expansion_ratio = jnp.exp(address_current)
        return ((retention * dividend_sum + expansion_ratio * payload_current, retention * normalizer_sum + expansion_ratio), blended_input)
    zero_state = jnp.zeros_like(address_matrix_tile[0])
    final_state, mixtures = lax.scan(advance, (zero_state, zero_state), (address_matrix_tile, payload_matrix_tile))
    return mixtures

def final_states(address_matrix_tile, payload_matrix_tile, fading_multiplier):
    length = address_matrix_tile.shape[0]
    distance = length - 1.0 - jnp.arange(length, dtype=jnp.float32)
    shifted = address_matrix_tile - distance[:, None] * fading_multiplier
    summit = lax.optimization_barrier(jnp.max(shifted, 0))
    scaled_terms = jnp.exp(shifted - summit)
    return (lax.optimization_barrier(jnp.sum(scaled_terms * payload_matrix_tile, 0)), lax.optimization_barrier(jnp.sum(scaled_terms, 0)), summit)

def layer(inputs, mixer_gain, mixer_bias, key_blend, value_blend, gate_blend, time_decay, time_first, key_weight, value_weight, gate_weight, output_weight, channel_gain, channel_bias, hidden_blend, screen_blend, hidden_weight, screen_weight, return_weight):
    normed_one = layer_norm(inputs, mixer_gain, mixer_bias)
    key_input = low(blend(normed_one, key_blend))
    value_input = low(blend(normed_one, value_blend))
    gate_input = low(blend(normed_one, gate_blend))
    address_matrix_tile = low_back(low(product(key_input, key_weight)))
    payload_matrix_tile = low_back(low(product(value_input, value_weight)))
    gate_logit = low_back(product(gate_input, gate_weight))
    fading_multiplier = jnp.exp(time_decay)
    blended_input = low_back(low(sequential_sweep(address_matrix_tile, payload_matrix_tile, fading_multiplier, time_first)))
    finals = final_states(address_matrix_tile, payload_matrix_tile, fading_multiplier)
    gated = low(jax.nn.sigmoid(gate_logit) * blended_input)
    residual = inputs + low_back(product(gated, output_weight))
    normed_two = layer_norm(residual, channel_gain, channel_bias)
    hidden_input = low(blend(normed_two, hidden_blend))
    screen_input = low(blend(normed_two, screen_blend))
    hidden_logit = low_back(product(hidden_input, hidden_weight))
    hidden_act = low(jnp.square(jnp.maximum(hidden_logit, 0.0)))
    returned = low_back(product(hidden_act, return_weight))
    screen_logit = low_back(product(screen_input, screen_weight))
    return (residual + jax.nn.sigmoid(screen_logit) * returned, finals)

def reference(tokens, mixer_gain, mixer_bias, key_blend, value_blend, gate_blend, time_decay, time_first, key_weight, value_weight, gate_weight, output_weight, channel_gain, channel_bias, hidden_blend, screen_blend, hidden_weight, screen_weight, return_weight, cotangent):
    weights = (mixer_gain, mixer_bias, key_blend, value_blend, gate_blend, time_decay, time_first, key_weight, value_weight, gate_weight, output_weight, channel_gain, channel_bias, hidden_blend, screen_blend, hidden_weight, screen_weight, return_weight)
    widened = tuple((member.astype(jnp.float32) for member in weights))

    def per_sequence(cumulative_sums, step_input):
        sequence, seed_grad = step_input
        feature_count = sequence.shape[-1]
        flat_input = sequence.reshape(-1, feature_count).astype(jnp.float32)
        result, pullback, finals = jax.vjp(layer, flat_input, *widened, has_aux=True)
        grads = pullback(seed_grad.reshape(-1, feature_count).astype(jnp.float32))
        cumulative_sums = tuple((running + fresh for running, fresh in zip(cumulative_sums, grads[1:])))
        return (cumulative_sums, (result.astype(jnp.bfloat16).reshape(sequence.shape), grads[0].reshape(sequence.shape), finals[0], finals[1], finals[2]))
    start_totals = tuple((jnp.zeros_like(member) for member in widened))
    cumulative_sums, stacked = lax.scan(per_sequence, start_totals, (tokens, cotangent))
    outputs, input_grads, final_numerator, final_denominator, final_maximum = stacked
    return (outputs, input_grads, final_numerator, final_denominator, final_maximum, cumulative_sums[0], cumulative_sums[1], cumulative_sums[2], cumulative_sums[3], cumulative_sums[4], cumulative_sums[5], cumulative_sums[6], cumulative_sums[7], cumulative_sums[8], cumulative_sums[9], cumulative_sums[10], cumulative_sums[11], cumulative_sums[12], cumulative_sums[13], cumulative_sums[14], cumulative_sums[15], cumulative_sums[16], cumulative_sums[17])
```

```python
import jax
import jax.numpy as jnp
from jax import lax
from jax.experimental import pallas as pl
from jax.experimental.pallas import tpu as pltpu
from jax.sharding import PartitionSpec as P

f32 = jnp.float32
bf16 = jnp.bfloat16
norm_eps = 1e-05
both = ("seq", "rep")


def mm(left, right):
    return jnp.dot(left, right, preferred_element_type=f32)


def mm_nt(left, right):
    return lax.dot_general(left, right, (((1,), (1,)), ((), ())), preferred_element_type=f32)


def mm_tn(left, right):
    return lax.dot_general(left, right, (((0,), (0,)), ((), ())), preferred_element_type=f32)


def normalise(values):
    centred = values - jnp.mean(values, -1, keepdims=True)
    inverse = lax.rsqrt(jnp.mean(centred * centred, -1, keepdims=True) + norm_eps)
    return centred * inverse, inverse


def norm_back(upstream, scaled, inverse, gain):
    inner = upstream * gain
    centred = inner - jnp.mean(inner, -1, keepdims=True)
    return inverse * (centred - scaled * jnp.mean(inner * scaled, -1, keepdims=True))


def ring(value, steps):
    count = lax.axis_size("seq")
    return lax.ppermute(value, "seq", [(i, (i + steps) % count) for i in range(count)])


def entering(last, spot):
    got = ring(last, 1)
    pairs = got.reshape(-1, 2, got.shape[-1])
    wrapped = jnp.concatenate([jnp.zeros_like(pairs[:, :1]), pairs[:, :1]], 1)
    return jnp.where(spot == 0, wrapped, pairs).reshape(got.shape)


def leaving(first, spot):
    count = lax.axis_size("seq")
    got = ring(first, -1)
    pairs = got.reshape(-1, 2, got.shape[-1])
    wrapped = jnp.concatenate([pairs[:, 1:], jnp.zeros_like(pairs[:, :1])], 1)
    return jnp.where(spot == count - 1, wrapped, pairs).reshape(got.shape)


def forward_kernel(k_ref, v_ref, carry_ref, decay_ref, first_ref, num_ref, den_ref, mix_ref):
    keep = jnp.exp(-jnp.exp(decay_ref[...]))
    boost_rate = jnp.exp(first_ref[...])

    def step(t, state):
        num, den = state
        k = jnp.exp(k_ref[t].astype(f32))
        v = v_ref[t].astype(f32)
        boost = k * boost_rate
        num_ref[t] = num
        den_ref[t] = den
        mix_ref[t] = (num + boost * v) / (den + boost)
        return keep * num + k * v, keep * den + k

    lax.fori_loop(0, k_ref.shape[0], step, (carry_ref[0], carry_ref[1]))


def backward_kernel(
    k_ref, v_ref, num_ref, den_ref, mix_ref, grad_ref, carry_ref, decay_ref, first_ref,
    kg_ref, vg_ref, first_grad_ref, decay_grad_ref,
):
    keep = jnp.exp(-jnp.exp(decay_ref[...]))
    boost_rate = jnp.exp(first_ref[...])
    length = k_ref.shape[0]

    def step(i, state):
        adj_num, adj_den, first_sum, decay_sum = state
        t = length - 1 - i
        k = jnp.exp(k_ref[t].astype(f32))
        v = v_ref[t].astype(f32)
        boost = k * boost_rate
        num_grad = grad_ref[t].astype(f32) / (den_ref[t] + boost)
        den_grad = -num_grad * mix_ref[t]
        inner = boost * (v * num_grad + den_grad)
        kg_ref[t] = (k * (v * adj_num + adj_den) + inner).astype(bf16)
        vg_ref[t] = (k * adj_num + boost * num_grad).astype(bf16)
        first_sum = first_sum + inner
        decay_sum = decay_sum + num_ref[t] * adj_num + den_ref[t] * adj_den
        return keep * adj_num + num_grad, keep * adj_den + den_grad, first_sum, decay_sum

    zero = jnp.zeros_like(carry_ref[0])
    out = lax.fori_loop(0, length, step, (carry_ref[0], carry_ref[1], zero, zero))
    first_grad_ref[...] = out[2]
    decay_grad_ref[...] = out[3]


def call(kernel, shapes, *operands):
    space = pl.BlockSpec(memory_space=pltpu.VMEM)
    return pl.pallas_call(
        kernel,
        out_shape=[jax.ShapeDtypeStruct(s, t) for s, t in shapes],
        in_specs=[space] * len(operands),
        out_specs=[space] * len(shapes),
        compiler_params=pltpu.CompilerParams(vmem_limit_bytes=48 * 2**20),
    )(*operands)


def body(
    tokens, mixer_gain, mixer_bias, key_blend, value_blend, gate_blend, time_decay, time_first,
    key_weight, value_weight, gate_weight, output_weight, channel_gain, channel_bias,
    hidden_blend, screen_blend, hidden_weight, screen_weight, return_weight, cotangent,
):
    groups, stretches, span, width = tokens.shape
    count = lax.axis_size("seq")
    owners = count * lax.axis_size("rep")
    spot = lax.axis_index("seq")
    segs = groups * stretches
    rows = span * segs
    own = width // owners
    inner = hidden_weight.shape[1]
    parts = inner // width

    vectors = (
        mixer_gain, mixer_bias, key_blend, value_blend, gate_blend, time_decay, time_first,
        channel_gain, channel_bias, hidden_blend, screen_blend,
    )
    squares = (key_weight, value_weight, gate_weight, output_weight, screen_weight)
    packed = jnp.concatenate(
        squares + (hidden_weight.reshape(own * parts, width), return_weight), 0
    )
    packed = lax.all_gather(packed, both, axis=0)
    spread_vectors = lax.all_gather(jnp.stack(vectors), both, axis=0)
    spread_vectors = jnp.swapaxes(spread_vectors, 0, 1).reshape(len(vectors), width).astype(f32)
    (
        mixer_g, mixer_b, key_share, value_share, gate_share, decay_log, first_log,
        channel_g, channel_b, hidden_share, screen_share,
    ) = [spread_vectors[i][None] for i in range(len(vectors))]

    def piece(start, size, shape):
        return packed[:, start : start + size].reshape(shape)

    w_key, w_value, w_gate, w_output, w_screen = [
        piece(own * i, own, (width, width)) for i in range(5)
    ]
    w_hidden = piece(own * 5, own * parts, (width, inner))
    w_return = piece(own * (5 + parts), own * parts, (inner, width))

    def position_major(a):
        return jnp.transpose(a, (2, 0, 1, 3)).reshape(rows, width)

    def shifted(a, first):
        return jnp.concatenate([first, a[:-segs]], 0)

    x = position_major(tokens).astype(f32)
    n1, inv1 = normalise(x)
    one = n1 * mixer_g + mixer_b
    before = shifted(one, entering(one[-segs:], spot))
    spread_one = one - before
    key_in = (before + spread_one * key_share).astype(bf16)
    value_in = (before + spread_one * value_share).astype(bf16)
    gate_in = (before + spread_one * gate_share).astype(bf16)
    k = mm(key_in, w_key).astype(bf16)
    v = mm(value_in, w_value).astype(bf16)
    gate = jax.nn.sigmoid(mm(gate_in, w_gate))

    rate = jnp.exp(decay_log)
    cube = (span, segs, width)
    offsets = jnp.arange(span, dtype=f32)[:, None, None]
    kw = k.reshape(cube).astype(f32)
    vw = v.reshape(cube).astype(f32)
    shifted_key = kw - (span - 1.0 - offsets) * rate
    ends = jnp.exp(shifted_key)
    totals = jnp.stack([jnp.sum(ends * vw, 0), jnp.sum(ends, 0)])
    tops = jnp.max(shifted_key, 0)
    everyone = lax.all_gather(jnp.concatenate([totals, tops[None]]), "seq", axis=0)
    everyone = everyone.reshape(count, 3, groups, stretches, width)
    everyone = jnp.transpose(everyone, (3, 0, 1, 2, 4)).reshape(
        stretches * count, 3, groups, width
    )
    order = jnp.arange(stretches * count, dtype=f32)

    def weights_for(here):
        gap = here - 1.0 - order[:, None]
        return jnp.where(gap >= 0, jnp.exp(-jnp.maximum(gap, 0.0) * (span * rate)), 0.0)

    def carried(here):
        return jnp.sum(weights_for(here)[:, None, None, :] * everyone[:, :2], 0)

    carry = jnp.stack([carried(j * count + spot.astype(f32)) for j in range(stretches)], 2)
    carry = carry.reshape(2, segs, width)
    final = carried(float(stretches * count))
    far = (stretches * count - 1.0 - order)[:, None] * (span * rate)
    top = jnp.max(everyone[:, 2] - far[:, None, :], 0)
    slab = width // count

    def own_slab(a):
        return lax.dynamic_slice_in_dim(a, spot * slab, slab, 1)

    final_top = own_slab(top)
    scaling = jnp.exp(-final_top)
    final_num = own_slab(final[0]) * scaling
    final_den = own_slab(final[1]) * scaling

    num, den, mix_raw = call(
        forward_kernel, [(cube, f32)] * 3, k.reshape(cube), v.reshape(cube), carry,
        decay_log, first_log,
    )
    mix = mix_raw.reshape(rows, width).astype(bf16).astype(f32)
    gated = (gate * mix).astype(bf16)
    residual = x + mm(gated, w_output)
    n2, inv2 = normalise(residual)
    two = n2 * channel_g + channel_b
    before = shifted(two, entering(two[-segs:], spot))
    spread_two = two - before
    hidden_in = (before + spread_two * hidden_share).astype(bf16)
    screen_in = (before + spread_two * screen_share).astype(bf16)
    screen = jax.nn.sigmoid(mm(screen_in, w_screen))
    cot = position_major(cotangent).astype(f32)
    returned_grad = (cot * screen).astype(bf16)
    relu = jnp.maximum(mm(hidden_in, w_hidden), 0.0)
    act = jnp.square(relu).astype(bf16)
    returned = mm(act, w_return)
    output = (residual + screen * returned).astype(bf16)

    screen_grad = (cot * returned * screen * (1.0 - screen)).astype(bf16)
    hidden_grad = (mm_nt(returned_grad, w_return) * (2.0 * relu)).astype(bf16)
    dw_return = mm_tn(act, returned_grad)
    dw_hidden = mm_tn(hidden_in, hidden_grad)
    dw_screen = mm_tn(screen_in, screen_grad)
    hidden_back = mm_nt(hidden_grad, w_hidden)
    screen_back = mm_nt(screen_grad, w_screen)
    d_hidden_blend = jnp.sum(hidden_back * spread_two, 0)
    d_screen_blend = jnp.sum(screen_back * spread_two, 0)
    ahead = hidden_back * (1.0 - hidden_share) + screen_back * (1.0 - screen_share)
    two_grad = (
        hidden_back * hidden_share
        + screen_back * screen_share
        + jnp.concatenate([ahead[segs:], leaving(ahead[:segs], spot)], 0)
    )
    d_channel_gain = jnp.sum(two_grad * n2, 0)
    d_channel_bias = jnp.sum(two_grad, 0)
    residual_grad = cot + norm_back(two_grad, n2, inv2, channel_g)
    output_grad = residual_grad.astype(bf16)
    dw_output = mm_tn(gated, output_grad)
    gated_grad = mm_nt(output_grad, w_output)
    mix_grad = (gated_grad * gate).astype(bf16)
    gate_grad = (gated_grad * mix * gate * (1.0 - gate)).astype(bf16)

    boost = jnp.exp(first_log + kw)
    num_grad = mix_grad.reshape(cube).astype(f32) / (den + boost)
    den_grad = -num_grad * mix_raw
    fade = jnp.exp(-offsets * rate)
    totals = jnp.stack([jnp.sum(fade * num_grad, 0), jnp.sum(fade * den_grad, 0)])
    everyone = lax.all_gather(totals, "seq", axis=0)
    everyone = everyone.reshape(count, 2, groups, stretches, width)
    everyone = jnp.transpose(everyone, (3, 0, 1, 2, 4)).reshape(
        stretches * count, 2, groups, width
    )

    def carried_back(here):
        gap = order[:, None] - here - 1.0
        scale = jnp.where(gap >= 0, jnp.exp(-jnp.maximum(gap, 0.0) * (span * rate)), 0.0)
        return jnp.sum(scale[:, None, None, :] * everyone, 0)

    carry = jnp.stack([carried_back(j * count + spot.astype(f32)) for j in range(stretches)], 2)
    carry = carry.reshape(2, segs, width)
    key_grad, value_grad, first_sum, decay_sum = call(
        backward_kernel, [(cube, bf16)] * 2 + [((segs, width), f32)] * 2,
        k.reshape(cube), v.reshape(cube), num, den, mix_raw, mix_grad.reshape(cube), carry,
        decay_log, first_log,
    )
    key_grad = key_grad.reshape(rows, width)
    value_grad = value_grad.reshape(rows, width)
    d_first = jnp.sum(first_sum, 0)
    d_decay = -rate[0] * jnp.exp(-rate[0]) * jnp.sum(decay_sum, 0)
    dw_key = mm_tn(key_in, key_grad)
    dw_value = mm_tn(value_in, value_grad)
    dw_gate = mm_tn(gate_in, gate_grad)
    key_back = mm_nt(key_grad, w_key)
    value_back = mm_nt(value_grad, w_value)
    gate_back = mm_nt(gate_grad, w_gate)
    d_key_blend = jnp.sum(key_back * spread_one, 0)
    d_value_blend = jnp.sum(value_back * spread_one, 0)
    d_gate_blend = jnp.sum(gate_back * spread_one, 0)
    ahead = (
        key_back * (1.0 - key_share)
        + value_back * (1.0 - value_share)
        + gate_back * (1.0 - gate_share)
    )
    one_grad = (
        key_back * key_share
        + value_back * value_share
        + gate_back * gate_share
        + jnp.concatenate([ahead[segs:], leaving(ahead[:segs], spot)], 0)
    )
    d_mixer_gain = jnp.sum(one_grad * n1, 0)
    d_mixer_bias = jnp.sum(one_grad, 0)
    input_grad = residual_grad + norm_back(one_grad, n1, inv1, mixer_g)

    packed = jnp.concatenate(
        [d.reshape(owners, own, width).astype(bf16) for d in (dw_key, dw_value, dw_gate, dw_output, dw_screen)]
        + [
            dw_hidden.reshape(owners, own * parts, width).astype(bf16),
            dw_return.reshape(owners, own * parts, width).astype(bf16),
        ],
        1,
    )
    summed = lax.psum_scatter(packed, both, scatter_dimension=0).astype(f32)
    small = jnp.stack(
        [
            d_mixer_gain, d_mixer_bias, d_key_blend, d_value_blend, d_gate_blend, d_decay, d_first,
            d_channel_gain, d_channel_bias, d_hidden_blend, d_screen_blend,
        ]
    )
    small = lax.psum(small, both)
    place = (spot * lax.axis_size("rep") + lax.axis_index("rep")) * own
    small = lax.dynamic_slice_in_dim(small, place, own, 1)

    def batch_major(a):
        return jnp.transpose(a.reshape(span, groups, stretches, width), (1, 2, 0, 3))

    return (
        batch_major(output),
        batch_major(input_grad),
        final_num,
        final_den,
        final_top,
        *[small[i] for i in range(7)],
        *[summed[own * i : own * (i + 1)] for i in range(4)],
        *[small[i] for i in range(7, 11)],
        summed[own * 5 : own * (5 + parts)].reshape(own, inner),
        summed[own * 4 : own * 5],
        summed[own * (5 + parts) :],
    )


def solution(mesh):
    rows = P("rep", None, "seq", None)
    owned = P(both)
    owned_rows = P(both, None)
    in_specs = (rows,) + (owned,) * 7 + (owned_rows,) * 4 + (owned,) * 4 + (owned_rows,) * 3 + (rows,)
    out_specs = (
        (rows,) * 2 + (P("rep", "seq"),) * 3 + (owned,) * 7 + (owned_rows,) * 4
        + (owned,) * 4 + (owned_rows,) * 3
    )
    return jax.shard_map(body, mesh=mesh, in_specs=in_specs, out_specs=out_specs, check_vma=False)
```

```python
import functools

import jax
import jax.numpy as jnp
from jax import lax
from jax.experimental import pallas as pl
from jax.experimental.pallas import tpu as pltpu
from jax.sharding import PartitionSpec as P

f32 = jnp.float32
bf16 = jnp.bfloat16
norm_eps = 1e-05
both = ("seq", "rep")
MESH = pl.DeviceIdType.MESH

KEY, VALUE, GATE, OUTPUT, SCREEN, FIRST_PART = 0, 1, 2, 3, 4, 5
GROUPS = ((0, 2), (2, 5), (5, 7), (7, 9), (9, 11), (11, 13))
VECTORS = 11
(
    MIXER_G, MIXER_B, KEY_SHARE, VALUE_SHARE, GATE_SHARE, DECAY, FIRST,
    CHANNEL_G, CHANNEL_B, HIDDEN_SHARE, SCREEN_SHARE,
) = range(VECTORS)


def dot(left, right):
    return jnp.dot(left, right, preferred_element_type=f32)


def dot_nt(left, right):
    return lax.dot_general(left, right, (((1,), (1,)), ((), ())), preferred_element_type=f32)


def dot_tn(left, right):
    return lax.dot_general(left, right, (((0,), (0,)), ((), ())), preferred_element_type=f32)


def sigmoid(a):
    return 1.0 / (1.0 + jnp.exp(-a))


def normalise(values):
    centred = values - jnp.mean(values, -1, keepdims=True)
    inverse = lax.rsqrt(jnp.mean(centred * centred, -1, keepdims=True) + norm_eps)
    return centred * inverse, inverse


def norm_back(upstream, scaled, inverse, gain):
    inner = upstream * gain
    centred = inner - jnp.mean(inner, -1, keepdims=True)
    return inverse * (centred - scaled * jnp.mean(inner * scaled, -1, keepdims=True))


class Shape:
    def __init__(self, count, span, groups, stretches, width, inner):
        self.count, self.span, self.groups, self.stretches = count, span, groups, stretches
        self.width, self.inner = width, inner
        self.segs = groups * stretches
        self.rows = span * self.segs
        self.depth = count // 4
        self.chip = width // count
        self.own = self.chip // 2
        self.parts = inner // width
        self.mats = FIRST_PART + 2 * self.parts
        self.half = width // 2

    def fits(self):
        return (
            self.count % 4 == 0 and self.chip % 16 == 0 and self.own % 8 == 0 and self.own <= 32
            and self.half % 128 == 0 and self.groups == 8 and self.stretches == 2
            and self.parts == 4 and self.inner % self.width == 0 and self.rows <= 1024
        )


class Place:
    def __init__(self, sh):
        self.sh = sh
        self.s = lax.axis_index("seq")
        self.r = lax.axis_index("rep")
        self.z = self.s // 4
        self.y = lax.rem(self.s // 2, 2)
        self.x = lax.rem(self.s, 2)

    def device(self, z, y, x, r):
        return ((z * 2 + y) * 2 + x, r)

    def sibling(self):
        return (self.s, 1 - self.r)

    def x_peer(self):
        return self.device(self.z, self.y, 1 - self.x, self.r)

    def y_peer(self):
        return self.device(self.z, 1 - self.y, self.x, self.r)

    def z_to(self, j):
        return lax.rem(self.z + 1 + j, self.sh.depth)

    def z_from(self, j):
        return lax.rem(self.z + self.sh.depth - 1 - j, self.sh.depth)

    def z_peer(self, j):
        return self.device(self.z_to(j), self.y, self.x, self.r)

    def ring(self, step):
        count = self.sh.count
        return (lax.rem(self.s + count + step, count), self.r)

    def a_peer(self):
        flip_y, flip_x = 1 - self.r, self.r
        y = self.y + flip_y * (1 - 2 * self.y)
        x = self.x + flip_x * (1 - 2 * self.x)
        return self.device(self.z, y, x, self.r)

    def b_peer(self):
        flip_y, flip_x = self.r, 1 - self.r
        y = self.y + flip_y * (1 - 2 * self.y)
        x = self.x + flip_x * (1 - 2 * self.x)
        return self.device(self.z, y, x, self.r)

    def columns(self, r):
        half = self.sh.half
        return pl.ds(pl.multiple_of(r * half, half), half)


def send(src, dst, sems, index, device):
    return pltpu.make_async_remote_copy(
        src_ref=src, dst_ref=dst, send_sem=sems[0].at[index], recv_sem=sems[1].at[index],
        device_id=device, device_id_type=MESH,
    )


class Gather:
    def __init__(self, at, buf, lead, sems, group):
        self.at, self.buf, self.lead, self.sems, self.group = at, buf, lead, sems, group
        self.mine = at.columns(at.r)

    def cut(self, z, y, x):
        return self.buf.at[self.lead + (z, y, x, slice(None), self.mine)]

    def z_copy(self, j):
        at = self.at
        block = self.cut(at.z, at.y, at.x)
        return send(block, block, self.sems, (self.group, j), at.z_peer(j))

    def a_copy(self):
        at = self.at
        block = self.cut(slice(None), at.y, at.x)
        return send(block, block, self.sems, (self.group, at.sh.depth - 1), at.a_peer())

    def b_copy(self, core):
        at = self.at
        block = self.cut(slice(None), slice(None), at.x) if core == 0 else self.cut(
            slice(None), at.y, slice(None)
        )
        return send(block, block, self.sems, (self.group, at.sh.depth), at.b_peer())

    def core_copy(self):
        at = self.at
        block = self.cut(slice(None), slice(None), slice(None))
        return send(block, block, self.sems, (self.group, at.sh.depth + 1), at.sibling())

    def z_start(self):
        for j in range(self.at.sh.depth - 1):
            self.z_copy(j).start()

    def z_wait(self):
        for j in range(self.at.sh.depth - 1):
            self.z_copy(j).wait_recv()

    def a_start(self):
        self.a_copy().start()

    def a_wait(self):
        self.a_copy().wait_recv()

    def b_start(self):
        for core in range(2):
            @pl.when(self.at.r == core)
            def _():
                self.b_copy(core).start()

    def b_wait(self):
        self.b_copy(0).wait_recv()

    def core_start(self):
        self.core_copy().start()

    def core_wait(self):
        self.core_copy().wait_recv()

    def sent(self):
        for j in range(self.at.sh.depth - 1):
            self.z_copy(j).wait_send()
        self.a_copy().wait_send()
        self.b_copy(0).wait_send()
        self.core_copy().wait_send()

    def step(self, stage):
        if stage == 0:
            self.z_start()
        elif stage == 1:
            self.z_wait()
            self.a_start()
        elif stage == 2:
            self.a_wait()
            self.b_start()
        elif stage == 3:
            self.b_wait()
            self.core_start()
        else:
            self.core_wait()


def enter(at):
    sh = at.sh
    partners = [at.sibling(), at.x_peer(), at.y_peer(), at.ring(1), at.ring(-1)]
    partners += [at.z_peer(j) for j in range(sh.depth - 1)]
    barrier = pltpu.get_barrier_semaphore()
    for partner in partners:
        pl.semaphore_signal(barrier, inc=1, device_id=partner, device_id_type=MESH)
    pl.semaphore_wait(barrier, len(partners))


def slab(p, segs):
    return pl.ds(pl.multiple_of(p * segs, segs), segs)


def to_position_major(sh, stage, lanes, dest):
    tiles = sh.width // 128
    for j in range(tiles):
        lanes[j] = stage[:, j * 128 : (j + 1) * 128].astype(f32)

    def move(p, _):
        for j in range(tiles):
            both_stretches = [
                lanes[j, pl.ds(p + st * sh.span, sh.groups, stride=sh.stretches * sh.span), :]
                for st in range(sh.stretches)
            ]
            dest[slab(p, sh.segs), j * 128 : (j + 1) * 128] = jnp.concatenate(
                both_stretches, 0
            ).astype(dest.dtype)
        return 0

    lax.fori_loop(0, sh.span, move, 0)


def wrap_before(sh, at, got):
    half = sh.groups
    wrapped = jnp.concatenate([jnp.zeros((half, sh.width), f32), got[:half]], 0)
    return jnp.where(at.s == 0, wrapped, got)


def wrap_after(sh, at, got):
    half = sh.groups
    wrapped = jnp.concatenate([got[half:], jnp.zeros((half, sh.width), f32)], 0)
    return jnp.where(at.s == sh.count - 1, wrapped, got)


def decay_over(rate, positions):
    return jnp.exp(-positions * rate)


class Exchange:
    def __init__(self, sh, at, planes, xy, zs, sems):
        self.sh, self.at, self.planes = sh, at, planes
        self.xy, self.zs, self.sems = xy, zs, sems

    def x_copy(self):
        return send(self.xy.at[0], self.xy.at[1], self.sems, 0, self.at.x_peer())

    def y_copy(self):
        return send(self.xy.at[2], self.xy.at[3], self.sems, 1, self.at.y_peer())

    def z_copy(self, j):
        return send(self.xy.at[4], self.zs.at[j], self.sems, 2 + j, self.at.z_peer(j))

    def sent(self):
        self.x_copy().wait_send()
        self.y_copy().wait_send()
        for j in range(self.sh.depth - 1):
            self.z_copy(j).wait_send()


class Forward(Exchange):
    def start(self, totals):
        for i, part in enumerate(totals):
            self.xy[0, i] = part
        self.x_copy().start()

    def after_x(self, rate):
        sh, at = self.sh, self.at
        self.x_copy().wait_recv()
        fade = decay_over(rate, float(sh.span))
        for i in range(2):
            own, other = self.xy[0, i], self.xy[1, i]
            first = jnp.where(at.x == 0, own, other)
            second = jnp.where(at.x == 0, other, own)
            self.xy[2, i] = fade * first + second
        self.y_copy().start()

    def after_y(self, rate):
        sh, at = self.sh, self.at
        self.y_copy().wait_recv()
        fade = decay_over(rate, 2.0 * sh.span)
        for i in range(2):
            own, other = self.xy[2, i], self.xy[3, i]
            first = jnp.where(at.y == 0, own, other)
            second = jnp.where(at.y == 0, other, own)
            self.xy[4, i] = fade * first + second
        for j in range(sh.depth - 1):
            self.z_copy(j).start()

    def after_z(self, rate, carry, total):
        sh, at = self.sh, self.at
        for j in range(sh.depth - 1):
            self.z_copy(j).wait_recv()
        plane = 4.0 * sh.span
        z = at.z.astype(f32)
        within = (2 * at.y + at.x).astype(f32) * sh.span
        x_span = at.x.astype(f32) * sh.span
        for i in range(2):
            every = decay_over(rate, (sh.depth - 1.0 - z) * plane) * self.xy[4, i]
            before = jnp.zeros_like(every)
            for j in range(sh.depth - 1):
                other = at.z_from(j)
                o = other.astype(f32)
                got = self.zs[j, i]
                gap = jnp.maximum(z - 1.0 - o, 0.0) * plane
                before += jnp.where(other < at.z, decay_over(rate, gap), 0.0) * got
                every += decay_over(rate, (sh.depth - 1.0 - o) * plane) * got
            state = decay_over(rate, within) * before
            state += jnp.where(at.y == 1, decay_over(rate, x_span), 0.0) * self.xy[3, i]
            state += jnp.where(at.x == 1, 1.0, 0.0) * self.xy[1, i]
            half = sh.groups
            earlier = decay_over(rate, z * plane + within) * every[:half]
            carry[i] = state + jnp.concatenate([jnp.zeros_like(earlier), earlier], 0)
            total[i] = every


class Tops(Exchange):
    def start(self, own):
        self.xy[0, 0] = own
        self.x_copy().start()

    def after_x(self, rate):
        sh, at = self.sh, self.at
        self.x_copy().wait_recv()
        own, other = self.xy[0, 0], self.xy[1, 0]
        first = jnp.where(at.x == 0, own, other)
        second = jnp.where(at.x == 0, other, own)
        self.xy[2, 0] = jnp.maximum(first - sh.span * rate, second)
        self.y_copy().start()

    def after_y(self, rate):
        sh, at = self.sh, self.at
        self.y_copy().wait_recv()
        own, other = self.xy[2, 0], self.xy[3, 0]
        first = jnp.where(at.y == 0, own, other)
        second = jnp.where(at.y == 0, other, own)
        self.xy[4, 0] = jnp.maximum(first - 2.0 * sh.span * rate, second)
        for j in range(sh.depth - 1):
            self.z_copy(j).start()

    def after_z(self, rate):
        sh, at = self.sh, self.at
        for j in range(sh.depth - 1):
            self.z_copy(j).wait_recv()
        plane = 4.0 * sh.span
        most = self.xy[4, 0] - (sh.depth - 1.0 - at.z.astype(f32)) * plane * rate
        for j in range(sh.depth - 1):
            gap = (sh.depth - 1.0 - at.z_from(j).astype(f32)) * plane
            most = jnp.maximum(most, self.zs[j, 0] - gap * rate)
        half = sh.groups
        return jnp.maximum(most[:half] - float(sh.count * sh.span) * rate, most[half:])


def forward_kernel(
    sh,
    tok_hbm, cot_hbm, pack_ref,
    w_out, vec_out, xp_out, cotp_out, k_out, v_out, gate_out, num_out, den_out, res_out, hin_out,
    sin_out, s2_out, rg_out, gated_out, keyin_out, valin_out, gatin_out, final_out,
    w, vall, vecs, got_pack, stage, lanes, xp, cotp, halo, halo32,
    key_in, value_in, gate_in, k, v, gate, num, den, gated, res, hin, sin, s2, rg,
    st_xy, st_z, top_xy, top_z, carry, total, finals,
    local_sem, park_sem, pack_sems, ag_send, ag_recv, st_send, st_recv, top_send, top_recv,
    halo_send, halo_recv,
):
    at = Place(sh)
    segs, span, rows, half = sh.segs, sh.span, sh.rows, sh.half
    mine, theirs = at.columns(at.r), at.columns(1 - at.r)
    ag = (ag_send, ag_recv)
    gathers = [Gather(at, w, (pl.ds(a, b - a),), ag, g) for g, (a, b) in enumerate(GROUPS)]
    gather_v = Gather(at, vall, (), ag, len(GROUPS))

    load_tok = pltpu.make_async_copy(tok_hbm, stage, local_sem.at[0])
    load_tok.start()
    enter(at)
    pack_copy = send(
        pack_ref.at[:, :, theirs], got_pack, (pack_sems.at[0], pack_sems.at[1]), 0, at.sibling()
    )
    pack_copy.start()
    load_tok.wait()
    to_position_major(sh, stage, lanes, xp)
    halo_x = send(xp.at[pl.ds(rows - segs, segs)], halo.at[0], (halo_send, halo_recv), 0, at.ring(1))
    halo_x.start()
    load_cot = pltpu.make_async_copy(cot_hbm, stage, local_sem.at[1])
    load_cot.start()

    pack_copy.wait_recv()
    for m in range(sh.mats):
        own = pack_ref[m, : sh.own, mine].astype(f32)
        other = got_pack[m, : sh.own].astype(f32)
        first = jnp.where(at.r == 0, own, other)
        second = jnp.where(at.r == 0, other, own)
        w[m, at.z, at.y, at.x, :, mine] = jnp.concatenate([first, second], 0).astype(bf16)
    vall[at.z, at.y, at.x, :, mine] = (
        pack_ref[sh.mats, :16, mine].astype(f32) + got_pack[sh.mats, :16].astype(f32)
    ).astype(bf16)
    gather_v.step(0)
    gathers[0].step(0)
    gathers[1].step(0)
    load_cot.wait()
    to_position_major(sh, stage, lanes, cotp)
    gather_v.step(1)
    gathers[0].step(1)
    gathers[2].step(0)
    gather_v.step(2)
    gathers[0].step(2)
    gathers[1].step(1)
    gathers[3].step(0)
    gather_v.step(3)
    gather_v.step(4)
    spread = jnp.zeros((16, sh.width), f32)
    for z in range(sh.depth):
        for i in range(4):
            spread += vall[z, i // 2, i % 2].astype(f32)
    vecs[...] = spread

    def vec(i):
        return vecs[i : i + 1, :]

    halo_x.wait_recv()
    got, _ = normalise(halo[0].astype(f32))
    got = wrap_before(sh, at, got * vec(MIXER_G) + vec(MIXER_B))

    def blend_one(p, before):
        here = slab(p, segs)
        n1, _ = normalise(xp[here, :].astype(f32))
        one = n1 * vec(MIXER_G) + vec(MIXER_B)
        step = one - before
        key_in[here, :] = (before + step * vec(KEY_SHARE)).astype(bf16)
        value_in[here, :] = (before + step * vec(VALUE_SHARE)).astype(bf16)
        gate_in[here, :] = (before + step * vec(GATE_SHARE)).astype(bf16)
        return one

    lax.fori_loop(0, span, blend_one, got)

    gathers[0].step(3)
    gathers[1].step(2)
    gathers[2].step(1)
    gathers[4].step(0)
    gathers[0].step(4)

    def matrix(m):
        return w[m].reshape(sh.width, sh.width)

    k[...] = dot(key_in[...], matrix(KEY)).astype(bf16)
    v[...] = dot(value_in[...], matrix(VALUE)).astype(bf16)

    rate = jnp.exp(vec(DECAY))
    keep = jnp.exp(-rate)
    zero = jnp.zeros((segs, sh.width), f32)

    def add_up(p, state):
        a, b, top = state
        here = slab(p, segs)
        key = k[here, :].astype(f32)
        grown = jnp.exp(key)
        top = jnp.maximum(top - rate, key)
        return keep * a + grown * v[here, :].astype(f32), keep * b + grown, top

    sum_num, sum_den, top = lax.fori_loop(
        0, span, add_up, (zero, zero, jnp.full((segs, sh.width), -jnp.inf, f32))
    )
    states = Forward(sh, at, 2, st_xy, st_z, (st_send, st_recv))
    states.start((sum_num, sum_den))
    tops = Tops(sh, at, 1, top_xy, top_z, (top_send, top_recv))
    tops.start(top)

    gathers[1].step(3)
    gathers[2].step(2)
    gathers[3].step(1)
    gathers[5].step(0)
    states.after_x(rate)
    gathers[1].step(4)
    gate[...] = sigmoid(dot(gate_in[...], matrix(GATE)))
    states.after_y(rate)
    tops.after_x(rate)
    gathers[2].step(3)
    gathers[3].step(2)
    gathers[4].step(1)
    states.after_z(rate, carry, total)
    tops.after_y(rate)

    boost_rate = jnp.exp(vec(FIRST))

    def recur(p, state):
        a, b = state
        here = slab(p, segs)
        grown = jnp.exp(k[here, :].astype(f32))
        value = v[here, :].astype(f32)
        boost = grown * boost_rate
        num[here, :] = a
        den[here, :] = b
        mix = ((a + boost * value) / (b + boost)).astype(bf16).astype(f32)
        gated[here, :] = (gate[here, :] * mix).astype(bf16)
        return keep * a + grown * value, keep * b + grown

    lax.fori_loop(0, span, recur, (carry[0], carry[1]))
    res[...] = xp[...].astype(f32) + dot(gated[...], matrix(OUTPUT))

    last = pl.ds(rows - segs, segs)
    n2, _ = normalise(res[last, :])
    halo32[0] = n2 * vec(CHANNEL_G) + vec(CHANNEL_B)
    halo_two = send(halo32.at[0], halo32.at[1], (halo_send, halo_recv), 1, at.ring(1))
    halo_two.start()
    gathers[3].step(3)
    gathers[4].step(2)
    gathers[5].step(1)
    final_top = tops.after_z(rate)
    far = decay_over(rate, float(sh.count * span))
    scale = jnp.exp(-final_top)
    for i in range(2):
        finals[i] = (far * total[i, : sh.groups] + total[i, sh.groups :]) * scale
    finals[2] = final_top
    halo_two.wait_recv()
    got = wrap_before(sh, at, halo32[1])

    def blend_two(p, before):
        here = slab(p, segs)
        n2, _ = normalise(res[here, :])
        two = n2 * vec(CHANNEL_G) + vec(CHANNEL_B)
        step = two - before
        hin[here, :] = (before + step * vec(HIDDEN_SHARE)).astype(bf16)
        sin[here, :] = (before + step * vec(SCREEN_SHARE)).astype(bf16)
        return two

    lax.fori_loop(0, span, blend_two, got)
    s2[...] = sigmoid(dot(sin[...], matrix(SCREEN)))
    rg[...] = (cotp[...].astype(f32) * s2[...]).astype(bf16)

    gathers[2].step(4)
    gathers[4].step(3)
    gathers[5].step(2)
    gathers[3].step(4)
    gathers[5].step(3)
    gathers[4].step(4)
    gathers[5].step(4)
    parks = [
        (w, w_out), (vecs, vec_out), (xp, xp_out), (cotp, cotp_out), (k, k_out), (v, v_out),
        (gate, gate_out), (num, num_out), (den, den_out), (res, res_out), (hin, hin_out),
        (sin, sin_out), (s2, s2_out), (rg, rg_out), (gated, gated_out), (key_in, keyin_out),
        (value_in, valin_out), (gate_in, gatin_out), (finals, final_out),
    ]
    copies = [pltpu.make_async_copy(a, b, park_sem.at[i]) for i, (a, b) in enumerate(parks)]
    for c in copies:
        c.start()
    pack_copy.wait_send()
    halo_x.wait_send()
    halo_two.wait_send()
    for g in gathers + [gather_v]:
        g.sent()
    states.sent()
    tops.sent()
    for c in copies:
        c.wait()


def forward(sh, tokens, cotangent, pack):
    R, D, S, Z = sh.rows, sh.width, sh.segs, sh.depth
    shape = jax.ShapeDtypeStruct
    narrow, wide = ((R, D), bf16), ((R, D), f32)
    w_shape = (sh.mats, Z, 2, 2, sh.chip, D)
    outs = [
        (w_shape, bf16), ((16, D), f32), narrow, narrow, narrow, narrow, wide, wide, wide, wide,
        narrow, narrow, wide, narrow, narrow, narrow, narrow, narrow, ((3, sh.groups, D), f32),
    ]
    V = pltpu.VMEM
    dma = pltpu.SemaphoreType.DMA
    scratch = [
        V(w_shape, bf16), V((Z, 2, 2, 16, D), bf16), V((16, D), f32),
        V((sh.mats + 1, 32, sh.half), bf16), V((R, D), bf16), V((D // 128, R, 128), f32),
        V(*narrow), V(*narrow), V((1, S, D), bf16), V((2, S, D), f32),
        V(*narrow), V(*narrow), V(*narrow), V(*narrow), V(*narrow), V(*wide), V(*wide), V(*wide),
        V(*narrow), V(*wide), V(*narrow), V(*narrow), V(*wide), V(*narrow),
        V((5, 2, S, D), f32), V((Z - 1, 2, S, D), f32), V((5, 1, S, D), f32),
        V((Z - 1, 1, S, D), f32), V((2, S, D), f32), V((2, S, D), f32), V((3, sh.groups, D), f32),
        dma((2,)), dma((len(outs),)), dma((2, 1)), dma((len(GROUPS) + 1, Z + 2)),
        dma((len(GROUPS) + 1, Z + 2)), dma((Z + 1,)), dma((Z + 1,)), dma((Z + 1,)), dma((Z + 1,)),
        dma((2,)), dma((2,)),
    ]
    anywhere = pl.BlockSpec(memory_space=pl.ANY)
    return pl.pallas_call(
        functools.partial(forward_kernel, sh),
        out_shape=[shape(s, t) for s, t in outs],
        in_specs=[anywhere, anywhere, pl.BlockSpec(memory_space=pltpu.VMEM)],
        out_specs=[anywhere] * len(outs),
        scratch_shapes=scratch,
        compiler_params=pltpu.CompilerParams(
            collective_id=0, has_side_effects=True, vmem_limit_bytes=60 * 2**20
        ),
    )(tokens.reshape(R, D), cotangent.reshape(R, D), pack)


def mm(left, right):
    return jnp.dot(left, right, preferred_element_type=f32)


def mm_nt(left, right):
    return lax.dot_general(left, right, (((1,), (1,)), ((), ())), preferred_element_type=f32)


def mm_tn(left, right):
    return lax.dot_general(left, right, (((0,), (0,)), ((), ())), preferred_element_type=f32)


def ring(value, steps):
    count = lax.axis_size("seq")
    return lax.ppermute(value, "seq", [(i, (i + steps) % count) for i in range(count)])


def entering(last, spot):
    got = ring(last, 1)
    pairs = got.reshape(-1, 2, got.shape[-1])
    wrapped = jnp.concatenate([jnp.zeros_like(pairs[:, :1]), pairs[:, :1]], 1)
    return jnp.where(spot == 0, wrapped, pairs).reshape(got.shape)


def leaving(first, spot):
    count = lax.axis_size("seq")
    got = ring(first, -1)
    pairs = got.reshape(-1, 2, got.shape[-1])
    wrapped = jnp.concatenate([pairs[:, 1:], jnp.zeros_like(pairs[:, :1])], 1)
    return jnp.where(spot == count - 1, wrapped, pairs).reshape(got.shape)


def plain_scan(k_ref, v_ref, carry_ref, decay_ref, first_ref, num_ref, den_ref, mix_ref):
    keep = jnp.exp(-jnp.exp(decay_ref[...]))
    boost_rate = jnp.exp(first_ref[...])

    def step(t, state):
        num, den = state
        k = jnp.exp(k_ref[t].astype(f32))
        v = v_ref[t].astype(f32)
        boost = k * boost_rate
        num_ref[t] = num
        den_ref[t] = den
        mix_ref[t] = (num + boost * v) / (den + boost)
        return keep * num + k * v, keep * den + k

    lax.fori_loop(0, k_ref.shape[0], step, (carry_ref[0], carry_ref[1]))


def plain_scan_back(
    k_ref, v_ref, num_ref, den_ref, mix_ref, grad_ref, carry_ref, decay_ref, first_ref,
    kg_ref, vg_ref, first_grad_ref, decay_grad_ref,
):
    keep = jnp.exp(-jnp.exp(decay_ref[...]))
    boost_rate = jnp.exp(first_ref[...])
    length = k_ref.shape[0]

    def step(i, state):
        adj_num, adj_den, first_sum, decay_sum = state
        t = length - 1 - i
        k = jnp.exp(k_ref[t].astype(f32))
        v = v_ref[t].astype(f32)
        boost = k * boost_rate
        num_grad = grad_ref[t].astype(f32) / (den_ref[t] + boost)
        den_grad = -num_grad * mix_ref[t]
        inner = boost * (v * num_grad + den_grad)
        kg_ref[t] = (k * (v * adj_num + adj_den) + inner).astype(bf16)
        vg_ref[t] = (k * adj_num + boost * num_grad).astype(bf16)
        first_sum = first_sum + inner
        decay_sum = decay_sum + num_ref[t] * adj_num + den_ref[t] * adj_den
        return keep * adj_num + num_grad, keep * adj_den + den_grad, first_sum, decay_sum

    zero = jnp.zeros_like(carry_ref[0])
    out = lax.fori_loop(0, length, step, (carry_ref[0], carry_ref[1], zero, zero))
    first_grad_ref[...] = out[2]
    decay_grad_ref[...] = out[3]


def call(kernel, shapes, *operands):
    space = pl.BlockSpec(memory_space=pltpu.VMEM)
    return pl.pallas_call(
        kernel,
        out_shape=[jax.ShapeDtypeStruct(s, t) for s, t in shapes],
        in_specs=[space] * len(operands),
        out_specs=[space] * len(shapes),
        compiler_params=pltpu.CompilerParams(vmem_limit_bytes=48 * 2**20),
    )(*operands)


def plain_body(
    tokens, mixer_gain, mixer_bias, key_blend, value_blend, gate_blend, time_decay, time_first,
    key_weight, value_weight, gate_weight, output_weight, channel_gain, channel_bias,
    hidden_blend, screen_blend, hidden_weight, screen_weight, return_weight, cotangent,
):
    groups, stretches, span, width = tokens.shape
    count = lax.axis_size("seq")
    owners = count * lax.axis_size("rep")
    spot = lax.axis_index("seq")
    segs = groups * stretches
    rows = span * segs
    own = width // owners
    inner = hidden_weight.shape[1]
    parts = inner // width

    vectors = (
        mixer_gain, mixer_bias, key_blend, value_blend, gate_blend, time_decay, time_first,
        channel_gain, channel_bias, hidden_blend, screen_blend,
    )
    squares = (key_weight, value_weight, gate_weight, output_weight, screen_weight)
    packed = jnp.concatenate(
        squares + (hidden_weight.reshape(own * parts, width), return_weight), 0
    )
    packed = lax.all_gather(packed, both, axis=0)
    spread_vectors = lax.all_gather(jnp.stack(vectors), both, axis=0)
    spread_vectors = jnp.swapaxes(spread_vectors, 0, 1).reshape(len(vectors), width).astype(f32)
    (
        mixer_g, mixer_b, key_share, value_share, gate_share, decay_log, first_log,
        channel_g, channel_b, hidden_share, screen_share,
    ) = [spread_vectors[i][None] for i in range(len(vectors))]

    def piece(start, size, shape):
        return packed[:, start : start + size].reshape(shape)

    w_key, w_value, w_gate, w_output, w_screen = [
        piece(own * i, own, (width, width)) for i in range(5)
    ]
    w_hidden = piece(own * 5, own * parts, (width, inner))
    w_return = piece(own * (5 + parts), own * parts, (inner, width))

    def position_major(a):
        return jnp.transpose(a, (2, 0, 1, 3)).reshape(rows, width)

    def shifted(a, first):
        return jnp.concatenate([first, a[:-segs]], 0)

    x = position_major(tokens).astype(f32)
    n1, inv1 = normalise(x)
    one = n1 * mixer_g + mixer_b
    before = shifted(one, entering(one[-segs:], spot))
    spread_one = one - before
    key_in = (before + spread_one * key_share).astype(bf16)
    value_in = (before + spread_one * value_share).astype(bf16)
    gate_in = (before + spread_one * gate_share).astype(bf16)
    k = mm(key_in, w_key).astype(bf16)
    v = mm(value_in, w_value).astype(bf16)
    gate = jax.nn.sigmoid(mm(gate_in, w_gate))

    rate = jnp.exp(decay_log)
    cube = (span, segs, width)
    offsets = jnp.arange(span, dtype=f32)[:, None, None]
    kw = k.reshape(cube).astype(f32)
    vw = v.reshape(cube).astype(f32)
    shifted_key = kw - (span - 1.0 - offsets) * rate
    ends = jnp.exp(shifted_key)
    totals = jnp.stack([jnp.sum(ends * vw, 0), jnp.sum(ends, 0)])
    tops = jnp.max(shifted_key, 0)
    everyone = lax.all_gather(jnp.concatenate([totals, tops[None]]), "seq", axis=0)
    everyone = everyone.reshape(count, 3, groups, stretches, width)
    everyone = jnp.transpose(everyone, (3, 0, 1, 2, 4)).reshape(
        stretches * count, 3, groups, width
    )
    order = jnp.arange(stretches * count, dtype=f32)

    def weights_for(here):
        gap = here - 1.0 - order[:, None]
        return jnp.where(gap >= 0, jnp.exp(-jnp.maximum(gap, 0.0) * (span * rate)), 0.0)

    def carried(here):
        return jnp.sum(weights_for(here)[:, None, None, :] * everyone[:, :2], 0)

    carry = jnp.stack([carried(j * count + spot.astype(f32)) for j in range(stretches)], 2)
    carry = carry.reshape(2, segs, width)
    final = carried(float(stretches * count))
    far = (stretches * count - 1.0 - order)[:, None] * (span * rate)
    top = jnp.max(everyone[:, 2] - far[:, None, :], 0)
    slab = width // count

    def own_slab(a):
        return lax.dynamic_slice_in_dim(a, spot * slab, slab, 1)

    final_top = own_slab(top)
    scaling = jnp.exp(-final_top)
    final_num = own_slab(final[0]) * scaling
    final_den = own_slab(final[1]) * scaling

    num, den, mix_raw = call(
        plain_scan, [(cube, f32)] * 3, k.reshape(cube), v.reshape(cube), carry,
        decay_log, first_log,
    )
    mix = mix_raw.reshape(rows, width).astype(bf16).astype(f32)
    gated = (gate * mix).astype(bf16)
    residual = x + mm(gated, w_output)
    n2, inv2 = normalise(residual)
    two = n2 * channel_g + channel_b
    before = shifted(two, entering(two[-segs:], spot))
    spread_two = two - before
    hidden_in = (before + spread_two * hidden_share).astype(bf16)
    screen_in = (before + spread_two * screen_share).astype(bf16)
    screen = jax.nn.sigmoid(mm(screen_in, w_screen))
    cot = position_major(cotangent).astype(f32)
    returned_grad = (cot * screen).astype(bf16)
    relu = jnp.maximum(mm(hidden_in, w_hidden), 0.0)
    act = jnp.square(relu).astype(bf16)
    returned = mm(act, w_return)
    output = (residual + screen * returned).astype(bf16)

    screen_grad = (cot * returned * screen * (1.0 - screen)).astype(bf16)
    hidden_grad = (mm_nt(returned_grad, w_return) * (2.0 * relu)).astype(bf16)
    dw_return = mm_tn(act, returned_grad)
    dw_hidden = mm_tn(hidden_in, hidden_grad)
    dw_screen = mm_tn(screen_in, screen_grad)
    hidden_back = mm_nt(hidden_grad, w_hidden)
    screen_back = mm_nt(screen_grad, w_screen)
    d_hidden_blend = jnp.sum(hidden_back * spread_two, 0)
    d_screen_blend = jnp.sum(screen_back * spread_two, 0)
    ahead = hidden_back * (1.0 - hidden_share) + screen_back * (1.0 - screen_share)
    two_grad = (
        hidden_back * hidden_share
        + screen_back * screen_share
        + jnp.concatenate([ahead[segs:], leaving(ahead[:segs], spot)], 0)
    )
    d_channel_gain = jnp.sum(two_grad * n2, 0)
    d_channel_bias = jnp.sum(two_grad, 0)
    residual_grad = cot + norm_back(two_grad, n2, inv2, channel_g)
    output_grad = residual_grad.astype(bf16)
    dw_output = mm_tn(gated, output_grad)
    gated_grad = mm_nt(output_grad, w_output)
    mix_grad = (gated_grad * gate).astype(bf16)
    gate_grad = (gated_grad * mix * gate * (1.0 - gate)).astype(bf16)

    boost = jnp.exp(first_log + kw)
    num_grad = mix_grad.reshape(cube).astype(f32) / (den + boost)
    den_grad = -num_grad * mix_raw
    fade = jnp.exp(-offsets * rate)
    totals = jnp.stack([jnp.sum(fade * num_grad, 0), jnp.sum(fade * den_grad, 0)])
    everyone = lax.all_gather(totals, "seq", axis=0)
    everyone = everyone.reshape(count, 2, groups, stretches, width)
    everyone = jnp.transpose(everyone, (3, 0, 1, 2, 4)).reshape(
        stretches * count, 2, groups, width
    )

    def carried_back(here):
        gap = order[:, None] - here - 1.0
        scale = jnp.where(gap >= 0, jnp.exp(-jnp.maximum(gap, 0.0) * (span * rate)), 0.0)
        return jnp.sum(scale[:, None, None, :] * everyone, 0)

    carry = jnp.stack([carried_back(j * count + spot.astype(f32)) for j in range(stretches)], 2)
    carry = carry.reshape(2, segs, width)
    key_grad, value_grad, first_sum, decay_sum = call(
        plain_scan_back, [(cube, bf16)] * 2 + [((segs, width), f32)] * 2,
        k.reshape(cube), v.reshape(cube), num, den, mix_raw, mix_grad.reshape(cube), carry,
        decay_log, first_log,
    )
    key_grad = key_grad.reshape(rows, width)
    value_grad = value_grad.reshape(rows, width)
    d_first = jnp.sum(first_sum, 0)
    d_decay = -rate[0] * jnp.exp(-rate[0]) * jnp.sum(decay_sum, 0)
    dw_key = mm_tn(key_in, key_grad)
    dw_value = mm_tn(value_in, value_grad)
    dw_gate = mm_tn(gate_in, gate_grad)
    key_back = mm_nt(key_grad, w_key)
    value_back = mm_nt(value_grad, w_value)
    gate_back = mm_nt(gate_grad, w_gate)
    d_key_blend = jnp.sum(key_back * spread_one, 0)
    d_value_blend = jnp.sum(value_back * spread_one, 0)
    d_gate_blend = jnp.sum(gate_back * spread_one, 0)
    ahead = (
        key_back * (1.0 - key_share)
        + value_back * (1.0 - value_share)
        + gate_back * (1.0 - gate_share)
    )
    one_grad = (
        key_back * key_share
        + value_back * value_share
        + gate_back * gate_share
        + jnp.concatenate([ahead[segs:], leaving(ahead[:segs], spot)], 0)
    )
    d_mixer_gain = jnp.sum(one_grad * n1, 0)
    d_mixer_bias = jnp.sum(one_grad, 0)
    input_grad = residual_grad + norm_back(one_grad, n1, inv1, mixer_g)

    packed = jnp.concatenate(
        [d.reshape(owners, own, width).astype(bf16) for d in (dw_key, dw_value, dw_gate, dw_output, dw_screen)]
        + [
            dw_hidden.reshape(owners, own * parts, width).astype(bf16),
            dw_return.reshape(owners, own * parts, width).astype(bf16),
        ],
        1,
    )
    summed = lax.psum_scatter(packed, both, scatter_dimension=0).astype(f32)
    small = jnp.stack(
        [
            d_mixer_gain, d_mixer_bias, d_key_blend, d_value_blend, d_gate_blend, d_decay, d_first,
            d_channel_gain, d_channel_bias, d_hidden_blend, d_screen_blend,
        ]
    )
    small = lax.psum(small, both)
    place = (spot * lax.axis_size("rep") + lax.axis_index("rep")) * own
    small = lax.dynamic_slice_in_dim(small, place, own, 1)

    def batch_major(a):
        return jnp.transpose(a.reshape(span, groups, stretches, width), (1, 2, 0, 3))

    return (
        batch_major(output),
        batch_major(input_grad),
        final_num,
        final_den,
        final_top,
        *[small[i] for i in range(7)],
        *[summed[own * i : own * (i + 1)] for i in range(4)],
        *[small[i] for i in range(7, 11)],
        summed[own * 5 : own * (5 + parts)].reshape(own, inner),
        summed[own * 4 : own * 5],
        summed[own * (5 + parts) :],
    )


def make_pack(sh, squares, hidden_weight, return_weight, vectors):
    own, width, parts = sh.own, sh.width, sh.parts
    owners = 2 * sh.count
    hidden = hidden_weight.reshape(own, owners, parts, own)
    hidden = jnp.transpose(hidden, (2, 0, 1, 3)).reshape(parts, own, width)
    back = return_weight.reshape(parts, own, width)
    both_parts = jnp.stack([hidden, back], 1).reshape(2 * parts, own, width)
    mats = jnp.concatenate([jnp.stack(squares), both_parts], 0)
    mats = jnp.pad(mats, ((0, 0), (0, 32 - own), (0, 0)))
    place = (lax.axis_index("seq") * 2 + lax.axis_index("rep")) * own
    tile = lax.dynamic_update_slice(
        jnp.zeros((32, width), bf16), jnp.stack(vectors), (0, place)
    )
    return jnp.concatenate([mats, tile[None]], 0)


def fused_body(sh, *args):
    (
        tokens, mixer_gain, mixer_bias, key_blend, value_blend, gate_blend, time_decay, time_first,
        key_weight, value_weight, gate_weight, output_weight, channel_gain, channel_bias,
        hidden_blend, screen_blend, hidden_weight, screen_weight, return_weight, cotangent,
    ) = args
    span, segs, width, own = sh.span, sh.segs, sh.width, sh.own
    rows, groups, parts, inner = sh.rows, sh.groups, sh.parts, sh.inner
    owners = 2 * sh.count
    spot = lax.axis_index("seq")
    vectors = (
        mixer_gain, mixer_bias, key_blend, value_blend, gate_blend, time_decay, time_first,
        channel_gain, channel_bias, hidden_blend, screen_blend,
    )
    squares = (key_weight, value_weight, gate_weight, output_weight, screen_weight)
    pack = make_pack(sh, squares, hidden_weight, return_weight, vectors)
    (
        w, vecs, xp, cotp, k, v, gate, num, den, residual, hidden_in, screen_in, screen,
        returned_grad, gated, key_in, value_in, gate_in, finals,
    ) = forward(sh, tokens, cotangent, pack)
    (
        mixer_g, mixer_b, key_share, value_share, gate_share, decay_log, first_log,
        channel_g, channel_b, hidden_share, screen_share,
    ) = [vecs[i][None] for i in range(len(vectors))]
    w = w.reshape(sh.mats, width, width)
    w_key, w_value, w_gate, w_output, w_screen = [w[i] for i in range(5)]
    w_hidden = jnp.concatenate([w[5 + 2 * c] for c in range(parts)], 1)
    w_return = jnp.concatenate([w[6 + 2 * c] for c in range(parts)], 0)
    cube = (span, segs, width)
    rate = jnp.exp(decay_log)

    def after(first):
        got = ring(first, -1)
        wrapped = jnp.concatenate([got[groups:], jnp.zeros_like(got[groups:])], 0)
        return jnp.where(spot == sh.count - 1, wrapped, got)

    def before_rows(last):
        got = ring(last, 1)
        wrapped = jnp.concatenate([jnp.zeros_like(got[:groups]), got[:groups]], 0)
        return jnp.where(spot == 0, wrapped, got)

    x = xp.astype(f32)
    n1, inv1 = normalise(x)
    one = n1 * mixer_g + mixer_b
    spread_one = one - jnp.concatenate([before_rows(one[-segs:]), one[:-segs]], 0)
    n2, inv2 = normalise(residual)
    two = n2 * channel_g + channel_b
    spread_two = two - jnp.concatenate([before_rows(two[-segs:]), two[:-segs]], 0)
    cot = cotp.astype(f32)
    relu = jnp.maximum(mm(hidden_in, w_hidden), 0.0)
    act = jnp.square(relu).astype(bf16)
    returned = mm(act, w_return)
    output = (residual + screen * returned).astype(bf16)

    screen_grad = (cot * returned * screen * (1.0 - screen)).astype(bf16)
    hidden_grad = (mm_nt(returned_grad, w_return) * (2.0 * relu)).astype(bf16)
    dw_return = mm_tn(act, returned_grad)
    dw_hidden = mm_tn(hidden_in, hidden_grad)
    dw_screen = mm_tn(screen_in, screen_grad)
    hidden_back = mm_nt(hidden_grad, w_hidden)
    screen_back = mm_nt(screen_grad, w_screen)
    d_hidden_blend = jnp.sum(hidden_back * spread_two, 0)
    d_screen_blend = jnp.sum(screen_back * spread_two, 0)
    ahead = hidden_back * (1.0 - hidden_share) + screen_back * (1.0 - screen_share)
    two_grad = (
        hidden_back * hidden_share
        + screen_back * screen_share
        + jnp.concatenate([ahead[segs:], after(ahead[:segs])], 0)
    )
    d_channel_gain = jnp.sum(two_grad * n2, 0)
    d_channel_bias = jnp.sum(two_grad, 0)
    residual_grad = cot + norm_back(two_grad, n2, inv2, channel_g)
    output_grad = residual_grad.astype(bf16)
    dw_output = mm_tn(gated, output_grad)
    gated_grad = mm_nt(output_grad, w_output)
    mix_grad = (gated_grad * gate).astype(bf16)

    num, den = num.reshape(cube), den.reshape(cube)
    kw = k.reshape(cube).astype(f32)
    vw = v.reshape(cube).astype(f32)
    boost = jnp.exp(first_log + kw)
    mix_raw = (num + boost * vw) / (den + boost)
    mix = mix_raw.reshape(rows, width).astype(bf16).astype(f32)
    gate_grad = (gated_grad * mix * gate * (1.0 - gate)).astype(bf16)
    num_grad = mix_grad.reshape(cube).astype(f32) / (den + boost)
    den_grad = -num_grad * mix_raw
    offsets = jnp.arange(span, dtype=f32)[:, None, None]
    fade = jnp.exp(-offsets * rate)
    totals = jnp.stack([jnp.sum(fade * num_grad, 0), jnp.sum(fade * den_grad, 0)])
    everyone = lax.all_gather(totals, "seq", axis=0)
    everyone = everyone.reshape(sh.count, 2, 2, groups, width)
    everyone = jnp.transpose(everyone, (2, 0, 1, 3, 4)).reshape(2 * sh.count, 2, groups, width)
    order = jnp.arange(2 * sh.count, dtype=f32)

    def carried_back(here):
        gap = order[:, None] - here - 1.0
        scale = jnp.where(gap >= 0, jnp.exp(-jnp.maximum(gap, 0.0) * (span * rate)), 0.0)
        return jnp.sum(scale[:, None, None, :] * everyone, 0)

    carry = jnp.stack([carried_back(j * sh.count + spot.astype(f32)) for j in range(2)], 1)
    carry = carry.reshape(2, segs, width)
    key_grad, value_grad, first_sum, decay_sum = call(
        plain_scan_back, [(cube, bf16)] * 2 + [((segs, width), f32)] * 2,
        k.reshape(cube), v.reshape(cube), num, den, mix_raw, mix_grad.reshape(cube), carry,
        decay_log, first_log,
    )
    key_grad = key_grad.reshape(rows, width)
    value_grad = value_grad.reshape(rows, width)
    d_first = jnp.sum(first_sum, 0)
    d_decay = -rate[0] * jnp.exp(-rate[0]) * jnp.sum(decay_sum, 0)
    dw_key = mm_tn(key_in, key_grad)
    dw_value = mm_tn(value_in, value_grad)
    dw_gate = mm_tn(gate_in, gate_grad)
    key_back = mm_nt(key_grad, w_key)
    value_back = mm_nt(value_grad, w_value)
    gate_back = mm_nt(gate_grad, w_gate)
    d_key_blend = jnp.sum(key_back * spread_one, 0)
    d_value_blend = jnp.sum(value_back * spread_one, 0)
    d_gate_blend = jnp.sum(gate_back * spread_one, 0)
    ahead = (
        key_back * (1.0 - key_share)
        + value_back * (1.0 - value_share)
        + gate_back * (1.0 - gate_share)
    )
    one_grad = (
        key_back * key_share
        + value_back * value_share
        + gate_back * gate_share
        + jnp.concatenate([ahead[segs:], after(ahead[:segs])], 0)
    )
    d_mixer_gain = jnp.sum(one_grad * n1, 0)
    d_mixer_bias = jnp.sum(one_grad, 0)
    input_grad = residual_grad + norm_back(one_grad, n1, inv1, mixer_g)

    grads = [dw_key, dw_value, dw_gate, dw_output, dw_screen]
    for c in range(parts):
        grads += [dw_hidden[:, c * width : (c + 1) * width], dw_return[c * width : (c + 1) * width]]
    packed = jnp.concatenate([d.reshape(owners, own, width).astype(bf16) for d in grads], 1)
    summed = lax.psum_scatter(packed, both, scatter_dimension=0).astype(f32)
    summed = summed.reshape(sh.mats, own, width)
    small = jnp.stack(
        [
            d_mixer_gain, d_mixer_bias, d_key_blend, d_value_blend, d_gate_blend, d_decay, d_first,
            d_channel_gain, d_channel_bias, d_hidden_blend, d_screen_blend,
        ]
    )
    small = lax.psum(small, both)
    place = (spot * 2 + lax.axis_index("rep")) * own
    small = lax.dynamic_slice_in_dim(small, place, own, 1)

    def batch_major(a):
        return jnp.transpose(a.reshape(span, 2, groups, width), (2, 1, 0, 3))

    return (
        batch_major(output),
        batch_major(input_grad),
        *own_finals(sh, finals),
        *own_grads(sh, small, summed),
    )


def own_finals(sh, finals):
    share = sh.width // sh.count
    cut = lax.dynamic_slice_in_dim(finals, lax.axis_index("seq") * share, share, 2)
    return [cut[i] for i in range(3)]


def own_grads(sh, small, summed):
    own, owners, parts, inner = sh.own, 2 * sh.count, sh.parts, sh.inner
    hidden = summed[FIRST_PART::2].reshape(parts, own, owners, own)
    hidden = jnp.transpose(hidden, (1, 2, 0, 3)).reshape(own, inner)
    back = summed[FIRST_PART + 1 :: 2].reshape(parts * own, sh.width)
    return (
        *[small[i] for i in range(7)],
        *[summed[i] for i in (KEY, VALUE, GATE, OUTPUT)],
        *[small[i] for i in range(7, 11)],
        hidden,
        summed[SCREEN],
        back,
    )


def body(*args):
    tokens, hidden_weight = args[0], args[16]
    groups, stretches, span, width = tokens.shape
    sh = Shape(lax.axis_size("seq"), span, groups, stretches, width, hidden_weight.shape[1])
    if lax.axis_size("rep") == 2 and sh.fits():
        return fused_body(sh, *args)
    return plain_body(*args)


def solution(mesh):
    rows = P("rep", None, "seq", None)
    owned = P(both)
    owned_rows = P(both, None)
    in_specs = (rows,) + (owned,) * 7 + (owned_rows,) * 4 + (owned,) * 4 + (owned_rows,) * 3 + (rows,)
    out_specs = (
        (rows,) * 2 + (P("rep", "seq"),) * 3 + (owned,) * 7 + (owned_rows,) * 4
        + (owned,) * 4 + (owned_rows,) * 3
    )
    return jax.shard_map(body, mesh=mesh, in_specs=in_specs, out_specs=out_specs, check_vma=False)
```

```python
import functools

import jax
import jax.numpy as jnp
from jax import lax
from jax.experimental import pallas as pl
from jax.experimental.pallas import tpu as pltpu
from jax.sharding import PartitionSpec as P

f32 = jnp.float32
bf16 = jnp.bfloat16
norm_eps = 1e-05
both = ("seq", "rep")
MESH = pl.DeviceIdType.MESH

KEY, VALUE, GATE, OUTPUT, SCREEN, FIRST_PART = 0, 1, 2, 3, 4, 5
GROUPS = ((0, 2), (2, 5), (5, 7), (7, 9), (9, 11), (11, 13))
VECTORS = 11
(
    MIXER_G, MIXER_B, KEY_SHARE, VALUE_SHARE, GATE_SHARE, DECAY, FIRST,
    CHANNEL_G, CHANNEL_B, HIDDEN_SHARE, SCREEN_SHARE,
) = range(VECTORS)


def dot(left, right):
    return jnp.dot(left, right, preferred_element_type=f32)


def dot_nt(left, right):
    return lax.dot_general(left, right, (((1,), (1,)), ((), ())), preferred_element_type=f32)


def dot_tn(left, right):
    return lax.dot_general(left, right, (((0,), (0,)), ((), ())), preferred_element_type=f32)


def sigmoid(a):
    return 1.0 / (1.0 + jnp.exp(-a))


def normalise(values):
    centred = values - jnp.mean(values, -1, keepdims=True)
    inverse = lax.rsqrt(jnp.mean(centred * centred, -1, keepdims=True) + norm_eps)
    return centred * inverse, inverse


def norm_back(upstream, scaled, inverse, gain):
    inner = upstream * gain
    centred = inner - jnp.mean(inner, -1, keepdims=True)
    return inverse * (centred - scaled * jnp.mean(inner * scaled, -1, keepdims=True))


class Shape:
    def __init__(self, count, span, groups, stretches, width, inner):
        self.count, self.span, self.groups, self.stretches = count, span, groups, stretches
        self.width, self.inner = width, inner
        self.segs = groups * stretches
        self.rows = span * self.segs
        self.depth = count // 4
        self.chip = width // count
        self.own = self.chip // 2
        self.parts = inner // width
        self.mats = FIRST_PART + 2 * self.parts
        self.half = width // 2

    def fits(self):
        return (
            self.count % 4 == 0 and self.chip % 16 == 0 and self.own % 8 == 0 and self.own <= 32
            and self.half % 128 == 0 and self.groups == 8 and self.stretches == 2
            and self.parts == 4 and self.inner % self.width == 0 and self.rows <= 1024
        )


class Place:
    def __init__(self, sh):
        self.sh = sh
        self.s = lax.axis_index("seq")
        self.r = lax.axis_index("rep")
        self.z = self.s // 4
        self.y = lax.rem(self.s // 2, 2)
        self.x = lax.rem(self.s, 2)

    def device(self, z, y, x, r):
        return ((z * 2 + y) * 2 + x, r)

    def sibling(self):
        return (self.s, 1 - self.r)

    def x_peer(self):
        return self.device(self.z, self.y, 1 - self.x, self.r)

    def y_peer(self):
        return self.device(self.z, 1 - self.y, self.x, self.r)

    def z_to(self, j):
        return lax.rem(self.z + 1 + j, self.sh.depth)

    def z_from(self, j):
        return lax.rem(self.z + self.sh.depth - 1 - j, self.sh.depth)

    def z_peer(self, j):
        return self.device(self.z_to(j), self.y, self.x, self.r)

    def ring(self, step):
        count = self.sh.count
        return (lax.rem(self.s + count + step, count), self.r)

    def a_peer(self):
        flip_y, flip_x = 1 - self.r, self.r
        y = self.y + flip_y * (1 - 2 * self.y)
        x = self.x + flip_x * (1 - 2 * self.x)
        return self.device(self.z, y, x, self.r)

    def b_peer(self):
        flip_y, flip_x = self.r, 1 - self.r
        y = self.y + flip_y * (1 - 2 * self.y)
        x = self.x + flip_x * (1 - 2 * self.x)
        return self.device(self.z, y, x, self.r)

    def columns(self, r):
        half = self.sh.half
        return pl.ds(pl.multiple_of(r * half, half), half)


def send(src, dst, sems, index, device):
    return pltpu.make_async_remote_copy(
        src_ref=src, dst_ref=dst, send_sem=sems[0].at[index], recv_sem=sems[1].at[index],
        device_id=device, device_id_type=MESH,
    )


class Gather:
    def __init__(self, at, buf, lead, sems, group):
        self.at, self.buf, self.lead, self.sems, self.group = at, buf, lead, sems, group
        self.mine = at.columns(at.r)

    def cut(self, z, y, x):
        return self.buf.at[self.lead + (z, y, x, slice(None), self.mine)]

    def z_copy(self, j):
        at = self.at
        block = self.cut(at.z, at.y, at.x)
        return send(block, block, self.sems, (self.group, j), at.z_peer(j))

    def a_copy(self):
        at = self.at
        block = self.cut(slice(None), at.y, at.x)
        return send(block, block, self.sems, (self.group, at.sh.depth - 1), at.a_peer())

    def b_copy(self, core):
        at = self.at
        block = self.cut(slice(None), slice(None), at.x) if core == 0 else self.cut(
            slice(None), at.y, slice(None)
        )
        return send(block, block, self.sems, (self.group, at.sh.depth), at.b_peer())

    def core_copy(self):
        at = self.at
        block = self.cut(slice(None), slice(None), slice(None))
        return send(block, block, self.sems, (self.group, at.sh.depth + 1), at.sibling())

    def z_start(self):
        for j in range(self.at.sh.depth - 1):
            self.z_copy(j).start()

    def z_wait(self):
        for j in range(self.at.sh.depth - 1):
            self.z_copy(j).wait_recv()

    def a_start(self):
        self.a_copy().start()

    def a_wait(self):
        self.a_copy().wait_recv()

    def b_start(self):
        for core in range(2):
            @pl.when(self.at.r == core)
            def _():
                self.b_copy(core).start()

    def b_wait(self):
        self.b_copy(0).wait_recv()

    def core_start(self):
        self.core_copy().start()

    def core_wait(self):
        self.core_copy().wait_recv()

    def sent(self):
        for j in range(self.at.sh.depth - 1):
            self.z_copy(j).wait_send()
        self.a_copy().wait_send()
        self.b_copy(0).wait_send()
        self.core_copy().wait_send()

    def step(self, stage):
        if stage == 0:
            self.z_start()
        elif stage == 1:
            self.z_wait()
            self.a_start()
        elif stage == 2:
            self.a_wait()
            self.b_start()
        elif stage == 3:
            self.b_wait()
            self.core_start()
        else:
            self.core_wait()


def enter(at):
    sh = at.sh
    partners = [at.sibling(), at.x_peer(), at.y_peer(), at.ring(1), at.ring(-1)]
    partners += [at.z_peer(j) for j in range(sh.depth - 1)]
    barrier = pltpu.get_barrier_semaphore()
    for partner in partners:
        pl.semaphore_signal(barrier, inc=1, device_id=partner, device_id_type=MESH)
    pl.semaphore_wait(barrier, len(partners))


def slab(p, segs):
    return pl.ds(pl.multiple_of(p * segs, segs), segs)


def to_position_major(sh, stage, lanes, dest):
    for j in range(sh.width // 128):
        slot = j % 2
        columns = slice(j * 128, (j + 1) * 128)
        lanes[slot] = stage[:, columns].astype(f32)

        def move(p, _):
            both_stretches = [
                lanes[slot, pl.ds(p + st * sh.span, sh.groups, stride=sh.stretches * sh.span), :]
                for st in range(sh.stretches)
            ]
            dest[slab(p, sh.segs), columns] = jnp.concatenate(both_stretches, 0).astype(dest.dtype)
            return 0

        lax.fori_loop(0, sh.span, move, 0, unroll=4)


def wrap_before(sh, at, got):
    half = sh.groups
    wrapped = jnp.concatenate([jnp.zeros((half, sh.width), f32), got[:half]], 0)
    return jnp.where(at.s == 0, wrapped, got)


def wrap_after(sh, at, got):
    half = sh.groups
    wrapped = jnp.concatenate([got[half:], jnp.zeros((half, sh.width), f32)], 0)
    return jnp.where(at.s == sh.count - 1, wrapped, got)


def decay_over(rate, positions):
    return jnp.exp(-positions * rate)


class Exchange:
    def __init__(self, sh, at, planes, xy, zs, sems):
        self.sh, self.at, self.planes = sh, at, planes
        self.xy, self.zs, self.sems = xy, zs, sems

    def x_copy(self):
        return send(self.xy.at[0], self.xy.at[1], self.sems, 0, self.at.x_peer())

    def y_copy(self):
        return send(self.xy.at[2], self.xy.at[3], self.sems, 1, self.at.y_peer())

    def z_copy(self, j):
        return send(self.xy.at[4], self.zs.at[j], self.sems, 2 + j, self.at.z_peer(j))

    def sent(self):
        self.x_copy().wait_send()
        self.y_copy().wait_send()
        for j in range(self.sh.depth - 1):
            self.z_copy(j).wait_send()


class Forward(Exchange):
    def start(self, totals):
        for i, part in enumerate(totals):
            self.xy[0, i] = part
        self.x_copy().start()

    def after_x(self, rate):
        sh, at = self.sh, self.at
        self.x_copy().wait_recv()
        fade = decay_over(rate, float(sh.span))
        for i in range(2):
            own, other = self.xy[0, i], self.xy[1, i]
            first = jnp.where(at.x == 0, own, other)
            second = jnp.where(at.x == 0, other, own)
            self.xy[2, i] = fade * first + second
        self.y_copy().start()

    def after_y(self, rate):
        sh, at = self.sh, self.at
        self.y_copy().wait_recv()
        fade = decay_over(rate, 2.0 * sh.span)
        for i in range(2):
            own, other = self.xy[2, i], self.xy[3, i]
            first = jnp.where(at.y == 0, own, other)
            second = jnp.where(at.y == 0, other, own)
            self.xy[4, i] = fade * first + second
        for j in range(sh.depth - 1):
            self.z_copy(j).start()

    def after_z(self, rate, carry, total):
        sh, at = self.sh, self.at
        for j in range(sh.depth - 1):
            self.z_copy(j).wait_recv()
        plane = 4.0 * sh.span
        z = at.z.astype(f32)
        within = (2 * at.y + at.x).astype(f32) * sh.span
        x_span = at.x.astype(f32) * sh.span
        for i in range(2):
            every = decay_over(rate, (sh.depth - 1.0 - z) * plane) * self.xy[4, i]
            before = jnp.zeros_like(every)
            for j in range(sh.depth - 1):
                other = at.z_from(j)
                o = other.astype(f32)
                got = self.zs[j, i]
                gap = jnp.maximum(z - 1.0 - o, 0.0) * plane
                before += jnp.where(other < at.z, decay_over(rate, gap), 0.0) * got
                every += decay_over(rate, (sh.depth - 1.0 - o) * plane) * got
            state = decay_over(rate, within) * before
            state += jnp.where(at.y == 1, decay_over(rate, x_span), 0.0) * self.xy[3, i]
            state += jnp.where(at.x == 1, 1.0, 0.0) * self.xy[1, i]
            half = sh.groups
            earlier = decay_over(rate, z * plane + within) * every[:half]
            carry[i] = state + jnp.concatenate([jnp.zeros_like(earlier), earlier], 0)
            total[i] = every


class Tops(Exchange):
    def start(self, own):
        self.xy[0, 0] = own
        self.x_copy().start()

    def after_x(self, rate):
        sh, at = self.sh, self.at
        self.x_copy().wait_recv()
        own, other = self.xy[0, 0], self.xy[1, 0]
        first = jnp.where(at.x == 0, own, other)
        second = jnp.where(at.x == 0, other, own)
        self.xy[2, 0] = jnp.maximum(first - sh.span * rate, second)
        self.y_copy().start()

    def after_y(self, rate):
        sh, at = self.sh, self.at
        self.y_copy().wait_recv()
        own, other = self.xy[2, 0], self.xy[3, 0]
        first = jnp.where(at.y == 0, own, other)
        second = jnp.where(at.y == 0, other, own)
        self.xy[4, 0] = jnp.maximum(first - 2.0 * sh.span * rate, second)
        for j in range(sh.depth - 1):
            self.z_copy(j).start()

    def after_z(self, rate):
        sh, at = self.sh, self.at
        for j in range(sh.depth - 1):
            self.z_copy(j).wait_recv()
        plane = 4.0 * sh.span
        most = self.xy[4, 0] - (sh.depth - 1.0 - at.z.astype(f32)) * plane * rate
        for j in range(sh.depth - 1):
            gap = (sh.depth - 1.0 - at.z_from(j).astype(f32)) * plane
            most = jnp.maximum(most, self.zs[j, 0] - gap * rate)
        half = sh.groups
        return jnp.maximum(most[:half] - float(sh.count * sh.span) * rate, most[half:])


class Backward(Exchange):
    def start(self, totals):
        for i, part in enumerate(totals):
            self.xy[0, i] = part
        self.x_copy().start()

    def after_x(self, rate):
        sh, at = self.sh, self.at
        self.x_copy().wait_recv()
        fade = decay_over(rate, float(sh.span))
        for i in range(2):
            own, other = self.xy[0, i], self.xy[1, i]
            first = jnp.where(at.x == 0, own, other)
            second = jnp.where(at.x == 0, other, own)
            self.xy[2, i] = first + fade * second
        self.y_copy().start()

    def after_y(self, rate):
        sh, at = self.sh, self.at
        self.y_copy().wait_recv()
        fade = decay_over(rate, 2.0 * sh.span)
        for i in range(2):
            own, other = self.xy[2, i], self.xy[3, i]
            first = jnp.where(at.y == 0, own, other)
            second = jnp.where(at.y == 0, other, own)
            self.xy[4, i] = first + fade * second
        for j in range(sh.depth - 1):
            self.z_copy(j).start()

    def after_z(self, rate, carry):
        sh, at = self.sh, self.at
        for j in range(sh.depth - 1):
            self.z_copy(j).wait_recv()
        plane = 4.0 * sh.span
        z = at.z.astype(f32)
        beyond = (3 - 2 * at.y - at.x).astype(f32) * sh.span
        x_span = (1 - at.x).astype(f32) * sh.span
        for i in range(2):
            every = decay_over(rate, z * plane) * self.xy[4, i]
            after = jnp.zeros_like(every)
            for j in range(sh.depth - 1):
                other = at.z_from(j)
                o = other.astype(f32)
                got = self.zs[j, i]
                gap = jnp.maximum(o - z - 1.0, 0.0) * plane
                after += jnp.where(other > at.z, decay_over(rate, gap), 0.0) * got
                every += decay_over(rate, o * plane) * got
            state = decay_over(rate, beyond) * after
            state += jnp.where(at.y == 0, decay_over(rate, x_span), 0.0) * self.xy[3, i]
            state += jnp.where(at.x == 0, 1.0, 0.0) * self.xy[1, i]
            half = sh.groups
            gap = (sh.depth - 1.0 - z) * plane + beyond
            later = decay_over(rate, gap) * every[half:]
            carry[i] = state + jnp.concatenate([later, jnp.zeros_like(later)], 0)


class Scatter:
    def __init__(self, at, buf, mats, bufs, sems, group, final, result):
        self.at, self.buf, self.sems, self.group = at, buf, sems, group
        self.m0, self.m1 = mats
        self.to = result
        self.core_in, self.b_in, self.a_in, self.z_in = [b.at[group % 2] for b in bufs]
        self.final, self.out = final
        self.mine, self.theirs = at.columns(at.r), at.columns(1 - at.r)
        self.stage = 0

    def cut(self, z, y, x, columns):
        return self.buf.at[pl.ds(self.m0, self.m1 - self.m0), z, y, x, :, columns]

    def core_copy(self):
        every = slice(None)
        n = self.m1 - self.m0
        return send(
            self.cut(every, every, every, self.theirs), self.core_in.at[pl.ds(0, n)], self.sems,
            (self.group, 0), self.at.sibling(),
        )

    def b_copy(self, core):
        at, every = self.at, slice(None)
        n = self.m1 - self.m0
        src = (
            self.cut(every, every, 1 - at.x, self.mine) if core == 0
            else self.cut(every, 1 - at.y, every, self.mine)
        )
        return send(src, self.b_in.at[pl.ds(0, n)], self.sems, (self.group, 1), at.b_peer())

    def a_copy(self):
        at, every = self.at, slice(None)
        n = self.m1 - self.m0
        y = at.y + (1 - at.r) * (1 - 2 * at.y)
        x = at.x + at.r * (1 - 2 * at.x)
        return send(
            self.cut(every, y, x, self.mine), self.a_in.at[pl.ds(0, n)], self.sems,
            (self.group, 2), at.a_peer(),
        )

    def z_copy(self, j):
        at = self.at
        n = self.m1 - self.m0
        return send(
            self.cut(at.z_to(j), at.y, at.x, self.mine), self.z_in.at[j, pl.ds(0, n)], self.sems,
            (self.group, 3 + j), at.z_peer(j),
        )

    def rows_of(self, r):
        own = self.at.sh.own
        return pl.ds(pl.multiple_of(r * own, own), own)

    def last_copy(self):
        at, n = self.at, self.m1 - self.m0
        return send(
            self.final.at[pl.ds(self.to, n), self.rows_of(1 - at.r)],
            self.out.at[pl.ds(self.to, n), :, self.mine], self.sems,
            (self.group, 2 + at.sh.depth), at.sibling(),
        )

    def add(self, at_index, got_index):
        buf, mine = self.buf, self.mine
        m, z, y, x = at_index
        total = buf[m, z, y, x, :, mine].astype(f32) + got_index.astype(f32)
        buf[m, z, y, x, :, mine] = total.astype(bf16)

    def advance(self):
        at, sh = self.at, self.at.sh
        n = self.m1 - self.m0
        if self.stage == 0:
            self.core_copy().start()
        elif self.stage == 1:
            self.core_copy().wait_recv()

            def each(i, _):
                m, z = i // sh.depth, lax.rem(i, sh.depth)
                for y in range(2):
                    for x in range(2):
                        self.add((self.m0 + m, z, y, x), self.core_in[m, z, y, x])
                return 0

            lax.fori_loop(0, n * sh.depth, each, 0)
            for core in range(2):
                @pl.when(at.r == core)
                def _():
                    self.b_copy(core).start()
        elif self.stage == 2:
            self.b_copy(0).wait_recv()

            def each(i, _):
                m, z = i // sh.depth, lax.rem(i, sh.depth)
                for q in range(2):
                    y = (1 - at.r) * q + at.r * at.y
                    x = at.r * q + (1 - at.r) * at.x
                    self.add((self.m0 + m, z, y, x), self.b_in[m, z, q])
                return 0

            lax.fori_loop(0, n * sh.depth, each, 0)
            self.a_copy().start()
        elif self.stage == 3:
            self.a_copy().wait_recv()

            def each(i, _):
                m, z = i // sh.depth, lax.rem(i, sh.depth)
                self.add((self.m0 + m, z, at.y, at.x), self.a_in[m, z])
                return 0

            lax.fori_loop(0, n * sh.depth, each, 0)
            for j in range(sh.depth - 1):
                self.z_copy(j).start()
        elif self.stage == 4:
            for j in range(sh.depth - 1):
                self.z_copy(j).wait_recv()
            for m in range(n):
                total = self.buf[self.m0 + m, at.z, at.y, at.x, :, self.mine].astype(f32)
                for j in range(sh.depth - 1):
                    total += self.z_in[j, m].astype(f32)
                self.final[self.to + m] = total
                self.out[self.to + m, :, self.mine] = self.final[self.to + m, self.rows_of(at.r)]
            self.last_copy().start()
        elif self.stage == 5:
            self.last_copy().wait_recv()
        self.stage += 1

    def sent(self):
        self.core_copy().wait_send()
        self.b_copy(0).wait_send()
        self.a_copy().wait_send()
        for j in range(self.at.sh.depth - 1):
            self.z_copy(j).wait_send()
        self.last_copy().wait_send()


def from_position_major(sh, source, lanes, narrow, dest_hbm, sems):
    copies = []
    for j in range(sh.width // 128):
        slot = j % 2
        if j >= 2:
            copies[j - 2].wait()

        def move(p, _):
            block = source[slab(p, sh.segs), j * 128 : (j + 1) * 128]
            for st in range(sh.stretches):
                lanes[slot, pl.ds(p + st * sh.span, sh.groups, stride=sh.stretches * sh.span), :] = (
                    block[st * sh.groups : (st + 1) * sh.groups]
                )
            return 0

        lax.fori_loop(0, sh.span, move, 0, unroll=4)
        held = lanes.at[slot]
        if narrow is not None:
            narrow[slot] = lanes[slot].astype(bf16)
            held = narrow.at[slot]
        copy = pltpu.make_async_copy(held, dest_hbm.at[:, j * 128 : (j + 1) * 128], sems.at[j])
        copy.start()
        copies.append(copy)
    return copies[-2:]


def layer_kernel(
    sh,
    tok_hbm, cot_hbm, pack_ref,
    out_hbm, ig_hbm, grads_out, small_out, final_out, den_park, gate_park, key_park, value_park,
    gatein_park,
    w, vall, vecs, got_pack, lanes, narrow,
    f0, f1, f2, f3, f4, f5, xp, b1, b2, b3, b4, k, v, cotp, b8, b9,
    halo, halo32, st_xy, st_z, bk_xy, bk_z, top_xy, top_z, carry, total, acc, tile, plane,
    core_in, b_in, a_in, z_in, final,
    local_sem, pack_sems, ag_send, ag_recv, st_send, st_recv, bk_send, bk_recv, top_send, top_recv,
    halo_send, halo_recv, rs_send, rs_recv, tile_send, tile_recv, emit_sem,
):
    at = Place(sh)
    segs, span, rows, width = sh.segs, sh.span, sh.rows, sh.width
    mine, theirs = at.columns(at.r), at.columns(1 - at.r)
    gathers = [
        Gather(at, w, (pl.ds(a, b - a),), (ag_send, ag_recv), g) for g, (a, b) in enumerate(GROUPS)
    ]
    gather_v = Gather(at, vall, (), (ag_send, ag_recv), len(GROUPS))
    halo_sems = (halo_send, halo_recv)

    def local(src, dst, i):
        return pltpu.make_async_copy(src, dst, local_sem.at[i])

    def matrix(m):
        return w[m].reshape(width, width)

    def set_matrix(m, value):
        w[m] = value.astype(bf16).reshape(sh.depth, 2, 2, sh.chip, width)

    def vec(i):
        return vecs[i : i + 1, :]

    load_tok = local(tok_hbm, b1, 0)
    load_tok.start()
    enter(at)
    pack_copy = send(
        pack_ref.at[:, :, theirs], got_pack, (pack_sems.at[0], pack_sems.at[1]), 0, at.sibling()
    )
    pack_copy.start()
    load_tok.wait()
    to_position_major(sh, b1, lanes, xp)
    halo_x = send(xp.at[pl.ds(rows - segs, segs)], halo.at[0], halo_sems, 0, at.ring(1))
    halo_x.start()
    load_cot = local(cot_hbm, b1, 1)
    load_cot.start()

    pack_copy.wait_recv()
    for m in range(sh.mats):
        own = pack_ref[m, : sh.own, mine].astype(f32)
        other = got_pack[m, : sh.own].astype(f32)
        first = jnp.where(at.r == 0, own, other)
        second = jnp.where(at.r == 0, other, own)
        w[m, at.z, at.y, at.x, :, mine] = jnp.concatenate([first, second], 0).astype(bf16)
    vall[at.z, at.y, at.x, :, mine] = (
        pack_ref[sh.mats, :16, mine].astype(f32) + got_pack[sh.mats, :16].astype(f32)
    ).astype(bf16)
    gather_v.step(0)
    gathers[0].step(0)
    gathers[1].step(0)
    load_cot.wait()
    to_position_major(sh, b1, lanes, cotp)
    gather_v.step(1)
    gathers[0].step(1)
    gathers[2].step(0)
    gather_v.step(2)
    gathers[0].step(2)
    gathers[1].step(1)
    gathers[3].step(0)
    gather_v.step(3)
    gather_v.step(4)
    spread = jnp.zeros((16, width), f32)
    for z in range(sh.depth):
        for i in range(4):
            spread += vall[z, i // 2, i % 2].astype(f32)
    vecs[...] = spread

    key_in, value_in, gate_in = b2, b3, b4
    halo_x.wait_recv()
    got, _ = normalise(halo[0].astype(f32))
    before_one = wrap_before(sh, at, got * vec(MIXER_G) + vec(MIXER_B))

    def blend_one(p, before):
        here = slab(p, segs)
        n1, _ = normalise(xp[here, :].astype(f32))
        one = n1 * vec(MIXER_G) + vec(MIXER_B)
        step = one - before
        key_in[here, :] = (before + step * vec(KEY_SHARE)).astype(bf16)
        value_in[here, :] = (before + step * vec(VALUE_SHARE)).astype(bf16)
        gate_in[here, :] = (before + step * vec(GATE_SHARE)).astype(bf16)
        return one

    lax.fori_loop(0, span, blend_one, before_one)
    parks = [local(key_in, key_park, 2), local(value_in, value_park, 3), local(gate_in, gatein_park, 4)]
    for copy in parks:
        copy.start()

    gathers[0].step(3)
    gathers[1].step(2)
    gathers[2].step(1)
    gathers[4].step(0)
    gathers[0].step(4)
    k[...] = dot(key_in[...], matrix(KEY)).astype(bf16)
    v[...] = dot(value_in[...], matrix(VALUE)).astype(bf16)

    rate = jnp.exp(vec(DECAY))
    keep = jnp.exp(-rate)
    zero = jnp.zeros((segs, width), f32)

    def add_up(p, state):
        a, b, top = state
        here = slab(p, segs)
        key = k[here, :].astype(f32)
        grown = jnp.exp(key)
        top = jnp.maximum(top - rate, key)
        return keep * a + grown * v[here, :].astype(f32), keep * b + grown, top

    sum_num, sum_den, top = lax.fori_loop(
        0, span, add_up, (zero, zero, jnp.full((segs, width), -jnp.inf, f32))
    )
    states = Forward(sh, at, 2, st_xy, st_z, (st_send, st_recv))
    states.start((sum_num, sum_den))
    tops = Tops(sh, at, 1, top_xy, top_z, (top_send, top_recv))
    tops.start(top)

    gathers[1].step(3)
    gathers[2].step(2)
    gathers[3].step(1)
    gathers[5].step(0)
    states.after_x(rate)
    gathers[1].step(4)
    gate = f1
    gate[...] = sigmoid(dot(gate_in[...], matrix(GATE)))
    gate_out = local(gate, gate_park, 5)
    gate_out.start()
    states.after_y(rate)
    tops.after_x(rate)
    gathers[2].step(3)
    gathers[3].step(2)
    gathers[4].step(1)
    states.after_z(rate, carry, total)
    tops.after_y(rate)

    num, den, res, s2 = f3, f2, f4, f5
    gated, rg, hin, sin = b8, b9, b2, b3
    boost_rate = jnp.exp(vec(FIRST))

    def recur(p, state):
        a, b = state
        here = slab(p, segs)
        grown = jnp.exp(k[here, :].astype(f32))
        value = v[here, :].astype(f32)
        boost = grown * boost_rate
        num[here, :] = a
        den[here, :] = b
        mix = ((a + boost * value) / (b + boost)).astype(bf16).astype(f32)
        gated[here, :] = (gate[here, :] * mix).astype(bf16)
        return keep * a + grown * value, keep * b + grown

    lax.fori_loop(0, span, recur, (carry[0], carry[1]))
    den_out = local(den, den_park, 6)
    den_out.start()
    res[...] = xp[...].astype(f32) + dot(gated[...], matrix(OUTPUT))

    last = pl.ds(rows - segs, segs)
    n2, _ = normalise(res[last, :])
    halo32[0] = n2 * vec(CHANNEL_G) + vec(CHANNEL_B)
    halo_two = send(halo32.at[0], halo32.at[1], halo_sems, 1, at.ring(1))
    halo_two.start()
    gathers[3].step(3)
    gathers[4].step(2)
    gathers[5].step(1)
    final_top = tops.after_z(rate)
    far = decay_over(rate, float(sh.count * span))
    scale = jnp.exp(-final_top)
    for i in range(2):
        final_out[i] = (far * total[i, : sh.groups] + total[i, sh.groups :]) * scale
    final_out[2] = final_top
    for copy in parks:
        copy.wait()
    halo_two.wait_recv()
    before_two = wrap_before(sh, at, halo32[1])

    def blend_two(p, before):
        here = slab(p, segs)
        n2, _ = normalise(res[here, :])
        two = n2 * vec(CHANNEL_G) + vec(CHANNEL_B)
        step = two - before
        hin[here, :] = (before + step * vec(HIDDEN_SHARE)).astype(bf16)
        sin[here, :] = (before + step * vec(SCREEN_SHARE)).astype(bf16)
        return two

    lax.fori_loop(0, span, blend_two, before_two)
    s2[...] = sigmoid(dot(sin[...], matrix(SCREEN)))
    rg[...] = (cotp[...].astype(f32) * s2[...]).astype(bf16)
    gate_out.wait()
    den_out.wait()

    bufs = (core_in, b_in, a_in, z_in)

    def scatter(group, m0, m1, result=None):
        return Scatter(
            at, w, (m0, m1), bufs, (rs_send, rs_recv), group, (final, grads_out),
            m0 if result is None else result,
        )

    flying, landed = [], []

    def tick():
        for one in list(flying):
            one.advance()
            if one.stage == 6:
                flying.remove(one)
                landed.append(one)

    def launch(one):
        one.advance()
        flying.append(one)

    relu, ret, hb, act, hg = f0, f1, f2, b4, b1
    for c in range(sh.parts):
        if c == 0:
            gathers[2].step(4)
            gathers[4].step(3)
            gathers[5].step(2)
        elif c == 1:
            gathers[3].step(4)
        elif c == 2:
            gathers[4].step(4)
        else:
            gathers[5].step(4)
        into, back = FIRST_PART + 2 * c, FIRST_PART + 2 * c + 1
        up = jnp.maximum(dot(hin[...], matrix(into)), 0.0)
        relu[...] = up
        act[...] = (up * up).astype(bf16)
        if c == 0:
            ret[...] = dot(act[...], matrix(back))
        else:
            ret[...] += dot(act[...], matrix(back))
        hg[...] = (dot_nt(rg[...], matrix(back)) * (2.0 * relu[...])).astype(bf16)
        if c == 1:
            gathers[5].step(3)
        tick()
        if c == 0:
            hb[...] = dot_nt(hg[...], matrix(into))
        else:
            hb[...] += dot_nt(hg[...], matrix(into))
        gathers[2 + c].sent()
        set_matrix(back, dot_tn(act[...], rg[...]))
        set_matrix(into, dot_tn(hin[...], hg[...]))
        launch(scatter(c, into, back + 1))

    sg, sb, og = b4, f5, b1
    first = pl.ds(0, segs)
    cot0 = cotp[first, :].astype(f32)
    sg0 = (cot0 * ret[first, :] * s2[first, :] * (1.0 - s2[first, :])).astype(bf16)
    sb0 = dot_nt(sg0, matrix(SCREEN))
    halo32[2] = hb[first, :] * (1.0 - vec(HIDDEN_SHARE)) + sb0 * (1.0 - vec(SCREEN_SHARE))
    back_two = send(halo32.at[2], halo32.at[3], halo_sems, 2, at.ring(-1))
    back_two.start()
    load_gatein = local(gatein_park, b2, 7)
    load_gatein.start()
    acc[...] = jnp.zeros_like(acc)

    def finish(p, _):
        here = slab(p, segs)
        s = s2[here, :]
        held = ret[here, :]
        f0[here, :] = res[here, :] + s * held
        sg[here, :] = (cotp[here, :].astype(f32) * held * s * (1.0 - s)).astype(bf16)
        return 0

    lax.fori_loop(0, span, finish, 0)
    sb[...] = dot_nt(sg[...], matrix(SCREEN))
    tick()
    out_copies = from_position_major(sh, f0, lanes, narrow, out_hbm, emit_sem.at[0])

    back_two.wait_recv()
    after_two = wrap_after(sh, at, halo32[3])

    def back_second(p, before, ahead):
        here = slab(p, segs)
        n2, inverse = normalise(res[here, :])
        two = n2 * vec(CHANNEL_G) + vec(CHANNEL_B)
        step = two - before
        hb_here, sb_here = hb[here, :], sb[here, :]
        acc[0] += hb_here * step
        acc[1] += sb_here * step
        grad = hb_here * vec(HIDDEN_SHARE) + sb_here * vec(SCREEN_SHARE) + ahead
        acc[2] += grad * n2
        acc[3] += grad
        down = cotp[here, :].astype(f32) + norm_back(grad, n2, inverse, vec(CHANNEL_G))
        res[here, :] = down
        og[here, :] = down.astype(bf16)
        return two

    def back_second_step(p, before):
        there = slab(p + 1, segs)
        ahead = hb[there, :] * (1.0 - vec(HIDDEN_SHARE)) + sb[there, :] * (1.0 - vec(SCREEN_SHARE))
        return back_second(p, before, ahead)

    before = lax.fori_loop(0, span - 1, back_second_step, before_two)
    back_second(span - 1, before, after_two)
    rgrad = res

    for copy in out_copies:
        copy.wait()
    load_gate = local(gate_park, f2, 8)
    load_gate.start()
    load_den = local(den_park, f0, 9)
    load_den.start()
    gated_grad = f1
    gated_grad[...] = dot_nt(og[...], matrix(OUTPUT))
    gathers[1].sent()
    set_matrix(OUTPUT, dot_tn(gated[...], og[...]))
    set_matrix(SCREEN, dot_tn(sin[...], sg[...]))
    tick()
    launch(scatter(sh.parts, OUTPUT, SCREEN + 1))
    load_keyin = local(key_park, b3, 10)
    load_keyin.start()
    load_valin = local(value_park, cotp, 11)
    load_valin.start()
    load_gate.wait()
    load_den.wait()

    gate, den, gate_grad, mg = f2, f0, b9, b4

    def totals_back(i, state):
        a, b = state
        here = slab(span - 1 - i, segs)
        grown = jnp.exp(k[here, :].astype(f32))
        value = v[here, :].astype(f32)
        boost = grown * boost_rate
        over = 1.0 / (den[here, :] + boost)
        raw = (num[here, :] + boost * value) * over
        mix = raw.astype(bf16).astype(f32)
        grad, s = gated_grad[here, :], gate[here, :]
        through = (grad * s).astype(bf16)
        mg[here, :] = through
        gate_grad[here, :] = (grad * mix * s * (1.0 - s)).astype(bf16)
        num_grad = through.astype(f32) * over
        return keep * a + num_grad, keep * b - num_grad * raw

    sum_num, sum_den = lax.fori_loop(0, span, totals_back, (zero, zero))
    adjoints = Backward(sh, at, 2, bk_xy, bk_z, (bk_send, bk_recv))
    adjoints.start((sum_num, sum_den))
    gate_back = f5
    gate_back[...] = dot_nt(gate_grad[...], matrix(GATE))
    adjoints.after_x(rate)
    load_gatein.wait()
    set_matrix(GATE, dot_tn(b2[...], gate_grad[...]))
    adjoints.after_y(rate)
    tick()
    launch(scatter(sh.parts + 1, GATE, GATE + 1))
    adjoints.after_z(rate, carry)

    kg, vg = b8, b1

    def recur_back(i, state):
        a, b = state
        here = slab(span - 1 - i, segs)
        grown = jnp.exp(k[here, :].astype(f32))
        value = v[here, :].astype(f32)
        boost = grown * boost_rate
        n, d = num[here, :], den[here, :]
        over = 1.0 / (d + boost)
        num_grad = mg[here, :].astype(f32) * over
        den_grad = -num_grad * ((n + boost * value) * over)
        inner = boost * (value * num_grad + den_grad)
        kg[here, :] = (grown * (value * a + b) + inner).astype(bf16)
        vg[here, :] = (grown * a + boost * num_grad).astype(bf16)
        acc[4] += inner
        acc[5] += n * a + d * b
        return keep * a + num_grad, keep * b + den_grad

    lax.fori_loop(0, span, recur_back, (carry[0], carry[1]))
    load_keyin.wait()
    load_valin.wait()
    landed_first = scatter_done(landed, flying, 0, tick)
    landed_first.sent()
    spare = FIRST_PART
    set_matrix(spare, dot_tn(b3[...], kg[...]))
    tick()
    launch(scatter(sh.parts + 2, spare, spare + 1, KEY))
    set_matrix(spare + 1, dot_tn(cotp[...], vg[...]))
    tick()
    launch(scatter(sh.parts + 3, spare + 1, spare + 2, VALUE))

    key_back, value_back = f1, f2
    key_back[...] = dot_nt(kg[...], matrix(KEY))
    value_back[...] = dot_nt(vg[...], matrix(VALUE))

    def ahead_of(where):
        return (
            key_back[where, :] * (1.0 - vec(KEY_SHARE))
            + value_back[where, :] * (1.0 - vec(VALUE_SHARE))
            + gate_back[where, :] * (1.0 - vec(GATE_SHARE))
        )

    halo32[4] = ahead_of(first)
    back_one = send(halo32.at[4], halo32.at[5], halo_sems, 3, at.ring(-1))
    back_one.start()
    tick()
    back_one.wait_recv()
    after_one = wrap_after(sh, at, halo32[5])
    got, _ = normalise(halo[0].astype(f32))
    before_one = wrap_before(sh, at, got * vec(MIXER_G) + vec(MIXER_B))

    def back_first(p, before, ahead):
        here = slab(p, segs)
        n1, inverse = normalise(xp[here, :].astype(f32))
        one = n1 * vec(MIXER_G) + vec(MIXER_B)
        step = one - before
        kb, vb, gb = key_back[here, :], value_back[here, :], gate_back[here, :]
        acc[6] += kb * step
        acc[7] += vb * step
        acc[8] += gb * step
        grad = kb * vec(KEY_SHARE) + vb * vec(VALUE_SHARE) + gb * vec(GATE_SHARE) + ahead
        acc[9] += grad * n1
        acc[10] += grad
        f3[here, :] = rgrad[here, :] + norm_back(grad, n1, inverse, vec(MIXER_G))
        return one

    def back_first_step(p, before):
        return back_first(p, before, ahead_of(slab(p + 1, segs)))

    before = lax.fori_loop(0, span - 1, back_first_step, before_one)
    back_first(span - 1, before, after_one)

    def line(i):
        return jnp.sum(acc[i], 0, keepdims=True)

    order = (9, 10, 6, 7, 8, 5, 4, 2, 3, 0, 1)
    tile[0] = jnp.zeros((16, width), f32)
    for i, which in enumerate(order):
        value = line(which)
        if i == DECAY:
            value = -rate * keep * value
        tile[0, i : i + 1, :] = value
    tile_sems = (tile_send, tile_recv)
    sums = [
        send(tile.at[0], tile.at[1], tile_sems, 0, at.sibling()),
        send(tile.at[2], tile.at[3], tile_sems, 1, at.x_peer()),
        send(tile.at[4], tile.at[5], tile_sems, 2, at.y_peer()),
    ]
    sums[0].start()
    tick()
    ig_copies = from_position_major(sh, f3, lanes, None, ig_hbm, emit_sem.at[1])
    for i in range(2):
        sums[i].wait_recv()
        tile[2 * i + 2] = tile[2 * i] + tile[2 * i + 1]
        sums[i + 1].start()
        tick()
    sums[2].wait_recv()
    tile[6] = tile[4] + tile[5]
    far_sums = [
        send(tile.at[6], plane.at[j], tile_sems, 3 + j, at.z_peer(j)) for j in range(sh.depth - 1)
    ]
    for copy in far_sums:
        copy.start()
    while flying:
        tick()
    everything = tile[6]
    for j, copy in enumerate(far_sums):
        copy.wait_recv()
        everything += plane[j]
    small_out[...] = everything
    for copy in ig_copies:
        copy.wait()

    pack_copy.wait_send()
    halo_x.wait_send()
    for copy in (halo_two, back_two, back_one):
        copy.wait_send()
    gather_v.sent()
    gathers[0].sent()
    for one in landed:
        if one is not landed_first:
            one.sent()
    for exchange in (states, tops, adjoints):
        exchange.sent()
    for copy in sums + far_sums:
        copy.wait_send()


def scatter_done(landed, flying, group, tick):
    while not any(one.group == group for one in landed):
        tick()
    return [one for one in landed if one.group == group][0]


def layer(sh, tokens, cotangent, pack):
    R, D, S, Z = sh.rows, sh.width, sh.segs, sh.depth
    shape = jax.ShapeDtypeStruct
    narrow, wide = ((R, D), bf16), ((R, D), f32)
    w_shape = (sh.mats, Z, 2, 2, sh.chip, D)
    V = pltpu.VMEM
    dma = pltpu.SemaphoreType.DMA
    anywhere, in_vmem = pl.BlockSpec(memory_space=pl.ANY), pl.BlockSpec(memory_space=pltpu.VMEM)
    outs = [
        (narrow, anywhere), (wide, anywhere), (((sh.mats, sh.own, D), f32), in_vmem),
        (((16, D), f32), in_vmem), (((3, sh.groups, D), f32), in_vmem),
        (wide, anywhere), (wide, anywhere), (narrow, anywhere), (narrow, anywhere),
        (narrow, anywhere),
    ]
    scatters = sh.parts + 4
    scratch = (
        [
            V(w_shape, bf16), V((Z, 2, 2, 16, D), bf16), V((16, D), f32),
            V((sh.mats + 1, 32, sh.half), bf16), V((2, R, 128), f32), V((2, R, 128), bf16),
        ]
        + [V(*wide)] * 6
        + [V(*narrow)] * 10
        + [
            V((1, S, D), bf16), V((6, S, D), f32),
            V((5, 2, S, D), f32), V((Z - 1, 2, S, D), f32),
            V((5, 2, S, D), f32), V((Z - 1, 2, S, D), f32),
            V((5, 1, S, D), f32), V((Z - 1, 1, S, D), f32),
            V((2, S, D), f32), V((2, S, D), f32), V((VECTORS, S, D), f32),
            V((7, 16, D), f32), V((Z - 1, 16, D), f32),
            V((2, 2, Z, 2, 2, sh.chip, sh.half), bf16), V((2, 2, Z, 2, sh.chip, sh.half), bf16),
            V((2, 2, Z, sh.chip, sh.half), bf16), V((2, Z - 1, 2, sh.chip, sh.half), bf16),
            V((sh.mats, sh.chip, sh.half), f32),
            dma((12,)), dma((2, 1)),
        ]
        + [dma((len(GROUPS) + 1, Z + 2))] * 2
        + [dma((Z + 1,))] * 6
        + [dma((4,))] * 2
        + [dma((scatters, Z + 3))] * 2
        + [dma((Z + 2,))] * 2
        + [dma((2, D // 128))]
    )
    return pl.pallas_call(
        functools.partial(layer_kernel, sh),
        out_shape=[shape(s, t) for (s, t), _ in outs],
        in_specs=[anywhere, anywhere, in_vmem],
        out_specs=[spec for _, spec in outs],
        scratch_shapes=scratch,
        compiler_params=pltpu.CompilerParams(
            collective_id=0, has_side_effects=True, vmem_limit_bytes=63 * 2**20
        ),
    )(tokens.reshape(R, D), cotangent.reshape(R, D), pack)


def mm(left, right):
    return jnp.dot(left, right, preferred_element_type=f32)


def mm_nt(left, right):
    return lax.dot_general(left, right, (((1,), (1,)), ((), ())), preferred_element_type=f32)


def mm_tn(left, right):
    return lax.dot_general(left, right, (((0,), (0,)), ((), ())), preferred_element_type=f32)


def ring(value, steps):
    count = lax.axis_size("seq")
    return lax.ppermute(value, "seq", [(i, (i + steps) % count) for i in range(count)])


def entering(last, spot):
    got = ring(last, 1)
    pairs = got.reshape(-1, 2, got.shape[-1])
    wrapped = jnp.concatenate([jnp.zeros_like(pairs[:, :1]), pairs[:, :1]], 1)
    return jnp.where(spot == 0, wrapped, pairs).reshape(got.shape)


def leaving(first, spot):
    count = lax.axis_size("seq")
    got = ring(first, -1)
    pairs = got.reshape(-1, 2, got.shape[-1])
    wrapped = jnp.concatenate([pairs[:, 1:], jnp.zeros_like(pairs[:, :1])], 1)
    return jnp.where(spot == count - 1, wrapped, pairs).reshape(got.shape)


def plain_scan(k_ref, v_ref, carry_ref, decay_ref, first_ref, num_ref, den_ref, mix_ref):
    keep = jnp.exp(-jnp.exp(decay_ref[...]))
    boost_rate = jnp.exp(first_ref[...])

    def step(t, state):
        num, den = state
        k = jnp.exp(k_ref[t].astype(f32))
        v = v_ref[t].astype(f32)
        boost = k * boost_rate
        num_ref[t] = num
        den_ref[t] = den
        mix_ref[t] = (num + boost * v) / (den + boost)
        return keep * num + k * v, keep * den + k

    lax.fori_loop(0, k_ref.shape[0], step, (carry_ref[0], carry_ref[1]))


def plain_scan_back(
    k_ref, v_ref, num_ref, den_ref, mix_ref, grad_ref, carry_ref, decay_ref, first_ref,
    kg_ref, vg_ref, first_grad_ref, decay_grad_ref,
):
    keep = jnp.exp(-jnp.exp(decay_ref[...]))
    boost_rate = jnp.exp(first_ref[...])
    length = k_ref.shape[0]

    def step(i, state):
        adj_num, adj_den, first_sum, decay_sum = state
        t = length - 1 - i
        k = jnp.exp(k_ref[t].astype(f32))
        v = v_ref[t].astype(f32)
        boost = k * boost_rate
        num_grad = grad_ref[t].astype(f32) / (den_ref[t] + boost)
        den_grad = -num_grad * mix_ref[t]
        inner = boost * (v * num_grad + den_grad)
        kg_ref[t] = (k * (v * adj_num + adj_den) + inner).astype(bf16)
        vg_ref[t] = (k * adj_num + boost * num_grad).astype(bf16)
        first_sum = first_sum + inner
        decay_sum = decay_sum + num_ref[t] * adj_num + den_ref[t] * adj_den
        return keep * adj_num + num_grad, keep * adj_den + den_grad, first_sum, decay_sum

    zero = jnp.zeros_like(carry_ref[0])
    out = lax.fori_loop(0, length, step, (carry_ref[0], carry_ref[1], zero, zero))
    first_grad_ref[...] = out[2]
    decay_grad_ref[...] = out[3]


def call(kernel, shapes, *operands):
    space = pl.BlockSpec(memory_space=pltpu.VMEM)
    return pl.pallas_call(
        kernel,
        out_shape=[jax.ShapeDtypeStruct(s, t) for s, t in shapes],
        in_specs=[space] * len(operands),
        out_specs=[space] * len(shapes),
        compiler_params=pltpu.CompilerParams(vmem_limit_bytes=48 * 2**20),
    )(*operands)


def plain_body(
    tokens, mixer_gain, mixer_bias, key_blend, value_blend, gate_blend, time_decay, time_first,
    key_weight, value_weight, gate_weight, output_weight, channel_gain, channel_bias,
    hidden_blend, screen_blend, hidden_weight, screen_weight, return_weight, cotangent,
):
    groups, stretches, span, width = tokens.shape
    count = lax.axis_size("seq")
    owners = count * lax.axis_size("rep")
    spot = lax.axis_index("seq")
    segs = groups * stretches
    rows = span * segs
    own = width // owners
    inner = hidden_weight.shape[1]
    parts = inner // width

    vectors = (
        mixer_gain, mixer_bias, key_blend, value_blend, gate_blend, time_decay, time_first,
        channel_gain, channel_bias, hidden_blend, screen_blend,
    )
    squares = (key_weight, value_weight, gate_weight, output_weight, screen_weight)
    packed = jnp.concatenate(
        squares + (hidden_weight.reshape(own * parts, width), return_weight), 0
    )
    packed = lax.all_gather(packed, both, axis=0)
    spread_vectors = lax.all_gather(jnp.stack(vectors), both, axis=0)
    spread_vectors = jnp.swapaxes(spread_vectors, 0, 1).reshape(len(vectors), width).astype(f32)
    (
        mixer_g, mixer_b, key_share, value_share, gate_share, decay_log, first_log,
        channel_g, channel_b, hidden_share, screen_share,
    ) = [spread_vectors[i][None] for i in range(len(vectors))]

    def piece(start, size, shape):
        return packed[:, start : start + size].reshape(shape)

    w_key, w_value, w_gate, w_output, w_screen = [
        piece(own * i, own, (width, width)) for i in range(5)
    ]
    w_hidden = piece(own * 5, own * parts, (width, inner))
    w_return = piece(own * (5 + parts), own * parts, (inner, width))

    def position_major(a):
        return jnp.transpose(a, (2, 0, 1, 3)).reshape(rows, width)

    def shifted(a, first):
        return jnp.concatenate([first, a[:-segs]], 0)

    x = position_major(tokens).astype(f32)
    n1, inv1 = normalise(x)
    one = n1 * mixer_g + mixer_b
    before = shifted(one, entering(one[-segs:], spot))
    spread_one = one - before
    key_in = (before + spread_one * key_share).astype(bf16)
    value_in = (before + spread_one * value_share).astype(bf16)
    gate_in = (before + spread_one * gate_share).astype(bf16)
    k = mm(key_in, w_key).astype(bf16)
    v = mm(value_in, w_value).astype(bf16)
    gate = jax.nn.sigmoid(mm(gate_in, w_gate))

    rate = jnp.exp(decay_log)
    cube = (span, segs, width)
    offsets = jnp.arange(span, dtype=f32)[:, None, None]
    kw = k.reshape(cube).astype(f32)
    vw = v.reshape(cube).astype(f32)
    shifted_key = kw - (span - 1.0 - offsets) * rate
    ends = jnp.exp(shifted_key)
    totals = jnp.stack([jnp.sum(ends * vw, 0), jnp.sum(ends, 0)])
    tops = jnp.max(shifted_key, 0)
    everyone = lax.all_gather(jnp.concatenate([totals, tops[None]]), "seq", axis=0)
    everyone = everyone.reshape(count, 3, groups, stretches, width)
    everyone = jnp.transpose(everyone, (3, 0, 1, 2, 4)).reshape(
        stretches * count, 3, groups, width
    )
    order = jnp.arange(stretches * count, dtype=f32)

    def weights_for(here):
        gap = here - 1.0 - order[:, None]
        return jnp.where(gap >= 0, jnp.exp(-jnp.maximum(gap, 0.0) * (span * rate)), 0.0)

    def carried(here):
        return jnp.sum(weights_for(here)[:, None, None, :] * everyone[:, :2], 0)

    carry = jnp.stack([carried(j * count + spot.astype(f32)) for j in range(stretches)], 2)
    carry = carry.reshape(2, segs, width)
    final = carried(float(stretches * count))
    far = (stretches * count - 1.0 - order)[:, None] * (span * rate)
    top = jnp.max(everyone[:, 2] - far[:, None, :], 0)
    slab = width // count

    def own_slab(a):
        return lax.dynamic_slice_in_dim(a, spot * slab, slab, 1)

    final_top = own_slab(top)
    scaling = jnp.exp(-final_top)
    final_num = own_slab(final[0]) * scaling
    final_den = own_slab(final[1]) * scaling

    num, den, mix_raw = call(
        plain_scan, [(cube, f32)] * 3, k.reshape(cube), v.reshape(cube), carry,
        decay_log, first_log,
    )
    mix = mix_raw.reshape(rows, width).astype(bf16).astype(f32)
    gated = (gate * mix).astype(bf16)
    residual = x + mm(gated, w_output)
    n2, inv2 = normalise(residual)
    two = n2 * channel_g + channel_b
    before = shifted(two, entering(two[-segs:], spot))
    spread_two = two - before
    hidden_in = (before + spread_two * hidden_share).astype(bf16)
    screen_in = (before + spread_two * screen_share).astype(bf16)
    screen = jax.nn.sigmoid(mm(screen_in, w_screen))
    cot = position_major(cotangent).astype(f32)
    returned_grad = (cot * screen).astype(bf16)
    relu = jnp.maximum(mm(hidden_in, w_hidden), 0.0)
    act = jnp.square(relu).astype(bf16)
    returned = mm(act, w_return)
    output = (residual + screen * returned).astype(bf16)

    screen_grad = (cot * returned * screen * (1.0 - screen)).astype(bf16)
    hidden_grad = (mm_nt(returned_grad, w_return) * (2.0 * relu)).astype(bf16)
    dw_return = mm_tn(act, returned_grad)
    dw_hidden = mm_tn(hidden_in, hidden_grad)
    dw_screen = mm_tn(screen_in, screen_grad)
    hidden_back = mm_nt(hidden_grad, w_hidden)
    screen_back = mm_nt(screen_grad, w_screen)
    d_hidden_blend = jnp.sum(hidden_back * spread_two, 0)
    d_screen_blend = jnp.sum(screen_back * spread_two, 0)
    ahead = hidden_back * (1.0 - hidden_share) + screen_back * (1.0 - screen_share)
    two_grad = (
        hidden_back * hidden_share
        + screen_back * screen_share
        + jnp.concatenate([ahead[segs:], leaving(ahead[:segs], spot)], 0)
    )
    d_channel_gain = jnp.sum(two_grad * n2, 0)
    d_channel_bias = jnp.sum(two_grad, 0)
    residual_grad = cot + norm_back(two_grad, n2, inv2, channel_g)
    output_grad = residual_grad.astype(bf16)
    dw_output = mm_tn(gated, output_grad)
    gated_grad = mm_nt(output_grad, w_output)
    mix_grad = (gated_grad * gate).astype(bf16)
    gate_grad = (gated_grad * mix * gate * (1.0 - gate)).astype(bf16)

    boost = jnp.exp(first_log + kw)
    num_grad = mix_grad.reshape(cube).astype(f32) / (den + boost)
    den_grad = -num_grad * mix_raw
    fade = jnp.exp(-offsets * rate)
    totals = jnp.stack([jnp.sum(fade * num_grad, 0), jnp.sum(fade * den_grad, 0)])
    everyone = lax.all_gather(totals, "seq", axis=0)
    everyone = everyone.reshape(count, 2, groups, stretches, width)
    everyone = jnp.transpose(everyone, (3, 0, 1, 2, 4)).reshape(
        stretches * count, 2, groups, width
    )

    def carried_back(here):
        gap = order[:, None] - here - 1.0
        scale = jnp.where(gap >= 0, jnp.exp(-jnp.maximum(gap, 0.0) * (span * rate)), 0.0)
        return jnp.sum(scale[:, None, None, :] * everyone, 0)

    carry = jnp.stack([carried_back(j * count + spot.astype(f32)) for j in range(stretches)], 2)
    carry = carry.reshape(2, segs, width)
    key_grad, value_grad, first_sum, decay_sum = call(
        plain_scan_back, [(cube, bf16)] * 2 + [((segs, width), f32)] * 2,
        k.reshape(cube), v.reshape(cube), num, den, mix_raw, mix_grad.reshape(cube), carry,
        decay_log, first_log,
    )
    key_grad = key_grad.reshape(rows, width)
    value_grad = value_grad.reshape(rows, width)
    d_first = jnp.sum(first_sum, 0)
    d_decay = -rate[0] * jnp.exp(-rate[0]) * jnp.sum(decay_sum, 0)
    dw_key = mm_tn(key_in, key_grad)
    dw_value = mm_tn(value_in, value_grad)
    dw_gate = mm_tn(gate_in, gate_grad)
    key_back = mm_nt(key_grad, w_key)
    value_back = mm_nt(value_grad, w_value)
    gate_back = mm_nt(gate_grad, w_gate)
    d_key_blend = jnp.sum(key_back * spread_one, 0)
    d_value_blend = jnp.sum(value_back * spread_one, 0)
    d_gate_blend = jnp.sum(gate_back * spread_one, 0)
    ahead = (
        key_back * (1.0 - key_share)
        + value_back * (1.0 - value_share)
        + gate_back * (1.0 - gate_share)
    )
    one_grad = (
        key_back * key_share
        + value_back * value_share
        + gate_back * gate_share
        + jnp.concatenate([ahead[segs:], leaving(ahead[:segs], spot)], 0)
    )
    d_mixer_gain = jnp.sum(one_grad * n1, 0)
    d_mixer_bias = jnp.sum(one_grad, 0)
    input_grad = residual_grad + norm_back(one_grad, n1, inv1, mixer_g)

    packed = jnp.concatenate(
        [d.reshape(owners, own, width).astype(bf16) for d in (dw_key, dw_value, dw_gate, dw_output, dw_screen)]
        + [
            dw_hidden.reshape(owners, own * parts, width).astype(bf16),
            dw_return.reshape(owners, own * parts, width).astype(bf16),
        ],
        1,
    )
    summed = lax.psum_scatter(packed, both, scatter_dimension=0).astype(f32)
    small = jnp.stack(
        [
            d_mixer_gain, d_mixer_bias, d_key_blend, d_value_blend, d_gate_blend, d_decay, d_first,
            d_channel_gain, d_channel_bias, d_hidden_blend, d_screen_blend,
        ]
    )
    small = lax.psum(small, both)
    place = (spot * lax.axis_size("rep") + lax.axis_index("rep")) * own
    small = lax.dynamic_slice_in_dim(small, place, own, 1)

    def batch_major(a):
        return jnp.transpose(a.reshape(span, groups, stretches, width), (1, 2, 0, 3))

    return (
        batch_major(output),
        batch_major(input_grad),
        final_num,
        final_den,
        final_top,
        *[small[i] for i in range(7)],
        *[summed[own * i : own * (i + 1)] for i in range(4)],
        *[small[i] for i in range(7, 11)],
        summed[own * 5 : own * (5 + parts)].reshape(own, inner),
        summed[own * 4 : own * 5],
        summed[own * (5 + parts) :],
    )


def make_pack(sh, squares, hidden_weight, return_weight, vectors):
    own, width, parts = sh.own, sh.width, sh.parts
    owners = 2 * sh.count
    hidden = hidden_weight.reshape(own, owners, parts, own)
    hidden = jnp.transpose(hidden, (2, 0, 1, 3)).reshape(parts, own, width)
    back = return_weight.reshape(parts, own, width)
    both_parts = jnp.stack([hidden, back], 1).reshape(2 * parts, own, width)
    mats = jnp.concatenate([jnp.stack(squares), both_parts], 0)
    mats = jnp.pad(mats, ((0, 0), (0, 32 - own), (0, 0)))
    place = (lax.axis_index("seq") * 2 + lax.axis_index("rep")) * own
    tile = lax.dynamic_update_slice(
        jnp.zeros((32, width), bf16), jnp.stack(vectors), (0, place)
    )
    return jnp.concatenate([mats, tile[None]], 0)


def fused_body(sh, *args):
    (
        tokens, mixer_gain, mixer_bias, key_blend, value_blend, gate_blend, time_decay, time_first,
        key_weight, value_weight, gate_weight, output_weight, channel_gain, channel_bias,
        hidden_blend, screen_blend, hidden_weight, screen_weight, return_weight, cotangent,
    ) = args
    vectors = (
        mixer_gain, mixer_bias, key_blend, value_blend, gate_blend, time_decay, time_first,
        channel_gain, channel_bias, hidden_blend, screen_blend,
    )
    squares = (key_weight, value_weight, gate_weight, output_weight, screen_weight)
    pack = make_pack(sh, squares, hidden_weight, return_weight, vectors)
    output, input_grad, grads, small, finals = layer(sh, tokens, cotangent, pack)[:5]
    place = (lax.axis_index("seq") * 2 + lax.axis_index("rep")) * sh.own
    small = lax.dynamic_slice_in_dim(small, place, sh.own, 1)
    return (
        output.reshape(tokens.shape),
        input_grad.reshape(tokens.shape),
        *own_finals(sh, finals),
        *own_grads(sh, small, grads),
    )


def own_finals(sh, finals):
    share = sh.width // sh.count
    cut = lax.dynamic_slice_in_dim(finals, lax.axis_index("seq") * share, share, 2)
    return [cut[i] for i in range(3)]


def own_grads(sh, small, summed):
    own, owners, parts, inner = sh.own, 2 * sh.count, sh.parts, sh.inner
    hidden = summed[FIRST_PART::2].reshape(parts, own, owners, own)
    hidden = jnp.transpose(hidden, (1, 2, 0, 3)).reshape(own, inner)
    back = summed[FIRST_PART + 1 :: 2].reshape(parts * own, sh.width)
    return (
        *[small[i] for i in range(7)],
        *[summed[i] for i in (KEY, VALUE, GATE, OUTPUT)],
        *[small[i] for i in range(7, 11)],
        hidden,
        summed[SCREEN],
        back,
    )


def body(*args):
    tokens, hidden_weight = args[0], args[16]
    groups, stretches, span, width = tokens.shape
    sh = Shape(lax.axis_size("seq"), span, groups, stretches, width, hidden_weight.shape[1])
    if lax.axis_size("rep") == 2 and sh.fits():
        return fused_body(sh, *args)
    return plain_body(*args)


def solution(mesh):
    rows = P("rep", None, "seq", None)
    owned = P(both)
    owned_rows = P(both, None)
    in_specs = (rows,) + (owned,) * 7 + (owned_rows,) * 4 + (owned,) * 4 + (owned_rows,) * 3 + (rows,)
    out_specs = (
        (rows,) * 2 + (P("rep", "seq"),) * 3 + (owned,) * 7 + (owned_rows,) * 4
        + (owned,) * 4 + (owned_rows,) * 3
    )
    return jax.shard_map(body, mesh=mesh, in_specs=in_specs, out_specs=out_specs, check_vma=False)
```

```python
import functools

import jax
import jax.numpy as jnp
from jax import lax
from jax.experimental import pallas as pl
from jax.experimental.pallas import tpu as pltpu
from jax.sharding import PartitionSpec as P

f32 = jnp.float32
bf16 = jnp.bfloat16
norm_eps = 1e-05
both = ("seq", "rep")
MESH = pl.DeviceIdType.MESH

KEY, VALUE, GATE, OUTPUT, SCREEN, FIRST_PART = 0, 1, 2, 3, 4, 5
GATHER_AT = (0, 2, 3, 5, 6)
SCATTER_AT = (0, 1, 3, 5, 7, 8)
HELD = (2, 4, 4, 4)
VECTORS = 11
(
    MIXER_G, MIXER_B, KEY_SHARE, VALUE_SHARE, GATE_SHARE, DECAY, FIRST,
    CHANNEL_G, CHANNEL_B, HIDDEN_SHARE, SCREEN_SHARE,
) = range(VECTORS)


def dot(left, right):
    return jnp.dot(left, right, preferred_element_type=f32)


def dot_nt(left, right):
    return lax.dot_general(left, right, (((1,), (1,)), ((), ())), preferred_element_type=f32)


def dot_tn(left, right):
    return lax.dot_general(left, right, (((0,), (0,)), ((), ())), preferred_element_type=f32)


def sigmoid(a):
    return 1.0 / (1.0 + jnp.exp(-a))


def normalise(values):
    centred = values - jnp.mean(values, -1, keepdims=True)
    inverse = lax.rsqrt(jnp.mean(centred * centred, -1, keepdims=True) + norm_eps)
    return centred * inverse, inverse


def norm_back(upstream, scaled, inverse, gain):
    inner = upstream * gain
    centred = inner - jnp.mean(inner, -1, keepdims=True)
    return inverse * (centred - scaled * jnp.mean(inner * scaled, -1, keepdims=True))


class Shape:
    def __init__(self, count, span, groups, stretches, width, inner):
        self.count, self.span, self.groups, self.stretches = count, span, groups, stretches
        self.width, self.inner = width, inner
        self.segs = groups * stretches
        self.rows = span * self.segs
        self.depth = count // 4
        self.chip = width // count
        self.own = self.chip // 2
        self.parts = inner // width
        self.mats = FIRST_PART + 2 * self.parts
        self.half = width // 2

    def fits(self):
        return (
            self.count % 4 == 0 and self.chip % 16 == 0 and self.own % 8 == 0 and self.own <= 32
            and self.half % 128 == 0 and self.groups == 8 and self.stretches == 2
            and self.parts == 4 and self.inner % self.width == 0 and self.rows <= 1024
        )


class Place:
    def __init__(self, sh):
        self.sh = sh
        self.s = lax.axis_index("seq")
        self.r = lax.axis_index("rep")
        self.z = self.s // 4
        self.y = lax.rem(self.s // 2, 2)
        self.x = lax.rem(self.s, 2)

    def device(self, z, y, x, r):
        return ((z * 2 + y) * 2 + x, r)

    def sibling(self):
        return (self.s, 1 - self.r)

    def x_peer(self):
        return self.device(self.z, self.y, 1 - self.x, self.r)

    def y_peer(self):
        return self.device(self.z, 1 - self.y, self.x, self.r)

    def z_to(self, j):
        return lax.rem(self.z + 1 + j, self.sh.depth)

    def z_from(self, j):
        return lax.rem(self.z + self.sh.depth - 1 - j, self.sh.depth)

    def z_peer(self, j):
        return self.device(self.z_to(j), self.y, self.x, self.r)

    def plane_place(self, j):
        return (self.y if j == 0 else 1 - self.y, self.x if j == 1 else 1 - self.x)

    def plane_peer(self, j):
        y, x = self.plane_place(j)
        return self.device(self.z, y, x, self.r)

    def ring(self, step):
        count = self.sh.count
        return (lax.rem(self.s + count + step, count), self.r)

    def a_peer(self):
        flip_y, flip_x = 1 - self.r, self.r
        y = self.y + flip_y * (1 - 2 * self.y)
        x = self.x + flip_x * (1 - 2 * self.x)
        return self.device(self.z, y, x, self.r)

    def b_peer(self):
        flip_y, flip_x = self.r, 1 - self.r
        y = self.y + flip_y * (1 - 2 * self.y)
        x = self.x + flip_x * (1 - 2 * self.x)
        return self.device(self.z, y, x, self.r)

    def columns(self, r):
        half = self.sh.half
        return pl.ds(pl.multiple_of(r * half, half), half)


def send(src, dst, sems, index, device):
    return pltpu.make_async_remote_copy(
        src_ref=src, dst_ref=dst, send_sem=sems[0].at[index], recv_sem=sems[1].at[index],
        device_id=device, device_id_type=MESH,
    )


class Gather:
    def __init__(self, at, buf, lead, sems, group):
        self.at, self.buf, self.lead, self.sems, self.group = at, buf, lead, sems, group
        self.mine = at.columns(at.r)

    def cut(self, z, y, x):
        return self.buf.at[self.lead + (z, y, x, slice(None), self.mine)]

    def z_copy(self, j):
        at = self.at
        block = self.cut(at.z, at.y, at.x)
        return send(block, block, self.sems, (self.group, j), at.z_peer(j))

    def a_copy(self):
        at = self.at
        block = self.cut(slice(None), at.y, at.x)
        return send(block, block, self.sems, (self.group, at.sh.depth - 1), at.a_peer())

    def b_copy(self, core):
        at = self.at
        block = self.cut(slice(None), slice(None), at.x) if core == 0 else self.cut(
            slice(None), at.y, slice(None)
        )
        return send(block, block, self.sems, (self.group, at.sh.depth), at.b_peer())

    def core_copy(self):
        at = self.at
        block = self.cut(slice(None), slice(None), slice(None))
        return send(block, block, self.sems, (self.group, at.sh.depth + 1), at.sibling())

    def z_start(self):
        for j in range(self.at.sh.depth - 1):
            self.z_copy(j).start()

    def z_wait(self):
        for j in range(self.at.sh.depth - 1):
            self.z_copy(j).wait_recv()

    def a_start(self):
        self.a_copy().start()

    def a_wait(self):
        self.a_copy().wait_recv()

    def b_start(self):
        for core in range(2):
            @pl.when(self.at.r == core)
            def _():
                self.b_copy(core).start()

    def b_wait(self):
        self.b_copy(0).wait_recv()

    def core_start(self):
        self.core_copy().start()

    def core_wait(self):
        self.core_copy().wait_recv()

    def sent(self):
        for j in range(self.at.sh.depth - 1):
            self.z_copy(j).wait_send()
        self.a_copy().wait_send()
        self.b_copy(0).wait_send()
        self.core_copy().wait_send()

    def step(self, stage):
        if stage == 0:
            self.z_start()
        elif stage == 1:
            self.z_wait()
            self.a_start()
        elif stage == 2:
            self.a_wait()
            self.b_start()
        elif stage == 3:
            self.b_wait()
            self.core_start()
        else:
            self.core_wait()


def enter(at):
    sh = at.sh
    partners = [at.sibling(), at.ring(1), at.ring(-1)] + [at.plane_peer(j) for j in range(3)]
    partners += [at.z_peer(j) for j in range(sh.depth - 1)]
    barrier = pltpu.get_barrier_semaphore()
    for partner in partners:
        pl.semaphore_signal(barrier, inc=1, device_id=partner, device_id_type=MESH)
    pl.semaphore_wait(barrier, len(partners))


def slab(p, segs):
    return pl.ds(pl.multiple_of(p * segs, segs), segs)


def sequence_rows(sh, p, stretch):
    return pl.ds(p + stretch * sh.span, sh.groups, stride=sh.stretches * sh.span)


def to_position_major(sh, stage, lanes, dest):
    tiles = sh.width // 128
    for j in range(tiles):
        lanes[j] = stage[:, j * 128 : (j + 1) * 128].astype(f32)

    def move(p, _):
        for j in range(tiles):
            both_stretches = [
                lanes[j, sequence_rows(sh, p, st), :] for st in range(sh.stretches)
            ]
            dest[slab(p, sh.segs), j * 128 : (j + 1) * 128] = jnp.concatenate(
                both_stretches, 0
            ).astype(dest.dtype)
        return 0

    lax.fori_loop(0, sh.span, move, 0, unroll=4)


def wrap_before(sh, at, got):
    half = sh.groups
    wrapped = jnp.concatenate([jnp.zeros((half, sh.width), f32), got[:half]], 0)
    return jnp.where(at.s == 0, wrapped, got)


def wrap_after(sh, at, got):
    half = sh.groups
    wrapped = jnp.concatenate([got[half:], jnp.zeros((half, sh.width), f32)], 0)
    return jnp.where(at.s == sh.count - 1, wrapped, got)


def decay_over(rate, positions):
    return jnp.exp(-positions * rate)


class Exchange:
    def __init__(self, sh, at, onward, own, near, whole, far, sems):
        self.sh, self.at, self.onward = sh, at, onward
        self.own, self.near, self.whole, self.far, self.sems = own, near, whole, far, sems
        self.u = self.turn(2 * at.y + at.x, 4)
        self.v = self.turn(at.z, sh.depth)

    def turn(self, place, count):
        return place if self.onward else count - 1 - place

    def near_copy(self, j):
        return send(self.own, self.near.at[j], self.sems, j, self.at.plane_peer(j))

    def far_copy(self, j):
        return send(self.whole, self.far.at[j], self.sems, 3 + j, self.at.z_peer(j))

    def from_near(self, j):
        y, x = self.at.plane_place(j)
        return self.turn(2 * y + x, 4)

    def from_far(self, j):
        return self.turn(self.at.z_from(j), self.sh.depth)

    def sent(self):
        for j in range(3):
            self.near_copy(j).wait_send()
        for j in range(self.sh.depth - 1):
            self.far_copy(j).wait_send()


def fade(rate, steps, length):
    return jnp.exp(-(steps.astype(f32) * length) * rate)


class Carry(Exchange):
    def __init__(self, sh, at, onward, own, near, whole, far, sems, give, take):
        super().__init__(sh, at, onward, own, near, whole, far, sems)
        self.give, self.take = give, take

    def piece(self, y, x):
        return self.own.at[y, :, self.at.columns(x)]

    def near_copy(self, j):
        y, x = self.at.plane_place(j)
        return send(self.piece(y, x), self.near.at[j], self.sems, j, self.at.plane_peer(j))

    def give_copy(self, j):
        at = self.at
        return send(
            self.give.at[j], self.take.at[:, at.y, :, at.columns(at.x)], self.sems,
            2 + self.sh.depth + j, at.plane_peer(j),
        )

    def start(self, totals):
        for i, part in enumerate(totals):
            self.own[i] = part
        for j in range(3):
            self.near_copy(j).start()

    def after_plane(self, rates):
        sh, at = self.sh, self.at
        span = float(sh.span)
        self.rate = rates[:, at.columns(at.x)]
        for j in range(3):
            self.near_copy(j).wait_recv()
        parts = [(self.u, self.own[at.y, :, at.columns(at.x)])]
        parts += [(self.from_near(j), self.near[j]) for j in range(3)]
        self.parts = parts
        self.whole[...] = sum(fade(self.rate, 3 - u, span) * part for u, part in parts)
        for j in range(sh.depth - 1):
            self.far_copy(j).start()

    def after_z(self):
        sh, at = self.sh, self.at
        span, plane, half = float(sh.span), 4.0 * sh.span, sh.groups
        rate = self.rate
        for j in range(sh.depth - 1):
            self.far_copy(j).wait_recv()
        planes = [(self.v, self.whole[...])]
        planes += [(self.from_far(j), self.far[j]) for j in range(sh.depth - 1)]
        before, every = self.before(planes, self.v, plane), 0.0
        for v, part in planes:
            every += fade(rate, sh.depth - 1 - v, plane) * part

        def entering(u):
            state = self.before(self.parts, u, span) + fade(rate, u, span) * before
            across = fade(rate, self.v * 4 + u, span)
            if self.onward:
                earlier = across * every[:half]
                return state + jnp.concatenate([jnp.zeros_like(earlier), earlier], 0)
            later = across * every[half:]
            return state + jnp.concatenate([later, jnp.zeros_like(later)], 0)

        for j in range(3):
            self.give[j, 0] = entering(self.from_near(j))
            if self.onward:
                self.give[j, 1] = every
            self.give_copy(j).start()
        mine = at.columns(at.x)
        self.take[0, at.y, :, mine] = entering(self.u)
        if self.onward:
            self.take[1, at.y, :, mine] = every

    def before(self, parts, place, length):
        total = 0.0
        for u, part in parts:
            gap = fade(self.rate, jnp.maximum(place - 1 - u, 0), length)
            total += jnp.where(u < place, gap, 0.0) * part
        return total

    def finish(self):
        for j in range(3):
            self.give_copy(j).wait_recv()

    def sent(self):
        super().sent()
        for j in range(3):
            self.give_copy(j).wait_send()


class Tops(Exchange):
    def start(self, own):
        self.own[...] = own
        for j in range(3):
            self.near_copy(j).start()

    def after_plane(self, rate):
        span = float(self.sh.span)
        for j in range(3):
            self.near_copy(j).wait_recv()
        most = self.own[...] - (3 - self.u).astype(f32) * span * rate
        for j in range(3):
            gap = (3 - self.from_near(j)).astype(f32) * span
            most = jnp.maximum(most, self.near[j] - gap * rate)
        self.whole[...] = most
        for j in range(self.sh.depth - 1):
            self.far_copy(j).start()

    def after_z(self, rate):
        sh = self.sh
        for j in range(sh.depth - 1):
            self.far_copy(j).wait_recv()
        plane = 4.0 * sh.span
        most = self.whole[...] - (sh.depth - 1 - self.v).astype(f32) * plane * rate
        for j in range(sh.depth - 1):
            gap = (sh.depth - 1 - self.from_far(j)).astype(f32) * plane
            most = jnp.maximum(most, self.far[j] - gap * rate)
        half = sh.groups
        return jnp.maximum(most[:half] - float(sh.count * sh.span) * rate, most[half:])


class Scatter:
    def __init__(self, at, buf, m, bufs, sems, number, final, out, result):
        self.at, self.buf, self.m, self.sems, self.number = at, buf, m, sems, number
        self.core_in, self.b_in, self.a_in, self.z_in = [
            held.at[number % slots] for held, slots in zip(bufs, HELD)
        ]
        self.final, self.out, self.result = final, out, result
        self.mine, self.theirs = at.columns(at.r), at.columns(1 - at.r)
        self.age = 0

    def cut(self, z, y, x, columns):
        return self.buf.at[self.m, z, y, x, :, columns]

    def core_copy(self):
        every = slice(None)
        return send(
            self.cut(every, every, every, self.theirs), self.core_in, self.sems,
            (self.number, 0), self.at.sibling(),
        )

    def b_copy(self, core):
        at, every = self.at, slice(None)
        src = (
            self.cut(every, every, 1 - at.x, self.mine) if core == 0
            else self.cut(every, 1 - at.y, every, self.mine)
        )
        return send(src, self.b_in, self.sems, (self.number, 1), at.b_peer())

    def a_copy(self):
        at, every = self.at, slice(None)
        y = at.y + (1 - at.r) * (1 - 2 * at.y)
        x = at.x + at.r * (1 - 2 * at.x)
        return send(
            self.cut(every, y, x, self.mine), self.a_in, self.sems, (self.number, 2), at.a_peer()
        )

    def z_copy(self, j):
        at = self.at
        return send(
            self.cut(at.z_to(j), at.y, at.x, self.mine), self.z_in.at[j], self.sems,
            (self.number, 3 + j), at.z_peer(j),
        )

    def rows_of(self, r):
        own = self.at.sh.own
        return pl.ds(pl.multiple_of(r * own, own), own)

    def last_copy(self):
        at = self.at
        return send(
            self.final.at[self.result, self.rows_of(1 - at.r)],
            self.out.at[self.result, :, self.mine], self.sems,
            (self.number, 2 + at.sh.depth), at.sibling(),
        )

    def add(self, z, y, x, got):
        where = (self.m, z, y, x, slice(None), self.mine)
        self.buf[where] = self.buf[where] + got

    def advance(self):
        if self.age in SCATTER_AT:
            self.step(SCATTER_AT.index(self.age))
        self.age += 1

    def done(self):
        return self.age > SCATTER_AT[-1]

    def step(self, stage):
        at, sh = self.at, self.at.sh
        if stage == 0:
            self.core_copy().start()
        elif stage == 1:
            self.core_copy().wait_recv()

            def each(z, _):
                for y in range(2):
                    for x in range(2):
                        self.add(z, y, x, self.core_in[z, y, x])
                return 0

            lax.fori_loop(0, sh.depth, each, 0)
            for core in range(2):
                @pl.when(at.r == core)
                def _():
                    self.b_copy(core).start()
        elif stage == 2:
            self.b_copy(0).wait_recv()

            def each(z, _):
                for q in range(2):
                    y = (1 - at.r) * q + at.r * at.y
                    x = at.r * q + (1 - at.r) * at.x
                    self.add(z, y, x, self.b_in[z, q])
                return 0

            lax.fori_loop(0, sh.depth, each, 0)
            self.a_copy().start()
        elif stage == 3:
            self.a_copy().wait_recv()

            def each(z, _):
                self.add(z, at.y, at.x, self.a_in[z])
                return 0

            lax.fori_loop(0, sh.depth, each, 0)
            for j in range(sh.depth - 1):
                self.z_copy(j).start()
        elif stage == 4:
            for j in range(sh.depth - 1):
                self.z_copy(j).wait_recv()
            total = self.buf[self.m, at.z, at.y, at.x, :, self.mine].astype(f32)
            for j in range(sh.depth - 1):
                total += self.z_in[j].astype(f32)
            self.final[self.result] = total
            self.out[self.result, :, self.mine] = self.final[self.result, self.rows_of(at.r)]
            self.last_copy().start()
        else:
            self.last_copy().wait_recv()

    def sent(self):
        self.core_copy().wait_send()
        self.b_copy(0).wait_send()
        self.a_copy().wait_send()
        for j in range(self.at.sh.depth - 1):
            self.z_copy(j).wait_send()
        self.last_copy().wait_send()


def put_in_sequence_order(sh, p, block, lanes):
    for j in range(sh.width // 128):
        for st in range(sh.stretches):
            lanes[j, sequence_rows(sh, p, st), :] = block[
                st * sh.groups : (st + 1) * sh.groups, j * 128 : (j + 1) * 128
            ]


def layer_kernel(
    sh,
    tok_hbm, cot_hbm, pack_ref,
    out_hbm, ig_hbm, grads_out, small_out, final_out, den_park, gate_park, key_park, value_park,
    gatein_park,
    w, vall, vecs, rates, got_pack, narrow,
    lanes, f1, f2, f3, f4, f5, xp, b1, b2, b3, b4, k, v, cotp, b8, b9,
    halo, halo32, st_own, st_near, st_whole, st_far, st_give, st_take,
    bk_own, bk_near, bk_whole, bk_far, bk_give, bk_take,
    top_own, top_near, top_whole, top_far, acc, tile, plane,
    core_in, b_in, a_in, z_in, final,
    local_sem, pack_sems, ag_send, ag_recv, st_send, st_recv, bk_send, bk_recv, top_send, top_recv,
    halo_send, halo_recv, rs_send, rs_recv, tile_send, tile_recv, emit_sem,
):
    at = Place(sh)
    segs, span, rows, width = sh.segs, sh.span, sh.rows, sh.width
    mine, theirs = at.columns(at.r), at.columns(1 - at.r)
    gathers = [Gather(at, w, (m,), (ag_send, ag_recv), m) for m in range(sh.mats)]
    gather_v = Gather(at, vall, (), (ag_send, ag_recv), sh.mats)
    clock = [0]

    def period():
        for stage, after in enumerate(GATHER_AT):
            m = clock[0] - after
            if 0 <= m < sh.mats:
                gathers[m].step(stage)
        clock[0] += 1

    def gathered(m):
        while clock[0] <= m + GATHER_AT[-1]:
            period()
    halo_sems = (halo_send, halo_recv)

    def local(src, dst, i):
        return pltpu.make_async_copy(src, dst, local_sem.at[i])

    def matrix(m):
        return w[m].reshape(width, width)

    def set_matrix(m, value):
        w[m] = value.astype(bf16).reshape(sh.depth, 2, 2, sh.chip, width)

    def vec(i):
        return vecs[i : i + 1, :]

    load_tok = local(tok_hbm, b1, 0)
    load_tok.start()
    enter(at)
    pack_copy = send(
        pack_ref.at[:, :, theirs], got_pack, (pack_sems.at[0], pack_sems.at[1]), 0, at.sibling()
    )
    pack_copy.start()
    load_tok.wait()
    to_position_major(sh, b1, lanes, xp)
    halo_x = send(xp.at[pl.ds(rows - segs, segs)], halo.at[0], halo_sems, 0, at.ring(1))
    halo_x.start()
    load_cot = local(cot_hbm, b1, 1)
    load_cot.start()

    pack_copy.wait_recv()
    for m in range(sh.mats):
        own = pack_ref[m, : sh.own, mine].astype(f32)
        other = got_pack[m, : sh.own].astype(f32)
        first = jnp.where(at.r == 0, own, other)
        second = jnp.where(at.r == 0, other, own)
        w[m, at.z, at.y, at.x, :, mine] = jnp.concatenate([first, second], 0).astype(bf16)
    vall[at.z, at.y, at.x, :, mine] = (
        pack_ref[sh.mats, :16, mine].astype(f32) + got_pack[sh.mats, :16].astype(f32)
    ).astype(bf16)
    gather_v.step(0)
    period()
    period()
    load_cot.wait()
    to_position_major(sh, b1, lanes, cotp)
    gather_v.step(1)
    period()
    gather_v.step(2)
    period()
    gather_v.step(3)
    gather_v.step(4)
    spread = jnp.zeros((16, width), f32)
    for z in range(sh.depth):
        for i in range(4):
            spread += vall[z, i // 2, i % 2].astype(f32)
    vecs[...] = spread

    key_in, value_in, gate_in = b2, b3, b4
    halo_x.wait_recv()
    got, _ = normalise(halo[0].astype(f32))
    before_one = wrap_before(sh, at, got * vec(MIXER_G) + vec(MIXER_B))

    def blend_one(p, before):
        here = slab(p, segs)
        n1, _ = normalise(xp[here, :].astype(f32))
        one = n1 * vec(MIXER_G) + vec(MIXER_B)
        step = one - before
        key_in[here, :] = (before + step * vec(KEY_SHARE)).astype(bf16)
        value_in[here, :] = (before + step * vec(VALUE_SHARE)).astype(bf16)
        gate_in[here, :] = (before + step * vec(GATE_SHARE)).astype(bf16)
        return one

    before_one = lax.fori_loop(0, span // 2, blend_one, before_one, unroll=4)
    period()
    lax.fori_loop(span // 2, span, blend_one, before_one, unroll=4)
    parks = [local(key_in, key_park, 2), local(value_in, value_park, 3), local(gate_in, gatein_park, 4)]
    for copy in parks:
        copy.start()

    gathered(KEY)
    k[...] = dot(key_in[...], matrix(KEY)).astype(bf16)
    gathered(VALUE)
    v[...] = dot(value_in[...], matrix(VALUE)).astype(bf16)

    rates[...] = jnp.exp(vec(DECAY))
    rate = rates[...]
    keep = jnp.exp(-rate)
    zero = jnp.zeros((segs, width), f32)

    def add_up(p, state):
        a, b, top = state
        here = slab(p, segs)
        key = k[here, :].astype(f32)
        grown = jnp.exp(key)
        top = jnp.maximum(top - rate, key)
        return keep * a + grown * v[here, :].astype(f32), keep * b + grown, top

    sum_num, sum_den, top = lax.fori_loop(
        0, span, add_up, (zero, zero, jnp.full((segs, width), -jnp.inf, f32)), unroll=4
    )
    states = Carry(
        sh, at, True, st_own, st_near, st_whole, st_far, (st_send, st_recv), st_give, st_take
    )
    states.start((sum_num, sum_den))
    tops = Tops(
        sh, at, True, top_own, top_near, top_whole, top_far, (top_send, top_recv)
    )
    gathered(GATE)
    gate = f1
    gate[...] = sigmoid(dot(gate_in[...], matrix(GATE)))
    gate_out = local(gate, gate_park, 5)
    gate_out.start()
    states.after_plane(rates)
    tops.start(top)
    gathered(OUTPUT)
    states.after_z()
    period()
    states.finish()
    carry, total = st_take.at[0], st_take.at[1]

    num, den, res, s2 = f3, f2, f4, f5
    gated, rg, hin, sin = b8, b9, b2, b3
    boost_rate = jnp.exp(vec(FIRST))

    def recur(p, state):
        a, b = state
        here = slab(p, segs)
        grown = jnp.exp(k[here, :].astype(f32))
        value = v[here, :].astype(f32)
        boost = grown * boost_rate
        num[here, :] = a
        den[here, :] = b
        mix = ((a + boost * value) / (b + boost)).astype(bf16).astype(f32)
        gated[here, :] = (gate[here, :] * mix).astype(bf16)
        return keep * a + grown * value, keep * b + grown

    lax.fori_loop(0, span, recur, (carry[0], carry[1]), unroll=4)
    den_out = local(den, den_park, 6)
    den_out.start()
    res[...] = xp[...].astype(f32) + dot(gated[...], matrix(OUTPUT))

    last = pl.ds(rows - segs, segs)
    n2, _ = normalise(res[last, :])
    halo32[0] = n2 * vec(CHANNEL_G) + vec(CHANNEL_B)
    halo_two = send(halo32.at[0], halo32.at[1], halo_sems, 1, at.ring(1))
    halo_two.start()
    tops.after_plane(rate)
    period()
    for copy in parks:
        copy.wait()

    def blend_two(p, before):
        here = slab(p, segs)
        n2, _ = normalise(res[here, :])
        two = n2 * vec(CHANNEL_G) + vec(CHANNEL_B)
        step = two - before
        hin[here, :] = (before + step * vec(HIDDEN_SHARE)).astype(bf16)
        sin[here, :] = (before + step * vec(SCREEN_SHARE)).astype(bf16)
        return two

    n2, _ = normalise(res[pl.ds(0, segs), :])
    first_two = n2 * vec(CHANNEL_G) + vec(CHANNEL_B)
    lax.fori_loop(1, span, blend_two, first_two, unroll=7)
    halo_two.wait_recv()
    before_two = wrap_before(sh, at, halo32[1])
    blend_two(0, before_two)
    final_top = tops.after_z(rate)
    far = decay_over(rate, float(sh.count * span))
    scale = jnp.exp(-final_top)
    for i in range(2):
        final_out[i] = (far * total[i, : sh.groups] + total[i, sh.groups :]) * scale
    final_out[2] = final_top
    s2[...] = sigmoid(dot(sin[...], matrix(SCREEN)))
    rg[...] = (cotp[...].astype(f32) * s2[...]).astype(bf16)
    gate_out.wait()
    den_out.wait()

    bufs = (core_in, b_in, a_in, z_in)
    started, flying, landed = [], [], []

    def tick():
        period()
        for one in list(flying):
            one.advance()
            if one.done():
                flying.remove(one)
                landed.append(one)

    def scatter(m, result=None):
        number = len(started)
        one = Scatter(
            at, w, m, bufs, (rs_send, rs_recv), number, final, grads_out,
            m if result is None else result,
        )
        started.append(one)
        flying.append(one)
        tick()

    def all_sent(number):
        one = started[number]
        while not one.done():
            tick()
        landed.remove(one)
        one.sent()

    ret, hb, act, hg = f1, f2, b4, b1
    tiles = [(j, slice(j * 128, (j + 1) * 128)) for j in range(width // 128)]
    for c in range(sh.parts):
        into, back = FIRST_PART + 2 * c, FIRST_PART + 2 * c + 1
        gathered(into)
        up = jnp.maximum(dot(hin[...], matrix(into)), 0.0)
        for j, columns in tiles:
            lanes[j] = up[:, columns]
        act[...] = (up * up).astype(bf16)
        gathered(back)
        if c == 0:
            ret[...] = dot(act[...], matrix(back))
        else:
            ret[...] += dot(act[...], matrix(back))
        relu = jnp.concatenate([lanes[j] for j, _ in tiles], 1)
        hg[...] = (dot_nt(rg[...], matrix(back)) * (2.0 * relu)).astype(bf16)
        gathers[back].sent()
        set_matrix(back, dot_tn(act[...], rg[...]))
        scatter(back)
        if c == 0:
            hb[...] = dot_nt(hg[...], matrix(into))
        else:
            hb[...] += dot_nt(hg[...], matrix(into))
        gathers[into].sent()
        set_matrix(into, dot_tn(hin[...], hg[...]))
        scatter(into)

    sg, sb, og = b4, f5, b1
    first = pl.ds(0, segs)
    cot0 = cotp[first, :].astype(f32)
    sg0 = (cot0 * ret[first, :] * s2[first, :] * (1.0 - s2[first, :])).astype(bf16)
    sb0 = dot_nt(sg0, matrix(SCREEN))
    halo32[2] = hb[first, :] * (1.0 - vec(HIDDEN_SHARE)) + sb0 * (1.0 - vec(SCREEN_SHARE))
    back_two = send(halo32.at[2], halo32.at[3], halo_sems, 2, at.ring(-1))
    back_two.start()
    load_gatein = local(gatein_park, b2, 7)
    load_gatein.start()
    acc[...] = jnp.zeros_like(acc)

    def finish(p, _):
        here = slab(p, segs)
        s = s2[here, :]
        held = ret[here, :]
        put_in_sequence_order(sh, p, res[here, :] + s * held, lanes)
        sg[here, :] = (cotp[here, :].astype(f32) * held * s * (1.0 - s)).astype(bf16)
        return 0

    lax.fori_loop(0, span, finish, 0, unroll=4)
    sb[...] = dot_nt(sg[...], matrix(SCREEN))
    tick()
    out_copies = []
    for j, columns in tiles:
        if j >= 2:
            out_copies[j - 2].wait()
        narrow[j % 2] = lanes[j].astype(bf16)
        copy = pltpu.make_async_copy(narrow.at[j % 2], out_hbm.at[:, columns], emit_sem.at[0, j])
        copy.start()
        out_copies.append(copy)

    rgrad = f1

    def back_second(p, before, ahead):
        here = slab(p, segs)
        n2, inverse = normalise(res[here, :])
        two = n2 * vec(CHANNEL_G) + vec(CHANNEL_B)
        step = two - before
        hb_here, sb_here = hb[here, :], sb[here, :]
        acc[0] += hb_here * step
        acc[1] += sb_here * step
        grad = hb_here * vec(HIDDEN_SHARE) + sb_here * vec(SCREEN_SHARE) + ahead
        acc[2] += grad * n2
        acc[3] += grad
        down = cotp[here, :].astype(f32) + norm_back(grad, n2, inverse, vec(CHANNEL_G))
        rgrad[here, :] = down
        og[here, :] = down.astype(bf16)
        return two

    def back_second_step(p, before):
        there = slab(p + 1, segs)
        ahead = hb[there, :] * (1.0 - vec(HIDDEN_SHARE)) + sb[there, :] * (1.0 - vec(SCREEN_SHARE))
        return back_second(p, before, ahead)

    before = lax.fori_loop(0, span - 1, back_second_step, before_two, unroll=7)
    back_two.wait_recv()
    back_second(span - 1, before, wrap_after(sh, at, halo32[3]))
    for copy in out_copies[-2:]:
        copy.wait()
    load_gate = local(gate_park, f2, 8)
    load_gate.start()
    load_den = local(den_park, f5, 9)
    load_den.start()
    tick()
    gated_grad = f4
    gated_grad[...] = dot_nt(og[...], matrix(OUTPUT))
    load_gate.wait()
    load_den.wait()

    gate, den, gate_grad, mg = f2, f5, b9, cotp

    def totals_back(i, state):
        a, b = state
        here = slab(span - 1 - i, segs)
        grown = jnp.exp(k[here, :].astype(f32))
        value = v[here, :].astype(f32)
        boost = grown * boost_rate
        over = 1.0 / (den[here, :] + boost)
        raw = (num[here, :] + boost * value) * over
        mix = raw.astype(bf16).astype(f32)
        grad, s = gated_grad[here, :], gate[here, :]
        through = (grad * s).astype(bf16)
        mg[here, :] = through
        gate_grad[here, :] = (grad * mix * s * (1.0 - s)).astype(bf16)
        num_grad = through.astype(f32) * over
        return keep * a + num_grad, keep * b - num_grad * raw

    sum_num, sum_den = lax.fori_loop(0, span, totals_back, (zero, zero), unroll=4)
    adjoints = Carry(
        sh, at, False, bk_own, bk_near, bk_whole, bk_far, (bk_send, bk_recv), bk_give, bk_take
    )
    adjoints.start((sum_num, sum_den))
    gathers[OUTPUT].sent()
    set_matrix(OUTPUT, dot_tn(gated[...], og[...]))
    scatter(OUTPUT)
    adjoints.after_plane(rates)
    gathers[SCREEN].sent()
    set_matrix(SCREEN, dot_tn(sin[...], sg[...]))
    scatter(SCREEN)
    load_keyin = local(key_park, b3, 10)
    load_keyin.start()
    load_valin = local(value_park, b4, 11)
    load_valin.start()
    adjoints.after_z()
    gate_back = f4
    gate_back[...] = dot_nt(gate_grad[...], matrix(GATE))
    load_gatein.wait()
    gathers[GATE].sent()
    set_matrix(GATE, dot_tn(b2[...], gate_grad[...]))
    scatter(GATE)
    adjoints.finish()
    carry = bk_take.at[0]

    kg, vg = b8, b1

    def recur_back(i, state):
        a, b = state
        here = slab(span - 1 - i, segs)
        grown = jnp.exp(k[here, :].astype(f32))
        value = v[here, :].astype(f32)
        boost = grown * boost_rate
        n, d = num[here, :], den[here, :]
        over = 1.0 / (d + boost)
        num_grad = mg[here, :].astype(f32) * over
        den_grad = -num_grad * ((n + boost * value) * over)
        inner = boost * (value * num_grad + den_grad)
        kg[here, :] = (grown * (value * a + b) + inner).astype(bf16)
        vg[here, :] = (grown * a + boost * num_grad).astype(bf16)
        acc[4] += inner
        acc[5] += n * a + d * b
        return keep * a + num_grad, keep * b + den_grad

    lax.fori_loop(0, span, recur_back, (carry[0], carry[1]), unroll=4)
    load_keyin.wait()
    load_valin.wait()
    spare = FIRST_PART
    all_sent(1)
    set_matrix(spare, dot_tn(b3[...], kg[...]))
    scatter(spare, KEY)
    all_sent(0)
    set_matrix(spare + 1, dot_tn(b4[...], vg[...]))
    scatter(spare + 1, VALUE)

    key_back, value_back = f2, f3
    key_back[...] = dot_nt(kg[...], matrix(KEY))
    value_back[...] = dot_nt(vg[...], matrix(VALUE))

    def ahead_of(where):
        return (
            key_back[where, :] * (1.0 - vec(KEY_SHARE))
            + value_back[where, :] * (1.0 - vec(VALUE_SHARE))
            + gate_back[where, :] * (1.0 - vec(GATE_SHARE))
        )

    halo32[4] = ahead_of(first)
    back_one = send(halo32.at[4], halo32.at[5], halo_sems, 3, at.ring(-1))
    back_one.start()
    tick()
    got, _ = normalise(halo[0].astype(f32))
    before_one = wrap_before(sh, at, got * vec(MIXER_G) + vec(MIXER_B))

    def back_first(p, before, ahead):
        here = slab(p, segs)
        n1, inverse = normalise(xp[here, :].astype(f32))
        one = n1 * vec(MIXER_G) + vec(MIXER_B)
        step = one - before
        kb, vb, gb = key_back[here, :], value_back[here, :], gate_back[here, :]
        acc[6] += kb * step
        acc[7] += vb * step
        acc[8] += gb * step
        grad = kb * vec(KEY_SHARE) + vb * vec(VALUE_SHARE) + gb * vec(GATE_SHARE) + ahead
        acc[9] += grad * n1
        acc[10] += grad
        down = rgrad[here, :] + norm_back(grad, n1, inverse, vec(MIXER_G))
        put_in_sequence_order(sh, p, down, lanes)
        return one

    def back_first_step(p, before):
        return back_first(p, before, ahead_of(slab(p + 1, segs)))

    middle = (span - 1) // 2 // 7 * 7
    before = lax.fori_loop(0, middle, back_first_step, before_one, unroll=7)
    tick()
    before = lax.fori_loop(middle, span - 1, back_first_step, before, unroll=7)
    back_one.wait_recv()
    back_first(span - 1, before, wrap_after(sh, at, halo32[5]))
    ig_copies = [
        pltpu.make_async_copy(lanes.at[j], ig_hbm.at[:, columns], emit_sem.at[1, j])
        for j, columns in tiles
    ]
    for copy in ig_copies:
        copy.start()

    def line(i):
        return jnp.sum(acc[i], 0, keepdims=True)

    order = (9, 10, 6, 7, 8, 5, 4, 2, 3, 0, 1)
    tile[0] = jnp.zeros((16, width), f32)
    for i, which in enumerate(order):
        value = line(which)
        if i == DECAY:
            value = -rate * keep * value
        tile[0, i : i + 1, :] = value
    tile_sems = (tile_send, tile_recv)
    sums = [
        send(tile.at[0], tile.at[1], tile_sems, 0, at.sibling()),
        send(tile.at[2], tile.at[3], tile_sems, 1, at.x_peer()),
        send(tile.at[4], tile.at[5], tile_sems, 2, at.y_peer()),
    ]
    sums[0].start()
    tick()
    for i in range(2):
        sums[i].wait_recv()
        tile[2 * i + 2] = tile[2 * i] + tile[2 * i + 1]
        sums[i + 1].start()
        tick()
    sums[2].wait_recv()
    tile[6] = tile[4] + tile[5]
    far_sums = [
        send(tile.at[6], plane.at[j], tile_sems, 3 + j, at.z_peer(j)) for j in range(sh.depth - 1)
    ]
    for copy in far_sums:
        copy.start()
    while flying:
        tick()
    everything = tile[6]
    for j, copy in enumerate(far_sums):
        copy.wait_recv()
        everything += plane[j]
    small_out[...] = everything
    for copy in ig_copies:
        copy.wait()

    pack_copy.wait_send()
    halo_x.wait_send()
    for copy in (halo_two, back_two, back_one):
        copy.wait_send()
    gather_v.sent()
    gathers[KEY].sent()
    gathers[VALUE].sent()
    for one in landed:
        one.sent()
    for exchange in (states, tops, adjoints):
        exchange.sent()
    for copy in sums + far_sums:
        copy.wait_send()


def layer(sh, tokens, cotangent, pack):
    R, D, S, Z = sh.rows, sh.width, sh.segs, sh.depth
    shape = jax.ShapeDtypeStruct
    narrow, wide = ((R, D), bf16), ((R, D), f32)
    w_shape = (sh.mats, Z, 2, 2, sh.chip, D)
    V = pltpu.VMEM
    dma = pltpu.SemaphoreType.DMA
    anywhere, in_vmem = pl.BlockSpec(memory_space=pl.ANY), pl.BlockSpec(memory_space=pltpu.VMEM)
    outs = [
        (narrow, anywhere), (wide, anywhere), (((sh.mats, sh.own, D), f32), in_vmem),
        (((16, D), f32), in_vmem), (((3, sh.groups, D), f32), in_vmem),
        (wide, anywhere), (wide, anywhere), (narrow, anywhere), (narrow, anywhere),
        (narrow, anywhere),
    ]
    scratch = (
        [
            V(w_shape, bf16), V((Z, 2, 2, 16, D), bf16), V((16, D), f32), V((1, D), f32),
            V((sh.mats + 1, 32, sh.half), bf16), V((2, R, 128), bf16), V((D // 128, R, 128), f32),
        ]
        + [V(*wide)] * 5
        + [V(*narrow)] * 10
        + [
            V((1, S, D), bf16), V((6, S, D), f32),
            V((2, S, D), f32), V((3, S, sh.half), f32), V((S, sh.half), f32),
            V((Z - 1, S, sh.half), f32), V((3, 2, S, sh.half), f32), V((2, 2, S, D), f32),
            V((2, S, D), f32), V((3, S, sh.half), f32), V((S, sh.half), f32),
            V((Z - 1, S, sh.half), f32), V((3, 1, S, sh.half), f32), V((1, 2, S, D), f32),
            V((S, D), f32), V((3, S, D), f32), V((S, D), f32), V((Z - 1, S, D), f32),
            V((VECTORS, S, D), f32),
            V((7, 16, D), f32), V((Z - 1, 16, D), f32),
            V((HELD[0], Z, 2, 2, sh.chip, sh.half), bf16), V((HELD[1], Z, 2, sh.chip, sh.half), bf16),
            V((HELD[2], Z, sh.chip, sh.half), bf16), V((HELD[3], Z - 1, sh.chip, sh.half), bf16),
            V((sh.mats, sh.chip, sh.half), f32),
            dma((12,)), dma((2, 1)),
        ]
        + [dma((sh.mats + 1, Z + 2))] * 2
        + [dma((Z + 5,))] * 6
        + [dma((4,))] * 2
        + [dma((sh.mats, Z + 3))] * 2
        + [dma((Z + 2,))] * 2
        + [dma((2, D // 128))]
    )
    return pl.pallas_call(
        functools.partial(layer_kernel, sh),
        out_shape=[shape(s, t) for (s, t), _ in outs],
        in_specs=[anywhere, anywhere, in_vmem],
        out_specs=[spec for _, spec in outs],
        scratch_shapes=scratch,
        compiler_params=pltpu.CompilerParams(
            collective_id=0, has_side_effects=True, vmem_limit_bytes=63 * 2**20
        ),
    )(tokens.reshape(R, D), cotangent.reshape(R, D), pack)


def mm(left, right):
    return jnp.dot(left, right, preferred_element_type=f32)


def mm_nt(left, right):
    return lax.dot_general(left, right, (((1,), (1,)), ((), ())), preferred_element_type=f32)


def mm_tn(left, right):
    return lax.dot_general(left, right, (((0,), (0,)), ((), ())), preferred_element_type=f32)


def ring(value, steps):
    count = lax.axis_size("seq")
    return lax.ppermute(value, "seq", [(i, (i + steps) % count) for i in range(count)])


def entering(last, spot):
    got = ring(last, 1)
    pairs = got.reshape(-1, 2, got.shape[-1])
    wrapped = jnp.concatenate([jnp.zeros_like(pairs[:, :1]), pairs[:, :1]], 1)
    return jnp.where(spot == 0, wrapped, pairs).reshape(got.shape)


def leaving(first, spot):
    count = lax.axis_size("seq")
    got = ring(first, -1)
    pairs = got.reshape(-1, 2, got.shape[-1])
    wrapped = jnp.concatenate([pairs[:, 1:], jnp.zeros_like(pairs[:, :1])], 1)
    return jnp.where(spot == count - 1, wrapped, pairs).reshape(got.shape)


def plain_scan(k_ref, v_ref, carry_ref, decay_ref, first_ref, num_ref, den_ref, mix_ref):
    keep = jnp.exp(-jnp.exp(decay_ref[...]))
    boost_rate = jnp.exp(first_ref[...])

    def step(t, state):
        num, den = state
        k = jnp.exp(k_ref[t].astype(f32))
        v = v_ref[t].astype(f32)
        boost = k * boost_rate
        num_ref[t] = num
        den_ref[t] = den
        mix_ref[t] = (num + boost * v) / (den + boost)
        return keep * num + k * v, keep * den + k

    lax.fori_loop(0, k_ref.shape[0], step, (carry_ref[0], carry_ref[1]))


def plain_scan_back(
    k_ref, v_ref, num_ref, den_ref, mix_ref, grad_ref, carry_ref, decay_ref, first_ref,
    kg_ref, vg_ref, first_grad_ref, decay_grad_ref,
):
    keep = jnp.exp(-jnp.exp(decay_ref[...]))
    boost_rate = jnp.exp(first_ref[...])
    length = k_ref.shape[0]

    def step(i, state):
        adj_num, adj_den, first_sum, decay_sum = state
        t = length - 1 - i
        k = jnp.exp(k_ref[t].astype(f32))
        v = v_ref[t].astype(f32)
        boost = k * boost_rate
        num_grad = grad_ref[t].astype(f32) / (den_ref[t] + boost)
        den_grad = -num_grad * mix_ref[t]
        inner = boost * (v * num_grad + den_grad)
        kg_ref[t] = (k * (v * adj_num + adj_den) + inner).astype(bf16)
        vg_ref[t] = (k * adj_num + boost * num_grad).astype(bf16)
        first_sum = first_sum + inner
        decay_sum = decay_sum + num_ref[t] * adj_num + den_ref[t] * adj_den
        return keep * adj_num + num_grad, keep * adj_den + den_grad, first_sum, decay_sum

    zero = jnp.zeros_like(carry_ref[0])
    out = lax.fori_loop(0, length, step, (carry_ref[0], carry_ref[1], zero, zero))
    first_grad_ref[...] = out[2]
    decay_grad_ref[...] = out[3]


def call(kernel, shapes, *operands):
    space = pl.BlockSpec(memory_space=pltpu.VMEM)
    return pl.pallas_call(
        kernel,
        out_shape=[jax.ShapeDtypeStruct(s, t) for s, t in shapes],
        in_specs=[space] * len(operands),
        out_specs=[space] * len(shapes),
        compiler_params=pltpu.CompilerParams(vmem_limit_bytes=48 * 2**20),
    )(*operands)


def plain_body(
    tokens, mixer_gain, mixer_bias, key_blend, value_blend, gate_blend, time_decay, time_first,
    key_weight, value_weight, gate_weight, output_weight, channel_gain, channel_bias,
    hidden_blend, screen_blend, hidden_weight, screen_weight, return_weight, cotangent,
):
    groups, stretches, span, width = tokens.shape
    count = lax.axis_size("seq")
    owners = count * lax.axis_size("rep")
    spot = lax.axis_index("seq")
    segs = groups * stretches
    rows = span * segs
    own = width // owners
    inner = hidden_weight.shape[1]
    parts = inner // width

    vectors = (
        mixer_gain, mixer_bias, key_blend, value_blend, gate_blend, time_decay, time_first,
        channel_gain, channel_bias, hidden_blend, screen_blend,
    )
    squares = (key_weight, value_weight, gate_weight, output_weight, screen_weight)
    packed = jnp.concatenate(
        squares + (hidden_weight.reshape(own * parts, width), return_weight), 0
    )
    packed = lax.all_gather(packed, both, axis=0)
    spread_vectors = lax.all_gather(jnp.stack(vectors), both, axis=0)
    spread_vectors = jnp.swapaxes(spread_vectors, 0, 1).reshape(len(vectors), width).astype(f32)
    (
        mixer_g, mixer_b, key_share, value_share, gate_share, decay_log, first_log,
        channel_g, channel_b, hidden_share, screen_share,
    ) = [spread_vectors[i][None] for i in range(len(vectors))]

    def piece(start, size, shape):
        return packed[:, start : start + size].reshape(shape)

    w_key, w_value, w_gate, w_output, w_screen = [
        piece(own * i, own, (width, width)) for i in range(5)
    ]
    w_hidden = piece(own * 5, own * parts, (width, inner))
    w_return = piece(own * (5 + parts), own * parts, (inner, width))

    def position_major(a):
        return jnp.transpose(a, (2, 0, 1, 3)).reshape(rows, width)

    def shifted(a, first):
        return jnp.concatenate([first, a[:-segs]], 0)

    x = position_major(tokens).astype(f32)
    n1, inv1 = normalise(x)
    one = n1 * mixer_g + mixer_b
    before = shifted(one, entering(one[-segs:], spot))
    spread_one = one - before
    key_in = (before + spread_one * key_share).astype(bf16)
    value_in = (before + spread_one * value_share).astype(bf16)
    gate_in = (before + spread_one * gate_share).astype(bf16)
    k = mm(key_in, w_key).astype(bf16)
    v = mm(value_in, w_value).astype(bf16)
    gate = jax.nn.sigmoid(mm(gate_in, w_gate))

    rate = jnp.exp(decay_log)
    cube = (span, segs, width)
    offsets = jnp.arange(span, dtype=f32)[:, None, None]
    kw = k.reshape(cube).astype(f32)
    vw = v.reshape(cube).astype(f32)
    shifted_key = kw - (span - 1.0 - offsets) * rate
    ends = jnp.exp(shifted_key)
    totals = jnp.stack([jnp.sum(ends * vw, 0), jnp.sum(ends, 0)])
    tops = jnp.max(shifted_key, 0)
    everyone = lax.all_gather(jnp.concatenate([totals, tops[None]]), "seq", axis=0)
    everyone = everyone.reshape(count, 3, groups, stretches, width)
    everyone = jnp.transpose(everyone, (3, 0, 1, 2, 4)).reshape(
        stretches * count, 3, groups, width
    )
    order = jnp.arange(stretches * count, dtype=f32)

    def weights_for(here):
        gap = here - 1.0 - order[:, None]
        return jnp.where(gap >= 0, jnp.exp(-jnp.maximum(gap, 0.0) * (span * rate)), 0.0)

    def carried(here):
        return jnp.sum(weights_for(here)[:, None, None, :] * everyone[:, :2], 0)

    carry = jnp.stack([carried(j * count + spot.astype(f32)) for j in range(stretches)], 2)
    carry = carry.reshape(2, segs, width)
    final = carried(float(stretches * count))
    far = (stretches * count - 1.0 - order)[:, None] * (span * rate)
    top = jnp.max(everyone[:, 2] - far[:, None, :], 0)
    slab = width // count

    def own_slab(a):
        return lax.dynamic_slice_in_dim(a, spot * slab, slab, 1)

    final_top = own_slab(top)
    scaling = jnp.exp(-final_top)
    final_num = own_slab(final[0]) * scaling
    final_den = own_slab(final[1]) * scaling

    num, den, mix_raw = call(
        plain_scan, [(cube, f32)] * 3, k.reshape(cube), v.reshape(cube), carry,
        decay_log, first_log,
    )
    mix = mix_raw.reshape(rows, width).astype(bf16).astype(f32)
    gated = (gate * mix).astype(bf16)
    residual = x + mm(gated, w_output)
    n2, inv2 = normalise(residual)
    two = n2 * channel_g + channel_b
    before = shifted(two, entering(two[-segs:], spot))
    spread_two = two - before
    hidden_in = (before + spread_two * hidden_share).astype(bf16)
    screen_in = (before + spread_two * screen_share).astype(bf16)
    screen = jax.nn.sigmoid(mm(screen_in, w_screen))
    cot = position_major(cotangent).astype(f32)
    returned_grad = (cot * screen).astype(bf16)
    relu = jnp.maximum(mm(hidden_in, w_hidden), 0.0)
    act = jnp.square(relu).astype(bf16)
    returned = mm(act, w_return)
    output = (residual + screen * returned).astype(bf16)

    screen_grad = (cot * returned * screen * (1.0 - screen)).astype(bf16)
    hidden_grad = (mm_nt(returned_grad, w_return) * (2.0 * relu)).astype(bf16)
    dw_return = mm_tn(act, returned_grad)
    dw_hidden = mm_tn(hidden_in, hidden_grad)
    dw_screen = mm_tn(screen_in, screen_grad)
    hidden_back = mm_nt(hidden_grad, w_hidden)
    screen_back = mm_nt(screen_grad, w_screen)
    d_hidden_blend = jnp.sum(hidden_back * spread_two, 0)
    d_screen_blend = jnp.sum(screen_back * spread_two, 0)
    ahead = hidden_back * (1.0 - hidden_share) + screen_back * (1.0 - screen_share)
    two_grad = (
        hidden_back * hidden_share
        + screen_back * screen_share
        + jnp.concatenate([ahead[segs:], leaving(ahead[:segs], spot)], 0)
    )
    d_channel_gain = jnp.sum(two_grad * n2, 0)
    d_channel_bias = jnp.sum(two_grad, 0)
    residual_grad = cot + norm_back(two_grad, n2, inv2, channel_g)
    output_grad = residual_grad.astype(bf16)
    dw_output = mm_tn(gated, output_grad)
    gated_grad = mm_nt(output_grad, w_output)
    mix_grad = (gated_grad * gate).astype(bf16)
    gate_grad = (gated_grad * mix * gate * (1.0 - gate)).astype(bf16)

    boost = jnp.exp(first_log + kw)
    num_grad = mix_grad.reshape(cube).astype(f32) / (den + boost)
    den_grad = -num_grad * mix_raw
    fade = jnp.exp(-offsets * rate)
    totals = jnp.stack([jnp.sum(fade * num_grad, 0), jnp.sum(fade * den_grad, 0)])
    everyone = lax.all_gather(totals, "seq", axis=0)
    everyone = everyone.reshape(count, 2, groups, stretches, width)
    everyone = jnp.transpose(everyone, (3, 0, 1, 2, 4)).reshape(
        stretches * count, 2, groups, width
    )

    def carried_back(here):
        gap = order[:, None] - here - 1.0
        scale = jnp.where(gap >= 0, jnp.exp(-jnp.maximum(gap, 0.0) * (span * rate)), 0.0)
        return jnp.sum(scale[:, None, None, :] * everyone, 0)

    carry = jnp.stack([carried_back(j * count + spot.astype(f32)) for j in range(stretches)], 2)
    carry = carry.reshape(2, segs, width)
    key_grad, value_grad, first_sum, decay_sum = call(
        plain_scan_back, [(cube, bf16)] * 2 + [((segs, width), f32)] * 2,
        k.reshape(cube), v.reshape(cube), num, den, mix_raw, mix_grad.reshape(cube), carry,
        decay_log, first_log,
    )
    key_grad = key_grad.reshape(rows, width)
    value_grad = value_grad.reshape(rows, width)
    d_first = jnp.sum(first_sum, 0)
    d_decay = -rate[0] * jnp.exp(-rate[0]) * jnp.sum(decay_sum, 0)
    dw_key = mm_tn(key_in, key_grad)
    dw_value = mm_tn(value_in, value_grad)
    dw_gate = mm_tn(gate_in, gate_grad)
    key_back = mm_nt(key_grad, w_key)
    value_back = mm_nt(value_grad, w_value)
    gate_back = mm_nt(gate_grad, w_gate)
    d_key_blend = jnp.sum(key_back * spread_one, 0)
    d_value_blend = jnp.sum(value_back * spread_one, 0)
    d_gate_blend = jnp.sum(gate_back * spread_one, 0)
    ahead = (
        key_back * (1.0 - key_share)
        + value_back * (1.0 - value_share)
        + gate_back * (1.0 - gate_share)
    )
    one_grad = (
        key_back * key_share
        + value_back * value_share
        + gate_back * gate_share
        + jnp.concatenate([ahead[segs:], leaving(ahead[:segs], spot)], 0)
    )
    d_mixer_gain = jnp.sum(one_grad * n1, 0)
    d_mixer_bias = jnp.sum(one_grad, 0)
    input_grad = residual_grad + norm_back(one_grad, n1, inv1, mixer_g)

    packed = jnp.concatenate(
        [d.reshape(owners, own, width).astype(bf16) for d in (dw_key, dw_value, dw_gate, dw_output, dw_screen)]
        + [
            dw_hidden.reshape(owners, own * parts, width).astype(bf16),
            dw_return.reshape(owners, own * parts, width).astype(bf16),
        ],
        1,
    )
    summed = lax.psum_scatter(packed, both, scatter_dimension=0).astype(f32)
    small = jnp.stack(
        [
            d_mixer_gain, d_mixer_bias, d_key_blend, d_value_blend, d_gate_blend, d_decay, d_first,
            d_channel_gain, d_channel_bias, d_hidden_blend, d_screen_blend,
        ]
    )
    small = lax.psum(small, both)
    place = (spot * lax.axis_size("rep") + lax.axis_index("rep")) * own
    small = lax.dynamic_slice_in_dim(small, place, own, 1)

    def batch_major(a):
        return jnp.transpose(a.reshape(span, groups, stretches, width), (1, 2, 0, 3))

    return (
        batch_major(output),
        batch_major(input_grad),
        final_num,
        final_den,
        final_top,
        *[small[i] for i in range(7)],
        *[summed[own * i : own * (i + 1)] for i in range(4)],
        *[small[i] for i in range(7, 11)],
        summed[own * 5 : own * (5 + parts)].reshape(own, inner),
        summed[own * 4 : own * 5],
        summed[own * (5 + parts) :],
    )


def make_pack(sh, squares, hidden_weight, return_weight, vectors):
    own, width, parts = sh.own, sh.width, sh.parts
    owners = 2 * sh.count
    hidden = hidden_weight.reshape(own, owners, parts, own)
    hidden = jnp.transpose(hidden, (2, 0, 1, 3)).reshape(parts, own, width)
    back = return_weight.reshape(parts, own, width)
    both_parts = jnp.stack([hidden, back], 1).reshape(2 * parts, own, width)
    mats = jnp.concatenate([jnp.stack(squares), both_parts], 0)
    mats = jnp.pad(mats, ((0, 0), (0, 32 - own), (0, 0)))
    place = (lax.axis_index("seq") * 2 + lax.axis_index("rep")) * own
    tile = lax.dynamic_update_slice(
        jnp.zeros((32, width), bf16), jnp.stack(vectors), (0, place)
    )
    return jnp.concatenate([mats, tile[None]], 0)


def fused_body(sh, *args):
    (
        tokens, mixer_gain, mixer_bias, key_blend, value_blend, gate_blend, time_decay, time_first,
        key_weight, value_weight, gate_weight, output_weight, channel_gain, channel_bias,
        hidden_blend, screen_blend, hidden_weight, screen_weight, return_weight, cotangent,
    ) = args
    vectors = (
        mixer_gain, mixer_bias, key_blend, value_blend, gate_blend, time_decay, time_first,
        channel_gain, channel_bias, hidden_blend, screen_blend,
    )
    squares = (key_weight, value_weight, gate_weight, output_weight, screen_weight)
    pack = make_pack(sh, squares, hidden_weight, return_weight, vectors)
    output, input_grad, grads, small, finals = layer(sh, tokens, cotangent, pack)[:5]
    place = (lax.axis_index("seq") * 2 + lax.axis_index("rep")) * sh.own
    small = lax.dynamic_slice_in_dim(small, place, sh.own, 1)
    return (
        output.reshape(tokens.shape),
        input_grad.reshape(tokens.shape),
        *own_finals(sh, finals),
        *own_grads(sh, small, grads),
    )


def own_finals(sh, finals):
    share = sh.width // sh.count
    cut = lax.dynamic_slice_in_dim(finals, lax.axis_index("seq") * share, share, 2)
    return [cut[i] for i in range(3)]


def own_grads(sh, small, summed):
    own, owners, parts, inner = sh.own, 2 * sh.count, sh.parts, sh.inner
    hidden = summed[FIRST_PART::2].reshape(parts, own, owners, own)
    hidden = jnp.transpose(hidden, (1, 2, 0, 3)).reshape(own, inner)
    back = summed[FIRST_PART + 1 :: 2].reshape(parts * own, sh.width)
    return (
        *[small[i] for i in range(7)],
        *[summed[i] for i in (KEY, VALUE, GATE, OUTPUT)],
        *[small[i] for i in range(7, 11)],
        hidden,
        summed[SCREEN],
        back,
    )


def body(*args):
    tokens, hidden_weight = args[0], args[16]
    groups, stretches, span, width = tokens.shape
    sh = Shape(lax.axis_size("seq"), span, groups, stretches, width, hidden_weight.shape[1])
    if lax.axis_size("rep") == 2 and sh.fits():
        return fused_body(sh, *args)
    return plain_body(*args)


def solution(mesh):
    rows = P("rep", None, "seq", None)
    owned = P(both)
    owned_rows = P(both, None)
    in_specs = (rows,) + (owned,) * 7 + (owned_rows,) * 4 + (owned,) * 4 + (owned_rows,) * 3 + (rows,)
    out_specs = (
        (rows,) * 2 + (P("rep", "seq"),) * 3 + (owned,) * 7 + (owned_rows,) * 4
        + (owned,) * 4 + (owned_rows,) * 3
    )
    return jax.shard_map(body, mesh=mesh, in_specs=in_specs, out_specs=out_specs, check_vma=False)
```

```python
import functools

import jax
import jax.numpy as jnp
from jax import lax
from jax.experimental import pallas as pl
from jax.experimental.pallas import tpu as pltpu
from jax.sharding import PartitionSpec as P

f32 = jnp.float32
bf16 = jnp.bfloat16
norm_eps = 1e-05
both = ("seq", "rep")
MESH = pl.DeviceIdType.MESH

KEY, VALUE, GATE, OUTPUT, SCREEN, FIRST_PART = 0, 1, 2, 3, 4, 5
GATHER_AT = (0, 2, 3, 5, 6)
SCATTER_AT = (0, 1, 3, 5, 7, 8)
HELD = (2, 4, 4, 4)
VECTORS = 11
(
    MIXER_G, MIXER_B, KEY_SHARE, VALUE_SHARE, GATE_SHARE, DECAY, FIRST,
    CHANNEL_G, CHANNEL_B, HIDDEN_SHARE, SCREEN_SHARE,
) = range(VECTORS)


def dot(left, right):
    return jnp.dot(left, right, preferred_element_type=f32)


def dot_nt(left, right):
    return lax.dot_general(left, right, (((1,), (1,)), ((), ())), preferred_element_type=f32)


def dot_tn(left, right):
    return lax.dot_general(left, right, (((0,), (0,)), ((), ())), preferred_element_type=f32)


def sigmoid(a):
    return 1.0 / (1.0 + jnp.exp(-a))


def normalise(values):
    centred = values - jnp.mean(values, -1, keepdims=True)
    inverse = lax.rsqrt(jnp.mean(centred * centred, -1, keepdims=True) + norm_eps)
    return centred * inverse, inverse


def norm_back(upstream, scaled, inverse, gain):
    inner = upstream * gain
    centred = inner - jnp.mean(inner, -1, keepdims=True)
    return inverse * (centred - scaled * jnp.mean(inner * scaled, -1, keepdims=True))


class Shape:
    def __init__(self, count, span, groups, stretches, width, inner):
        self.count, self.span, self.groups, self.stretches = count, span, groups, stretches
        self.width, self.inner = width, inner
        self.segs = groups * stretches
        self.rows = span * self.segs
        self.depth = count // 4
        self.chip = width // count
        self.own = self.chip // 2
        self.parts = inner // width
        self.mats = FIRST_PART + 2 * self.parts
        self.half = width // 2

    def fits(self):
        return (
            self.count % 4 == 0 and self.chip % 16 == 0 and self.own % 8 == 0 and self.own <= 32
            and self.half % 128 == 0 and self.groups == 8 and self.stretches == 2
            and self.parts == 4 and self.inner == 4 * self.width and self.rows == 1024
            and self.width // self.own == 32 and self.width // self.count <= 128
        )


class Place:
    def __init__(self, sh):
        self.sh = sh
        self.s = lax.axis_index("seq")
        self.r = lax.axis_index("rep")
        self.z = self.s // 4
        self.y = lax.rem(self.s // 2, 2)
        self.x = lax.rem(self.s, 2)

    def device(self, z, y, x, r):
        return ((z * 2 + y) * 2 + x, r)

    def sibling(self):
        return (self.s, 1 - self.r)

    def x_peer(self):
        return self.device(self.z, self.y, 1 - self.x, self.r)

    def y_peer(self):
        return self.device(self.z, 1 - self.y, self.x, self.r)

    def z_to(self, j):
        return lax.rem(self.z + 1 + j, self.sh.depth)

    def z_from(self, j):
        return lax.rem(self.z + self.sh.depth - 1 - j, self.sh.depth)

    def z_peer(self, j):
        return self.device(self.z_to(j), self.y, self.x, self.r)

    def plane_place(self, j):
        return (self.y if j == 0 else 1 - self.y, self.x if j == 1 else 1 - self.x)

    def plane_peer(self, j):
        y, x = self.plane_place(j)
        return self.device(self.z, y, x, self.r)

    def ring(self, step):
        count = self.sh.count
        return (lax.rem(self.s + count + step, count), self.r)

    def a_peer(self):
        flip_y, flip_x = 1 - self.r, self.r
        y = self.y + flip_y * (1 - 2 * self.y)
        x = self.x + flip_x * (1 - 2 * self.x)
        return self.device(self.z, y, x, self.r)

    def b_peer(self):
        flip_y, flip_x = self.r, 1 - self.r
        y = self.y + flip_y * (1 - 2 * self.y)
        x = self.x + flip_x * (1 - 2 * self.x)
        return self.device(self.z, y, x, self.r)

    def columns(self, r):
        half = self.sh.half
        return pl.ds(pl.multiple_of(r * half, half), half)


def send(src, dst, sems, index, device):
    return pltpu.make_async_remote_copy(
        src_ref=src, dst_ref=dst, send_sem=sems[0].at[index], recv_sem=sems[1].at[index],
        device_id=device, device_id_type=MESH,
    )


class Gather:
    def __init__(self, at, buf, lead, sems, group):
        self.at, self.buf, self.lead, self.sems, self.group = at, buf, lead, sems, group
        self.mine = at.columns(at.r)

    def cut(self, z, y, x):
        return self.buf.at[self.lead + (z, y, x, slice(None), self.mine)]

    def z_copy(self, j):
        at = self.at
        block = self.cut(at.z, at.y, at.x)
        return send(block, block, self.sems, (self.group, j), at.z_peer(j))

    def a_copy(self):
        at = self.at
        block = self.cut(slice(None), at.y, at.x)
        return send(block, block, self.sems, (self.group, at.sh.depth - 1), at.a_peer())

    def b_copy(self, core):
        at = self.at
        block = self.cut(slice(None), slice(None), at.x) if core == 0 else self.cut(
            slice(None), at.y, slice(None)
        )
        return send(block, block, self.sems, (self.group, at.sh.depth), at.b_peer())

    def core_copy(self):
        at = self.at
        block = self.cut(slice(None), slice(None), slice(None))
        return send(block, block, self.sems, (self.group, at.sh.depth + 1), at.sibling())

    def z_start(self):
        for j in range(self.at.sh.depth - 1):
            self.z_copy(j).start()

    def z_wait(self):
        for j in range(self.at.sh.depth - 1):
            self.z_copy(j).wait_recv()

    def a_start(self):
        self.a_copy().start()

    def a_wait(self):
        self.a_copy().wait_recv()

    def b_start(self):
        for core in range(2):
            @pl.when(self.at.r == core)
            def _():
                self.b_copy(core).start()

    def b_wait(self):
        self.b_copy(0).wait_recv()

    def core_start(self):
        self.core_copy().start()

    def core_wait(self):
        self.core_copy().wait_recv()

    def sent(self):
        for j in range(self.at.sh.depth - 1):
            self.z_copy(j).wait_send()
        self.a_copy().wait_send()
        self.b_copy(0).wait_send()
        self.core_copy().wait_send()

    def step(self, stage):
        if stage == 0:
            self.z_start()
        elif stage == 1:
            self.z_wait()
            self.a_start()
        elif stage == 2:
            self.a_wait()
            self.b_start()
        elif stage == 3:
            self.b_wait()
            self.core_start()
        else:
            self.core_wait()


def enter(at, meanwhile):
    sh = at.sh
    partners = [at.sibling(), at.ring(1), at.ring(-1)] + [at.plane_peer(j) for j in range(3)]
    partners += [at.z_peer(j) for j in range(sh.depth - 1)]
    barrier = pltpu.get_barrier_semaphore()
    for partner in partners:
        pl.semaphore_signal(barrier, inc=1, device_id=partner, device_id_type=MESH)
    meanwhile()
    pl.semaphore_wait(barrier, len(partners))


def slab(p, segs):
    return pl.ds(pl.multiple_of(p * segs, segs), segs)


def sequence_rows(sh, p, stretch):
    return pl.ds(p + stretch * sh.span, sh.groups, stride=sh.stretches * sh.span)


def to_position_major(sh, stage, lanes, dest):
    tiles = sh.width // 128
    for j in range(tiles):
        lanes[j] = stage[:, j * 128 : (j + 1) * 128].astype(f32)

    def move(p, _):
        for j in range(tiles):
            both_stretches = [
                lanes[j, sequence_rows(sh, p, st), :] for st in range(sh.stretches)
            ]
            dest[slab(p, sh.segs), j * 128 : (j + 1) * 128] = jnp.concatenate(
                both_stretches, 0
            ).astype(dest.dtype)
        return 0

    lax.fori_loop(0, sh.span, move, 0, unroll=4)


def wrap_before(sh, at, got):
    half = sh.groups
    wrapped = jnp.concatenate([jnp.zeros((half, sh.width), f32), got[:half]], 0)
    return jnp.where(at.s == 0, wrapped, got)


def wrap_after(sh, at, got):
    half = sh.groups
    wrapped = jnp.concatenate([got[half:], jnp.zeros((half, sh.width), f32)], 0)
    return jnp.where(at.s == sh.count - 1, wrapped, got)


def decay_over(rate, positions):
    return jnp.exp(-positions * rate)


class Exchange:
    def __init__(self, sh, at, onward, own, near, whole, far, sems):
        self.sh, self.at, self.onward = sh, at, onward
        self.own, self.near, self.whole, self.far, self.sems = own, near, whole, far, sems
        self.u = self.turn(2 * at.y + at.x, 4)
        self.v = self.turn(at.z, sh.depth)

    def turn(self, place, count):
        return place if self.onward else count - 1 - place

    def near_copy(self, j):
        return send(self.own, self.near.at[j], self.sems, j, self.at.plane_peer(j))

    def far_copy(self, j):
        return send(self.whole, self.far.at[j], self.sems, 3 + j, self.at.z_peer(j))

    def from_near(self, j):
        y, x = self.at.plane_place(j)
        return self.turn(2 * y + x, 4)

    def from_far(self, j):
        return self.turn(self.at.z_from(j), self.sh.depth)

    def sent(self):
        for j in range(3):
            self.near_copy(j).wait_send()
        for j in range(self.sh.depth - 1):
            self.far_copy(j).wait_send()


def fade(rate, steps, length):
    return jnp.exp(-(steps.astype(f32) * length) * rate)


class Carry(Exchange):
    def __init__(self, sh, at, onward, own, near, whole, far, sems, give, take):
        super().__init__(sh, at, onward, own, near, whole, far, sems)
        self.give, self.take = give, take

    def piece(self, y, x):
        return self.own.at[y, :, self.at.columns(x)]

    def near_copy(self, j):
        y, x = self.at.plane_place(j)
        return send(self.piece(y, x), self.near.at[j], self.sems, j, self.at.plane_peer(j))

    def give_copy(self, j):
        at = self.at
        return send(
            self.give.at[j], self.take.at[:, at.y, :, at.columns(at.x)], self.sems,
            2 + self.sh.depth + j, at.plane_peer(j),
        )

    def start(self, totals):
        for i, part in enumerate(totals):
            self.own[i] = part
        for j in range(3):
            self.near_copy(j).start()

    def after_plane(self, rates):
        sh, at = self.sh, self.at
        span = float(sh.span)
        self.rate = rates[:, at.columns(at.x)]
        for j in range(3):
            self.near_copy(j).wait_recv()
        parts = [(self.u, self.own[at.y, :, at.columns(at.x)])]
        parts += [(self.from_near(j), self.near[j]) for j in range(3)]
        self.parts = parts
        self.whole[...] = sum(fade(self.rate, 3 - u, span) * part for u, part in parts)
        for j in range(sh.depth - 1):
            self.far_copy(j).start()

    def after_z(self):
        sh, at = self.sh, self.at
        span, plane, half = float(sh.span), 4.0 * sh.span, sh.groups
        rate = self.rate
        for j in range(sh.depth - 1):
            self.far_copy(j).wait_recv()
        planes = [(self.v, self.whole[...])]
        planes += [(self.from_far(j), self.far[j]) for j in range(sh.depth - 1)]
        before, every = self.before(planes, self.v, plane), 0.0
        for v, part in planes:
            every += fade(rate, sh.depth - 1 - v, plane) * part

        def entering(u):
            state = self.before(self.parts, u, span) + fade(rate, u, span) * before
            across = fade(rate, self.v * 4 + u, span)
            if self.onward:
                earlier = across * every[:half]
                return state + jnp.concatenate([jnp.zeros_like(earlier), earlier], 0)
            later = across * every[half:]
            return state + jnp.concatenate([later, jnp.zeros_like(later)], 0)

        for j in range(3):
            self.give[j, 0] = entering(self.from_near(j))
            if self.onward:
                self.give[j, 1] = every
            self.give_copy(j).start()
        mine = at.columns(at.x)
        self.take[0, at.y, :, mine] = entering(self.u)
        if self.onward:
            self.take[1, at.y, :, mine] = every

    def before(self, parts, place, length):
        total = 0.0
        for u, part in parts:
            gap = fade(self.rate, jnp.maximum(place - 1 - u, 0), length)
            total += jnp.where(u < place, gap, 0.0) * part
        return total

    def finish(self):
        for j in range(3):
            self.give_copy(j).wait_recv()

    def sent(self):
        super().sent()
        for j in range(3):
            self.give_copy(j).wait_send()


class Tops(Exchange):
    def start(self, own):
        self.own[...] = own
        for j in range(3):
            self.near_copy(j).start()

    def after_plane(self, rate):
        span = float(self.sh.span)
        for j in range(3):
            self.near_copy(j).wait_recv()
        most = self.own[...] - (3 - self.u).astype(f32) * span * rate
        for j in range(3):
            gap = (3 - self.from_near(j)).astype(f32) * span
            most = jnp.maximum(most, self.near[j] - gap * rate)
        self.whole[...] = most
        for j in range(self.sh.depth - 1):
            self.far_copy(j).start()

    def after_z(self, rate):
        sh = self.sh
        for j in range(sh.depth - 1):
            self.far_copy(j).wait_recv()
        plane = 4.0 * sh.span
        most = self.whole[...] - (sh.depth - 1 - self.v).astype(f32) * plane * rate
        for j in range(sh.depth - 1):
            gap = (sh.depth - 1 - self.from_far(j)).astype(f32) * plane
            most = jnp.maximum(most, self.far[j] - gap * rate)
        half = sh.groups
        return jnp.maximum(most[:half] - float(sh.count * sh.span) * rate, most[half:])


class Scatter:
    def __init__(self, at, buf, m, bufs, sems, number, final, out, result):
        self.at, self.buf, self.m, self.sems, self.number = at, buf, m, sems, number
        self.core_in, self.b_in, self.a_in, self.z_in = [
            held.at[number % slots] for held, slots in zip(bufs, HELD)
        ]
        self.final, self.out, self.result = final, out, result
        self.mine, self.theirs = at.columns(at.r), at.columns(1 - at.r)
        self.age = 0

    def cut(self, z, y, x, columns):
        return self.buf.at[self.m, z, y, x, :, columns]

    def core_copy(self):
        every = slice(None)
        return send(
            self.cut(every, every, every, self.theirs), self.core_in, self.sems,
            (self.number, 0), self.at.sibling(),
        )

    def b_copy(self, core):
        at, every = self.at, slice(None)
        src = (
            self.cut(every, every, 1 - at.x, self.mine) if core == 0
            else self.cut(every, 1 - at.y, every, self.mine)
        )
        return send(src, self.b_in, self.sems, (self.number, 1), at.b_peer())

    def a_copy(self):
        at, every = self.at, slice(None)
        y = at.y + (1 - at.r) * (1 - 2 * at.y)
        x = at.x + at.r * (1 - 2 * at.x)
        return send(
            self.cut(every, y, x, self.mine), self.a_in, self.sems, (self.number, 2), at.a_peer()
        )

    def z_copy(self, j):
        at = self.at
        return send(
            self.cut(at.z_to(j), at.y, at.x, self.mine), self.z_in.at[j], self.sems,
            (self.number, 3 + j), at.z_peer(j),
        )

    def rows_of(self, r):
        own = self.at.sh.own
        return pl.ds(pl.multiple_of(r * own, own), own)

    def last_copy(self):
        at = self.at
        return send(
            self.final.at[self.result, self.rows_of(1 - at.r)],
            self.out.at[self.result, :, self.mine], self.sems,
            (self.number, 2 + at.sh.depth), at.sibling(),
        )

    def add(self, z, y, x, got):
        where = (self.m, z, y, x, slice(None), self.mine)
        self.buf[where] = self.buf[where] + got

    def advance(self):
        if self.age in SCATTER_AT:
            self.step(SCATTER_AT.index(self.age))
        self.age += 1

    def done(self):
        return self.age > SCATTER_AT[-1]

    def step(self, stage):
        at, sh = self.at, self.at.sh
        if stage == 0:
            self.core_copy().start()
        elif stage == 1:
            self.core_copy().wait_recv()

            def each(z, _):
                for y in range(2):
                    for x in range(2):
                        self.add(z, y, x, self.core_in[z, y, x])
                return 0

            lax.fori_loop(0, sh.depth, each, 0)
            for core in range(2):
                @pl.when(at.r == core)
                def _():
                    self.b_copy(core).start()
        elif stage == 2:
            self.b_copy(0).wait_recv()

            def each(z, _):
                for q in range(2):
                    y = (1 - at.r) * q + at.r * at.y
                    x = at.r * q + (1 - at.r) * at.x
                    self.add(z, y, x, self.b_in[z, q])
                return 0

            lax.fori_loop(0, sh.depth, each, 0)
            self.a_copy().start()
        elif stage == 3:
            self.a_copy().wait_recv()

            def each(z, _):
                self.add(z, at.y, at.x, self.a_in[z])
                return 0

            lax.fori_loop(0, sh.depth, each, 0)
            for j in range(sh.depth - 1):
                self.z_copy(j).start()
        elif stage == 4:
            for j in range(sh.depth - 1):
                self.z_copy(j).wait_recv()
            total = self.buf[self.m, at.z, at.y, at.x, :, self.mine].astype(f32)
            for j in range(sh.depth - 1):
                total += self.z_in[j].astype(f32)
            self.final[self.result] = total
            self.out[self.result, :, self.mine] = self.final[self.result, self.rows_of(at.r)]
            self.last_copy().start()
        else:
            self.last_copy().wait_recv()

    def sent(self):
        self.core_copy().wait_send()
        self.b_copy(0).wait_send()
        self.a_copy().wait_send()
        for j in range(self.at.sh.depth - 1):
            self.z_copy(j).wait_send()
        self.last_copy().wait_send()


def put_in_sequence_order(sh, p, block, lanes):
    for j in range(sh.width // 128):
        for st in range(sh.stretches):
            lanes[j, sequence_rows(sh, p, st), :] = block[
                st * sh.groups : (st + 1) * sh.groups, j * 128 : (j + 1) * 128
            ]


def spread_units(sh, table):
    unit = lax.broadcasted_iota(jnp.int32, (1, sh.half), 1).astype(f32)
    owner = jnp.floor((unit + 0.5) * (1.0 / sh.own))
    source = unit + owner * float(sh.own * (sh.parts - 1))
    row = lax.broadcasted_iota(jnp.int32, (sh.width, sh.half), 0).astype(f32)
    for i in range(2):
        chosen = jnp.where(row + float(i * sh.width) == source, 1.0, 0.0)
        table[: sh.width, i * sh.half : (i + 1) * sh.half] = chosen.astype(bf16)


def split_units(sh, hidden, table):
    own, block = sh.own, 2 * sh.width
    wide = hidden.astype(f32)
    pieces = []
    for c in range(sh.parts):
        turned = wide if c == 0 else pltpu.roll(wide, sh.inner - c * own, 1)
        pieces += [turned[:, t * block : (t + 1) * block] for t in range(2)]
    left = jnp.concatenate(pieces, 0).astype(bf16)
    got = dot(left[:, : sh.width], table[: sh.width, : sh.half])
    got += dot(left[:, sh.width :], table[: sh.width, sh.half :])
    return [
        jnp.concatenate([got[(2 * c + t) * own : (2 * c + t + 1) * own] for t in range(2)], 1)
        for c in range(sh.parts)
    ]


def join_units(sh, parts, table, dest):
    own, block = sh.own, 2 * sh.width
    for c, part in enumerate(parts):
        rows = jnp.concatenate([part[:, t * sh.half : (t + 1) * sh.half] for t in range(2)], 0)
        high = rows.astype(bf16)
        low = (rows - high.astype(f32)).astype(bf16)
        both_terms = jnp.concatenate([high, low], 0)
        got = jnp.concatenate(
            [
                dot_nt(both_terms, table[: sh.width, i * sh.half : (i + 1) * sh.half])
                for i in range(2)
            ],
            1,
        )
        got = got[: 2 * own] + got[2 * own :]
        if c > 0:
            got = pltpu.roll(got, c * own, 1)
        for t in range(2):
            where = (slice(None), slice(t * block, (t + 1) * block))
            value = got[t * own : (t + 1) * own]
            dest[where] = value if c == 0 else dest[where] + value


def layer_kernel(
    sh,
    tok_hbm, cot_hbm, key_ref, value_ref, gate_ref, output_ref, screen_ref, hidden_ref, return_ref,
    vg0, vg1, vg2, vg3, vg4, vg5, vg6, vg7, vg8, vg9, vg10,
    out_hbm, ig_hbm, grads_out, hidden_out, small_out, final_out, den_park, gate_park, key_park, value_park,
    gatein_park,
    w, vall, vecs, rates, pack, got_pack, narrow,
    lanes, f1, f2, f3, f4, f5, xp, b1, b2, b3, b4, k, v, cotp, b8, b9,
    halo, halo32, st_own, st_near, st_whole, st_far, st_give, st_take,
    bk_own, bk_near, bk_whole, bk_far, bk_give, bk_take,
    top_own, top_near, top_whole, top_far, acc, tile, plane,
    core_in, b_in, a_in, z_in, final,
    local_sem, pack_sems, ag_send, ag_recv, st_send, st_recv, bk_send, bk_recv, top_send, top_recv,
    halo_send, halo_recv, rs_send, rs_recv, tile_send, tile_recv, emit_sem,
):
    at = Place(sh)
    segs, span, rows, width = sh.segs, sh.span, sh.rows, sh.width
    mine, theirs = at.columns(at.r), at.columns(1 - at.r)
    gathers = [Gather(at, w, (m,), (ag_send, ag_recv), m) for m in range(sh.mats)]
    gather_v = Gather(at, vall, (), (ag_send, ag_recv), sh.mats)
    clock = [0]

    def period():
        for stage, after in enumerate(GATHER_AT):
            m = clock[0] - after
            if 0 <= m < sh.mats:
                gathers[m].step(stage)
        clock[0] += 1

    def gathered(m):
        while clock[0] <= m + GATHER_AT[-1]:
            period()
    halo_sems = (halo_send, halo_recv)

    def local(src, dst, i):
        return pltpu.make_async_copy(src, dst, local_sem.at[i])

    def matrix(m):
        return w[m].reshape(width, width)

    def set_matrix(m, value):
        w[m] = value.astype(bf16).reshape(sh.depth, 2, 2, sh.chip, width)

    def vec(i):
        return vecs[i : i + 1, :]

    load_tok = local(tok_hbm, b1, 0)
    load_tok.start()
    turn = (2 * at.s + at.r) * sh.own

    def pack_up():
        for m, ref in enumerate((key_ref, value_ref, gate_ref, output_ref, screen_ref)):
            pack[m, : sh.own] = ref[...]
        vecs[...] = jnp.zeros_like(vecs)
        for i, ref in enumerate((vg0, vg1, vg2, vg3, vg4, vg5, vg6, vg7, vg8, vg9, vg10)):
            vecs[i : i + 1, : sh.own] = ref[...].astype(f32)
        pack[sh.mats, :16] = pltpu.roll(vecs[...], turn, 1).astype(bf16)

    enter(at, pack_up)

    def pack_copy(i, first, last):
        return send(
            pack.at[pl.ds(first, last - first), :, theirs], got_pack.at[pl.ds(first, last - first)],
            (pack_sems.at[0], pack_sems.at[1]), i, at.sibling(),
        )

    pack_vectors = pack_copy(0, sh.mats, sh.mats + 1)
    pack_squares = pack_copy(1, 0, FIRST_PART)
    pack_parts = pack_copy(2, FIRST_PART, sh.mats)
    pack_vectors.start()
    pack_squares.start()
    load_tok.wait()
    to_position_major(sh, b1, lanes, xp)
    halo_x = send(xp.at[pl.ds(rows - segs, segs)], halo.at[0], halo_sems, 0, at.ring(1))
    halo_x.start()
    load_cot = local(cot_hbm, b1, 1)
    load_cot.start()

    def assemble(first, last):
        for m in range(first, last):
            own = pack[m, : sh.own, mine].astype(f32)
            other = got_pack[m, : sh.own].astype(f32)
            above = jnp.where(at.r == 0, own, other)
            below = jnp.where(at.r == 0, other, own)
            w[m, at.z, at.y, at.x, :, mine] = jnp.concatenate([above, below], 0).astype(bf16)

    pack_vectors.wait_recv()
    vall[at.z, at.y, at.x, :, mine] = (
        pack[sh.mats, :16, mine].astype(f32) + got_pack[sh.mats, :16].astype(f32)
    ).astype(bf16)
    gather_v.step(0)
    pack_squares.wait_recv()
    assemble(0, FIRST_PART)
    period()
    period()
    spread_units(sh, b9)
    for c, part in enumerate(split_units(sh, hidden_ref[...], b9)):
        pack[FIRST_PART + 2 * c, : sh.own] = part.astype(bf16)
    back_rows = return_ref[...].astype(f32)
    for c in range(sh.parts):
        pack[FIRST_PART + 2 * c + 1, : sh.own] = back_rows[c * sh.own : (c + 1) * sh.own].astype(bf16)
    pack_parts.start()
    load_cot.wait()
    to_position_major(sh, b1, lanes, cotp)
    gather_v.step(1)
    period()
    gather_v.step(2)
    period()
    pack_parts.wait_recv()
    assemble(FIRST_PART, sh.mats)
    gather_v.step(3)
    gather_v.step(4)
    spread = jnp.zeros((16, width), f32)
    for z in range(sh.depth):
        for i in range(4):
            spread += vall[z, i // 2, i % 2].astype(f32)
    vecs[...] = spread

    key_in, value_in, gate_in = b2, b3, b4
    halo_x.wait_recv()
    got, _ = normalise(halo[0].astype(f32))
    before_one = wrap_before(sh, at, got * vec(MIXER_G) + vec(MIXER_B))

    def blend_one(p, before):
        here = slab(p, segs)
        n1, _ = normalise(xp[here, :].astype(f32))
        one = n1 * vec(MIXER_G) + vec(MIXER_B)
        step = one - before
        key_in[here, :] = (before + step * vec(KEY_SHARE)).astype(bf16)
        value_in[here, :] = (before + step * vec(VALUE_SHARE)).astype(bf16)
        gate_in[here, :] = (before + step * vec(GATE_SHARE)).astype(bf16)
        return one

    before_one = lax.fori_loop(0, span // 2, blend_one, before_one, unroll=4)
    period()
    lax.fori_loop(span // 2, span, blend_one, before_one, unroll=4)
    parks = [local(key_in, key_park, 2), local(value_in, value_park, 3), local(gate_in, gatein_park, 4)]
    for copy in parks:
        copy.start()

    gathered(KEY)
    k[...] = dot(key_in[...], matrix(KEY)).astype(bf16)
    gathered(VALUE)
    v[...] = dot(value_in[...], matrix(VALUE)).astype(bf16)

    rates[...] = jnp.exp(vec(DECAY))
    rate = rates[...]
    keep = jnp.exp(-rate)
    zero = jnp.zeros((segs, width), f32)

    def add_up(p, state):
        a, b, top = state
        here = slab(p, segs)
        key = k[here, :].astype(f32)
        grown = jnp.exp(key)
        top = jnp.maximum(top - rate, key)
        return keep * a + grown * v[here, :].astype(f32), keep * b + grown, top

    sum_num, sum_den, top = lax.fori_loop(
        0, span, add_up, (zero, zero, jnp.full((segs, width), -jnp.inf, f32)), unroll=4
    )
    states = Carry(
        sh, at, True, st_own, st_near, st_whole, st_far, (st_send, st_recv), st_give, st_take
    )
    states.start((sum_num, sum_den))
    tops = Tops(
        sh, at, True, top_own, top_near, top_whole, top_far, (top_send, top_recv)
    )
    gathered(GATE)
    gate = f1
    gate[...] = sigmoid(dot(gate_in[...], matrix(GATE)))
    gate_out = local(gate, gate_park, 5)
    gate_out.start()
    states.after_plane(rates)
    period()
    states.after_z()
    tops.start(top)
    period()
    states.finish()
    carry, total = st_take.at[0], st_take.at[1]

    num, den, res, s2 = f3, f2, f4, f5
    gated, rg, hin, sin = b8, b9, b2, b3
    boost_rate = jnp.exp(vec(FIRST))

    def recur(p, state):
        a, b = state
        here = slab(p, segs)
        grown = jnp.exp(k[here, :].astype(f32))
        value = v[here, :].astype(f32)
        boost = grown * boost_rate
        num[here, :] = a
        den[here, :] = b
        mix = ((a + boost * value) / (b + boost)).astype(bf16).astype(f32)
        gated[here, :] = (gate[here, :] * mix).astype(bf16)
        return keep * a + grown * value, keep * b + grown

    lax.fori_loop(0, span, recur, (carry[0], carry[1]), unroll=4)
    den_out = local(den, den_park, 6)
    den_out.start()
    gathered(OUTPUT)
    res[...] = xp[...].astype(f32) + dot(gated[...], matrix(OUTPUT))

    last = pl.ds(rows - segs, segs)
    n2, _ = normalise(res[last, :])
    halo32[0] = n2 * vec(CHANNEL_G) + vec(CHANNEL_B)
    halo_two = send(halo32.at[0], halo32.at[1], halo_sems, 1, at.ring(1))
    halo_two.start()
    tops.after_plane(rate)
    period()
    for copy in parks:
        copy.wait()

    def blend_two(p, before):
        here = slab(p, segs)
        n2, _ = normalise(res[here, :])
        two = n2 * vec(CHANNEL_G) + vec(CHANNEL_B)
        step = two - before
        hin[here, :] = (before + step * vec(HIDDEN_SHARE)).astype(bf16)
        sin[here, :] = (before + step * vec(SCREEN_SHARE)).astype(bf16)
        return two

    n2, _ = normalise(res[pl.ds(0, segs), :])
    first_two = n2 * vec(CHANNEL_G) + vec(CHANNEL_B)
    lax.fori_loop(1, span, blend_two, first_two, unroll=7)
    halo_two.wait_recv()
    before_two = wrap_before(sh, at, halo32[1])
    blend_two(0, before_two)
    final_top = tops.after_z(rate)
    far = decay_over(rate, float(sh.count * span))
    scale = jnp.exp(-final_top)
    ends = [(far * total[i, : sh.groups] + total[i, sh.groups :]) * scale for i in range(2)]
    lane = lax.rem(width - at.s * (width // sh.count), width)
    ends = pltpu.roll(jnp.concatenate(ends + [final_top], 0), lane, 1)
    for i in range(3):
        final_out[i] = ends[i * sh.groups : (i + 1) * sh.groups, :128]
    gathered(SCREEN)
    s2[...] = sigmoid(dot(sin[...], matrix(SCREEN)))
    rg[...] = (cotp[...].astype(f32) * s2[...]).astype(bf16)
    gate_out.wait()
    den_out.wait()

    bufs = (core_in, b_in, a_in, z_in)
    started, flying, landed = [], [], []

    def tick():
        period()
        for one in list(flying):
            one.advance()
            if one.done():
                flying.remove(one)
                landed.append(one)

    def scatter(m, result=None):
        number = len(started)
        one = Scatter(
            at, w, m, bufs, (rs_send, rs_recv), number, final, grads_out,
            m if result is None else result,
        )
        started.append(one)
        flying.append(one)
        tick()

    def all_sent(number):
        one = started[number]
        while not one.done():
            tick()
        landed.remove(one)
        one.sent()

    ret, hb, act, hg = f1, f2, b4, b1
    tiles = [(j, slice(j * 128, (j + 1) * 128)) for j in range(width // 128)]
    for c in range(sh.parts):
        into, back = FIRST_PART + 2 * c, FIRST_PART + 2 * c + 1
        gathered(into)
        up = jnp.maximum(dot(hin[...], matrix(into)), 0.0)
        for j, columns in tiles:
            lanes[j] = up[:, columns]
        act[...] = (up * up).astype(bf16)
        gathered(back)
        if c == 0:
            ret[...] = dot(act[...], matrix(back))
        else:
            ret[...] += dot(act[...], matrix(back))
        relu = jnp.concatenate([lanes[j] for j, _ in tiles], 1)
        hg[...] = (dot_nt(rg[...], matrix(back)) * (2.0 * relu)).astype(bf16)
        gathers[back].sent()
        set_matrix(back, dot_tn(act[...], rg[...]))
        scatter(back, FIRST_PART + c)
        if c == 0:
            hb[...] = dot_nt(hg[...], matrix(into))
        else:
            hb[...] += dot_nt(hg[...], matrix(into))
        gathers[into].sent()
        set_matrix(into, dot_tn(hin[...], hg[...]))
        scatter(into, FIRST_PART + sh.parts + c)

    sg, sb, og = b4, f5, b1
    first = pl.ds(0, segs)
    cot0 = cotp[first, :].astype(f32)
    sg0 = (cot0 * ret[first, :] * s2[first, :] * (1.0 - s2[first, :])).astype(bf16)
    sb0 = dot_nt(sg0, matrix(SCREEN))
    halo32[2] = hb[first, :] * (1.0 - vec(HIDDEN_SHARE)) + sb0 * (1.0 - vec(SCREEN_SHARE))
    back_two = send(halo32.at[2], halo32.at[3], halo_sems, 2, at.ring(-1))
    back_two.start()
    load_gatein = local(gatein_park, b2, 7)
    load_gatein.start()
    acc[...] = jnp.zeros_like(acc)

    def finish(p, _):
        here = slab(p, segs)
        s = s2[here, :]
        held = ret[here, :]
        put_in_sequence_order(sh, p, res[here, :] + s * held, lanes)
        sg[here, :] = (cotp[here, :].astype(f32) * held * s * (1.0 - s)).astype(bf16)
        return 0

    lax.fori_loop(0, span, finish, 0, unroll=4)
    sb[...] = dot_nt(sg[...], matrix(SCREEN))
    tick()
    out_copies = []
    for j, columns in tiles:
        if j >= 2:
            out_copies[j - 2].wait()
        narrow[j % 2] = lanes[j].astype(bf16)
        copy = pltpu.make_async_copy(narrow.at[j % 2], out_hbm.at[:, columns], emit_sem.at[0, j])
        copy.start()
        out_copies.append(copy)

    rgrad = f1

    def back_second(p, before, ahead):
        here = slab(p, segs)
        n2, inverse = normalise(res[here, :])
        two = n2 * vec(CHANNEL_G) + vec(CHANNEL_B)
        step = two - before
        hb_here, sb_here = hb[here, :], sb[here, :]
        acc[0] += hb_here * step
        acc[1] += sb_here * step
        grad = hb_here * vec(HIDDEN_SHARE) + sb_here * vec(SCREEN_SHARE) + ahead
        acc[2] += grad * n2
        acc[3] += grad
        down = cotp[here, :].astype(f32) + norm_back(grad, n2, inverse, vec(CHANNEL_G))
        rgrad[here, :] = down
        og[here, :] = down.astype(bf16)
        return two

    def back_second_step(p, before):
        there = slab(p + 1, segs)
        ahead = hb[there, :] * (1.0 - vec(HIDDEN_SHARE)) + sb[there, :] * (1.0 - vec(SCREEN_SHARE))
        return back_second(p, before, ahead)

    before = lax.fori_loop(0, span - 1, back_second_step, before_two, unroll=7)
    back_two.wait_recv()
    back_second(span - 1, before, wrap_after(sh, at, halo32[3]))
    for copy in out_copies[-2:]:
        copy.wait()
    load_gate = local(gate_park, f2, 8)
    load_gate.start()
    load_den = local(den_park, f5, 9)
    load_den.start()
    tick()
    gated_grad = f4
    gated_grad[...] = dot_nt(og[...], matrix(OUTPUT))
    load_gate.wait()
    load_den.wait()

    gate, den, gate_grad, mg = f2, f5, b9, cotp

    def totals_back(i, state):
        a, b = state
        here = slab(span - 1 - i, segs)
        grown = jnp.exp(k[here, :].astype(f32))
        value = v[here, :].astype(f32)
        boost = grown * boost_rate
        over = 1.0 / (den[here, :] + boost)
        raw = (num[here, :] + boost * value) * over
        mix = raw.astype(bf16).astype(f32)
        grad, s = gated_grad[here, :], gate[here, :]
        through = (grad * s).astype(bf16)
        mg[here, :] = through
        gate_grad[here, :] = (grad * mix * s * (1.0 - s)).astype(bf16)
        num_grad = through.astype(f32) * over
        return keep * a + num_grad, keep * b - num_grad * raw

    sum_num, sum_den = lax.fori_loop(0, span, totals_back, (zero, zero), unroll=4)
    adjoints = Carry(
        sh, at, False, bk_own, bk_near, bk_whole, bk_far, (bk_send, bk_recv), bk_give, bk_take
    )
    adjoints.start((sum_num, sum_den))
    gathers[OUTPUT].sent()
    set_matrix(OUTPUT, dot_tn(gated[...], og[...]))
    scatter(OUTPUT)
    adjoints.after_plane(rates)
    gathers[SCREEN].sent()
    set_matrix(SCREEN, dot_tn(sin[...], sg[...]))
    scatter(SCREEN)
    load_keyin = local(key_park, b3, 10)
    load_keyin.start()
    load_valin = local(value_park, b4, 11)
    load_valin.start()
    adjoints.after_z()
    gate_back = f4
    gate_back[...] = dot_nt(gate_grad[...], matrix(GATE))
    load_gatein.wait()
    gathers[GATE].sent()
    set_matrix(GATE, dot_tn(b2[...], gate_grad[...]))
    scatter(GATE)
    adjoints.finish()
    carry = bk_take.at[0]

    kg, vg = b8, b1

    def recur_back(i, state):
        a, b = state
        here = slab(span - 1 - i, segs)
        grown = jnp.exp(k[here, :].astype(f32))
        value = v[here, :].astype(f32)
        boost = grown * boost_rate
        n, d = num[here, :], den[here, :]
        over = 1.0 / (d + boost)
        num_grad = mg[here, :].astype(f32) * over
        den_grad = -num_grad * ((n + boost * value) * over)
        inner = boost * (value * num_grad + den_grad)
        kg[here, :] = (grown * (value * a + b) + inner).astype(bf16)
        vg[here, :] = (grown * a + boost * num_grad).astype(bf16)
        acc[4] += inner
        acc[5] += n * a + d * b
        return keep * a + num_grad, keep * b + den_grad

    lax.fori_loop(0, span, recur_back, (carry[0], carry[1]), unroll=4)
    load_keyin.wait()
    load_valin.wait()
    spare = FIRST_PART
    all_sent(1)
    set_matrix(spare, dot_tn(b3[...], kg[...]))
    scatter(spare, KEY)
    all_sent(0)
    set_matrix(spare + 1, dot_tn(b4[...], vg[...]))
    scatter(spare + 1, VALUE)

    key_back, value_back = f2, f3
    key_back[...] = dot_nt(kg[...], matrix(KEY))
    value_back[...] = dot_nt(vg[...], matrix(VALUE))

    def ahead_of(where):
        return (
            key_back[where, :] * (1.0 - vec(KEY_SHARE))
            + value_back[where, :] * (1.0 - vec(VALUE_SHARE))
            + gate_back[where, :] * (1.0 - vec(GATE_SHARE))
        )

    halo32[4] = ahead_of(first)
    back_one = send(halo32.at[4], halo32.at[5], halo_sems, 3, at.ring(-1))
    back_one.start()
    tick()
    got, _ = normalise(halo[0].astype(f32))
    before_one = wrap_before(sh, at, got * vec(MIXER_G) + vec(MIXER_B))

    def back_first(p, before, ahead):
        here = slab(p, segs)
        n1, inverse = normalise(xp[here, :].astype(f32))
        one = n1 * vec(MIXER_G) + vec(MIXER_B)
        step = one - before
        kb, vb, gb = key_back[here, :], value_back[here, :], gate_back[here, :]
        acc[6] += kb * step
        acc[7] += vb * step
        acc[8] += gb * step
        grad = kb * vec(KEY_SHARE) + vb * vec(VALUE_SHARE) + gb * vec(GATE_SHARE) + ahead
        acc[9] += grad * n1
        acc[10] += grad
        down = rgrad[here, :] + norm_back(grad, n1, inverse, vec(MIXER_G))
        put_in_sequence_order(sh, p, down, lanes)
        return one

    def back_first_step(p, before):
        return back_first(p, before, ahead_of(slab(p + 1, segs)))

    middle = (span - 1) // 2 // 7 * 7
    before = lax.fori_loop(0, middle, back_first_step, before_one, unroll=7)
    tick()
    before = lax.fori_loop(middle, span - 1, back_first_step, before, unroll=7)
    back_one.wait_recv()
    back_first(span - 1, before, wrap_after(sh, at, halo32[5]))
    ig_copies = [
        pltpu.make_async_copy(lanes.at[j], ig_hbm.at[:, columns], emit_sem.at[1, j])
        for j, columns in tiles
    ]
    for copy in ig_copies:
        copy.start()

    def line(i):
        return jnp.sum(acc[i], 0, keepdims=True)

    order = (9, 10, 6, 7, 8, 5, 4, 2, 3, 0, 1)
    tile[0] = jnp.zeros((16, width), f32)
    for i, which in enumerate(order):
        value = line(which)
        if i == DECAY:
            value = -rate * keep * value
        tile[0, i : i + 1, :] = value
    tile_sems = (tile_send, tile_recv)
    sums = [
        send(tile.at[0], tile.at[1], tile_sems, 0, at.sibling()),
        send(tile.at[2], tile.at[3], tile_sems, 1, at.x_peer()),
        send(tile.at[4], tile.at[5], tile_sems, 2, at.y_peer()),
    ]
    sums[0].start()
    tick()
    for i in range(2):
        sums[i].wait_recv()
        tile[2 * i + 2] = tile[2 * i] + tile[2 * i + 1]
        sums[i + 1].start()
        tick()
    sums[2].wait_recv()
    tile[6] = tile[4] + tile[5]
    far_sums = [
        send(tile.at[6], plane.at[j], tile_sems, 3 + j, at.z_peer(j)) for j in range(sh.depth - 1)
    ]
    for copy in far_sums:
        copy.start()
    spread_units(sh, b9)
    while flying:
        tick()
    join_units(
        sh, [grads_out[FIRST_PART + sh.parts + c] for c in range(sh.parts)], b9, hidden_out
    )
    everything = tile[6]
    for j, copy in enumerate(far_sums):
        copy.wait_recv()
        everything += plane[j]
    small_out[...] = pltpu.roll(everything, lax.rem(width - turn, width), 1)[:, :128]
    for copy in ig_copies:
        copy.wait()

    for copy in (pack_vectors, pack_squares, pack_parts):
        copy.wait_send()
    halo_x.wait_send()
    for copy in (halo_two, back_two, back_one):
        copy.wait_send()
    gather_v.sent()
    gathers[KEY].sent()
    gathers[VALUE].sent()
    for one in landed:
        one.sent()
    for exchange in (states, tops, adjoints):
        exchange.sent()
    for copy in sums + far_sums:
        copy.wait_send()


def layer(sh, tokens, cotangent, matrices, vectors):
    R, D, S, Z = sh.rows, sh.width, sh.segs, sh.depth
    shape = jax.ShapeDtypeStruct
    narrow, wide = ((R, D), bf16), ((R, D), f32)
    w_shape = (sh.mats, Z, 2, 2, sh.chip, D)
    V = pltpu.VMEM
    dma = pltpu.SemaphoreType.DMA
    anywhere, in_vmem = pl.BlockSpec(memory_space=pl.ANY), pl.BlockSpec(memory_space=pltpu.VMEM)
    outs = [
        (narrow, anywhere), (wide, anywhere), (((sh.mats, sh.own, D), f32), in_vmem),
        (((sh.own, sh.inner), f32), in_vmem),
        (((16, 128), f32), in_vmem), (((3, sh.groups, 128), f32), in_vmem),
        (wide, anywhere), (wide, anywhere), (narrow, anywhere), (narrow, anywhere),
        (narrow, anywhere),
    ]
    scratch = (
        [
            V(w_shape, bf16), V((Z, 2, 2, 16, D), bf16), V((16, D), f32), V((1, D), f32),
            V((sh.mats + 1, 32, D), bf16), V((sh.mats + 1, 32, sh.half), bf16), V((2, R, 128), bf16), V((D // 128, R, 128), f32),
        ]
        + [V(*wide)] * 5
        + [V(*narrow)] * 10
        + [
            V((1, S, D), bf16), V((6, S, D), f32),
            V((2, S, D), f32), V((3, S, sh.half), f32), V((S, sh.half), f32),
            V((Z - 1, S, sh.half), f32), V((3, 2, S, sh.half), f32), V((2, 2, S, D), f32),
            V((2, S, D), f32), V((3, S, sh.half), f32), V((S, sh.half), f32),
            V((Z - 1, S, sh.half), f32), V((3, 1, S, sh.half), f32), V((1, 2, S, D), f32),
            V((S, D), f32), V((3, S, D), f32), V((S, D), f32), V((Z - 1, S, D), f32),
            V((VECTORS, S, D), f32),
            V((7, 16, D), f32), V((Z - 1, 16, D), f32),
            V((HELD[0], Z, 2, 2, sh.chip, sh.half), bf16), V((HELD[1], Z, 2, sh.chip, sh.half), bf16),
            V((HELD[2], Z, sh.chip, sh.half), bf16), V((HELD[3], Z - 1, sh.chip, sh.half), bf16),
            V((sh.mats, sh.chip, sh.half), f32),
            dma((12,)), dma((2, 3)),
        ]
        + [dma((sh.mats + 1, Z + 2))] * 2
        + [dma((Z + 5,))] * 6
        + [dma((4,))] * 2
        + [dma((sh.mats, Z + 3))] * 2
        + [dma((Z + 2,))] * 2
        + [dma((2, D // 128))]
    )
    return pl.pallas_call(
        functools.partial(layer_kernel, sh),
        out_shape=[shape(s, t) for (s, t), _ in outs],
        in_specs=[anywhere, anywhere] + [in_vmem] * (len(matrices) + len(vectors)),
        out_specs=[spec for _, spec in outs],
        scratch_shapes=scratch,
        compiler_params=pltpu.CompilerParams(
            collective_id=0, has_side_effects=True, vmem_limit_bytes=63 * 2**20
        ),
    )(
        tokens.reshape(R, D), cotangent.reshape(R, D), *matrices,
        *[vector.reshape(1, sh.own) for vector in vectors],
    )


def mm(left, right):
    return jnp.dot(left, right, preferred_element_type=f32)


def mm_nt(left, right):
    return lax.dot_general(left, right, (((1,), (1,)), ((), ())), preferred_element_type=f32)


def mm_tn(left, right):
    return lax.dot_general(left, right, (((0,), (0,)), ((), ())), preferred_element_type=f32)


def ring(value, steps):
    count = lax.axis_size("seq")
    return lax.ppermute(value, "seq", [(i, (i + steps) % count) for i in range(count)])


def entering(last, spot):
    got = ring(last, 1)
    pairs = got.reshape(-1, 2, got.shape[-1])
    wrapped = jnp.concatenate([jnp.zeros_like(pairs[:, :1]), pairs[:, :1]], 1)
    return jnp.where(spot == 0, wrapped, pairs).reshape(got.shape)


def leaving(first, spot):
    count = lax.axis_size("seq")
    got = ring(first, -1)
    pairs = got.reshape(-1, 2, got.shape[-1])
    wrapped = jnp.concatenate([pairs[:, 1:], jnp.zeros_like(pairs[:, :1])], 1)
    return jnp.where(spot == count - 1, wrapped, pairs).reshape(got.shape)


def plain_scan(k_ref, v_ref, carry_ref, decay_ref, first_ref, num_ref, den_ref, mix_ref):
    keep = jnp.exp(-jnp.exp(decay_ref[...]))
    boost_rate = jnp.exp(first_ref[...])

    def step(t, state):
        num, den = state
        k = jnp.exp(k_ref[t].astype(f32))
        v = v_ref[t].astype(f32)
        boost = k * boost_rate
        num_ref[t] = num
        den_ref[t] = den
        mix_ref[t] = (num + boost * v) / (den + boost)
        return keep * num + k * v, keep * den + k

    lax.fori_loop(0, k_ref.shape[0], step, (carry_ref[0], carry_ref[1]))


def plain_scan_back(
    k_ref, v_ref, num_ref, den_ref, mix_ref, grad_ref, carry_ref, decay_ref, first_ref,
    kg_ref, vg_ref, first_grad_ref, decay_grad_ref,
):
    keep = jnp.exp(-jnp.exp(decay_ref[...]))
    boost_rate = jnp.exp(first_ref[...])
    length = k_ref.shape[0]

    def step(i, state):
        adj_num, adj_den, first_sum, decay_sum = state
        t = length - 1 - i
        k = jnp.exp(k_ref[t].astype(f32))
        v = v_ref[t].astype(f32)
        boost = k * boost_rate
        num_grad = grad_ref[t].astype(f32) / (den_ref[t] + boost)
        den_grad = -num_grad * mix_ref[t]
        inner = boost * (v * num_grad + den_grad)
        kg_ref[t] = (k * (v * adj_num + adj_den) + inner).astype(bf16)
        vg_ref[t] = (k * adj_num + boost * num_grad).astype(bf16)
        first_sum = first_sum + inner
        decay_sum = decay_sum + num_ref[t] * adj_num + den_ref[t] * adj_den
        return keep * adj_num + num_grad, keep * adj_den + den_grad, first_sum, decay_sum

    zero = jnp.zeros_like(carry_ref[0])
    out = lax.fori_loop(0, length, step, (carry_ref[0], carry_ref[1], zero, zero))
    first_grad_ref[...] = out[2]
    decay_grad_ref[...] = out[3]


def call(kernel, shapes, *operands):
    space = pl.BlockSpec(memory_space=pltpu.VMEM)
    return pl.pallas_call(
        kernel,
        out_shape=[jax.ShapeDtypeStruct(s, t) for s, t in shapes],
        in_specs=[space] * len(operands),
        out_specs=[space] * len(shapes),
        compiler_params=pltpu.CompilerParams(vmem_limit_bytes=48 * 2**20),
    )(*operands)


def plain_body(
    tokens, mixer_gain, mixer_bias, key_blend, value_blend, gate_blend, time_decay, time_first,
    key_weight, value_weight, gate_weight, output_weight, channel_gain, channel_bias,
    hidden_blend, screen_blend, hidden_weight, screen_weight, return_weight, cotangent,
):
    groups, stretches, span, width = tokens.shape
    count = lax.axis_size("seq")
    owners = count * lax.axis_size("rep")
    spot = lax.axis_index("seq")
    segs = groups * stretches
    rows = span * segs
    own = width // owners
    inner = hidden_weight.shape[1]
    parts = inner // width

    vectors = (
        mixer_gain, mixer_bias, key_blend, value_blend, gate_blend, time_decay, time_first,
        channel_gain, channel_bias, hidden_blend, screen_blend,
    )
    squares = (key_weight, value_weight, gate_weight, output_weight, screen_weight)
    packed = jnp.concatenate(
        squares + (hidden_weight.reshape(own * parts, width), return_weight), 0
    )
    packed = lax.all_gather(packed, both, axis=0)
    spread_vectors = lax.all_gather(jnp.stack(vectors), both, axis=0)
    spread_vectors = jnp.swapaxes(spread_vectors, 0, 1).reshape(len(vectors), width).astype(f32)
    (
        mixer_g, mixer_b, key_share, value_share, gate_share, decay_log, first_log,
        channel_g, channel_b, hidden_share, screen_share,
    ) = [spread_vectors[i][None] for i in range(len(vectors))]

    def piece(start, size, shape):
        return packed[:, start : start + size].reshape(shape)

    w_key, w_value, w_gate, w_output, w_screen = [
        piece(own * i, own, (width, width)) for i in range(5)
    ]
    w_hidden = piece(own * 5, own * parts, (width, inner))
    w_return = piece(own * (5 + parts), own * parts, (inner, width))

    def position_major(a):
        return jnp.transpose(a, (2, 0, 1, 3)).reshape(rows, width)

    def shifted(a, first):
        return jnp.concatenate([first, a[:-segs]], 0)

    x = position_major(tokens).astype(f32)
    n1, inv1 = normalise(x)
    one = n1 * mixer_g + mixer_b
    before = shifted(one, entering(one[-segs:], spot))
    spread_one = one - before
    key_in = (before + spread_one * key_share).astype(bf16)
    value_in = (before + spread_one * value_share).astype(bf16)
    gate_in = (before + spread_one * gate_share).astype(bf16)
    k = mm(key_in, w_key).astype(bf16)
    v = mm(value_in, w_value).astype(bf16)
    gate = jax.nn.sigmoid(mm(gate_in, w_gate))

    rate = jnp.exp(decay_log)
    cube = (span, segs, width)
    offsets = jnp.arange(span, dtype=f32)[:, None, None]
    kw = k.reshape(cube).astype(f32)
    vw = v.reshape(cube).astype(f32)
    shifted_key = kw - (span - 1.0 - offsets) * rate
    ends = jnp.exp(shifted_key)
    totals = jnp.stack([jnp.sum(ends * vw, 0), jnp.sum(ends, 0)])
    tops = jnp.max(shifted_key, 0)
    everyone = lax.all_gather(jnp.concatenate([totals, tops[None]]), "seq", axis=0)
    everyone = everyone.reshape(count, 3, groups, stretches, width)
    everyone = jnp.transpose(everyone, (3, 0, 1, 2, 4)).reshape(
        stretches * count, 3, groups, width
    )
    order = jnp.arange(stretches * count, dtype=f32)

    def weights_for(here):
        gap = here - 1.0 - order[:, None]
        return jnp.where(gap >= 0, jnp.exp(-jnp.maximum(gap, 0.0) * (span * rate)), 0.0)

    def carried(here):
        return jnp.sum(weights_for(here)[:, None, None, :] * everyone[:, :2], 0)

    carry = jnp.stack([carried(j * count + spot.astype(f32)) for j in range(stretches)], 2)
    carry = carry.reshape(2, segs, width)
    final = carried(float(stretches * count))
    far = (stretches * count - 1.0 - order)[:, None] * (span * rate)
    top = jnp.max(everyone[:, 2] - far[:, None, :], 0)
    slab = width // count

    def own_slab(a):
        return lax.dynamic_slice_in_dim(a, spot * slab, slab, 1)

    final_top = own_slab(top)
    scaling = jnp.exp(-final_top)
    final_num = own_slab(final[0]) * scaling
    final_den = own_slab(final[1]) * scaling

    num, den, mix_raw = call(
        plain_scan, [(cube, f32)] * 3, k.reshape(cube), v.reshape(cube), carry,
        decay_log, first_log,
    )
    mix = mix_raw.reshape(rows, width).astype(bf16).astype(f32)
    gated = (gate * mix).astype(bf16)
    residual = x + mm(gated, w_output)
    n2, inv2 = normalise(residual)
    two = n2 * channel_g + channel_b
    before = shifted(two, entering(two[-segs:], spot))
    spread_two = two - before
    hidden_in = (before + spread_two * hidden_share).astype(bf16)
    screen_in = (before + spread_two * screen_share).astype(bf16)
    screen = jax.nn.sigmoid(mm(screen_in, w_screen))
    cot = position_major(cotangent).astype(f32)
    returned_grad = (cot * screen).astype(bf16)
    relu = jnp.maximum(mm(hidden_in, w_hidden), 0.0)
    act = jnp.square(relu).astype(bf16)
    returned = mm(act, w_return)
    output = (residual + screen * returned).astype(bf16)

    screen_grad = (cot * returned * screen * (1.0 - screen)).astype(bf16)
    hidden_grad = (mm_nt(returned_grad, w_return) * (2.0 * relu)).astype(bf16)
    dw_return = mm_tn(act, returned_grad)
    dw_hidden = mm_tn(hidden_in, hidden_grad)
    dw_screen = mm_tn(screen_in, screen_grad)
    hidden_back = mm_nt(hidden_grad, w_hidden)
    screen_back = mm_nt(screen_grad, w_screen)
    d_hidden_blend = jnp.sum(hidden_back * spread_two, 0)
    d_screen_blend = jnp.sum(screen_back * spread_two, 0)
    ahead = hidden_back * (1.0 - hidden_share) + screen_back * (1.0 - screen_share)
    two_grad = (
        hidden_back * hidden_share
        + screen_back * screen_share
        + jnp.concatenate([ahead[segs:], leaving(ahead[:segs], spot)], 0)
    )
    d_channel_gain = jnp.sum(two_grad * n2, 0)
    d_channel_bias = jnp.sum(two_grad, 0)
    residual_grad = cot + norm_back(two_grad, n2, inv2, channel_g)
    output_grad = residual_grad.astype(bf16)
    dw_output = mm_tn(gated, output_grad)
    gated_grad = mm_nt(output_grad, w_output)
    mix_grad = (gated_grad * gate).astype(bf16)
    gate_grad = (gated_grad * mix * gate * (1.0 - gate)).astype(bf16)

    boost = jnp.exp(first_log + kw)
    num_grad = mix_grad.reshape(cube).astype(f32) / (den + boost)
    den_grad = -num_grad * mix_raw
    fade = jnp.exp(-offsets * rate)
    totals = jnp.stack([jnp.sum(fade * num_grad, 0), jnp.sum(fade * den_grad, 0)])
    everyone = lax.all_gather(totals, "seq", axis=0)
    everyone = everyone.reshape(count, 2, groups, stretches, width)
    everyone = jnp.transpose(everyone, (3, 0, 1, 2, 4)).reshape(
        stretches * count, 2, groups, width
    )

    def carried_back(here):
        gap = order[:, None] - here - 1.0
        scale = jnp.where(gap >= 0, jnp.exp(-jnp.maximum(gap, 0.0) * (span * rate)), 0.0)
        return jnp.sum(scale[:, None, None, :] * everyone, 0)

    carry = jnp.stack([carried_back(j * count + spot.astype(f32)) for j in range(stretches)], 2)
    carry = carry.reshape(2, segs, width)
    key_grad, value_grad, first_sum, decay_sum = call(
        plain_scan_back, [(cube, bf16)] * 2 + [((segs, width), f32)] * 2,
        k.reshape(cube), v.reshape(cube), num, den, mix_raw, mix_grad.reshape(cube), carry,
        decay_log, first_log,
    )
    key_grad = key_grad.reshape(rows, width)
    value_grad = value_grad.reshape(rows, width)
    d_first = jnp.sum(first_sum, 0)
    d_decay = -rate[0] * jnp.exp(-rate[0]) * jnp.sum(decay_sum, 0)
    dw_key = mm_tn(key_in, key_grad)
    dw_value = mm_tn(value_in, value_grad)
    dw_gate = mm_tn(gate_in, gate_grad)
    key_back = mm_nt(key_grad, w_key)
    value_back = mm_nt(value_grad, w_value)
    gate_back = mm_nt(gate_grad, w_gate)
    d_key_blend = jnp.sum(key_back * spread_one, 0)
    d_value_blend = jnp.sum(value_back * spread_one, 0)
    d_gate_blend = jnp.sum(gate_back * spread_one, 0)
    ahead = (
        key_back * (1.0 - key_share)
        + value_back * (1.0 - value_share)
        + gate_back * (1.0 - gate_share)
    )
    one_grad = (
        key_back * key_share
        + value_back * value_share
        + gate_back * gate_share
        + jnp.concatenate([ahead[segs:], leaving(ahead[:segs], spot)], 0)
    )
    d_mixer_gain = jnp.sum(one_grad * n1, 0)
    d_mixer_bias = jnp.sum(one_grad, 0)
    input_grad = residual_grad + norm_back(one_grad, n1, inv1, mixer_g)

    packed = jnp.concatenate(
        [d.reshape(owners, own, width).astype(bf16) for d in (dw_key, dw_value, dw_gate, dw_output, dw_screen)]
        + [
            dw_hidden.reshape(owners, own * parts, width).astype(bf16),
            dw_return.reshape(owners, own * parts, width).astype(bf16),
        ],
        1,
    )
    summed = lax.psum_scatter(packed, both, scatter_dimension=0).astype(f32)
    small = jnp.stack(
        [
            d_mixer_gain, d_mixer_bias, d_key_blend, d_value_blend, d_gate_blend, d_decay, d_first,
            d_channel_gain, d_channel_bias, d_hidden_blend, d_screen_blend,
        ]
    )
    small = lax.psum(small, both)
    place = (spot * lax.axis_size("rep") + lax.axis_index("rep")) * own
    small = lax.dynamic_slice_in_dim(small, place, own, 1)

    def batch_major(a):
        return jnp.transpose(a.reshape(span, groups, stretches, width), (1, 2, 0, 3))

    return (
        batch_major(output),
        batch_major(input_grad),
        final_num,
        final_den,
        final_top,
        *[small[i] for i in range(7)],
        *[summed[own * i : own * (i + 1)] for i in range(4)],
        *[small[i] for i in range(7, 11)],
        summed[own * 5 : own * (5 + parts)].reshape(own, inner),
        summed[own * 4 : own * 5],
        summed[own * (5 + parts) :],
    )


def fused_body(sh, *args):
    (
        tokens, mixer_gain, mixer_bias, key_blend, value_blend, gate_blend, time_decay, time_first,
        key_weight, value_weight, gate_weight, output_weight, channel_gain, channel_bias,
        hidden_blend, screen_blend, hidden_weight, screen_weight, return_weight, cotangent,
    ) = args
    vectors = (
        mixer_gain, mixer_bias, key_blend, value_blend, gate_blend, time_decay, time_first,
        channel_gain, channel_bias, hidden_blend, screen_blend,
    )
    matrices = (
        key_weight, value_weight, gate_weight, output_weight, screen_weight, hidden_weight,
        return_weight,
    )
    output, input_grad, grads, hidden, small, finals = layer(
        sh, tokens, cotangent, matrices, vectors
    )[:6]
    share = sh.width // sh.count
    back = grads[FIRST_PART : FIRST_PART + sh.parts].reshape(sh.parts * sh.own, sh.width)
    small = [small[i, : sh.own] for i in range(VECTORS)]
    return (
        output.reshape(tokens.shape),
        input_grad.reshape(tokens.shape),
        *[finals[i, :, :share] for i in range(3)],
        *small[:7],
        *[grads[i] for i in (KEY, VALUE, GATE, OUTPUT)],
        *small[7:],
        hidden,
        grads[SCREEN],
        back,
    )


def body(*args):
    tokens, hidden_weight = args[0], args[16]
    groups, stretches, span, width = tokens.shape
    sh = Shape(lax.axis_size("seq"), span, groups, stretches, width, hidden_weight.shape[1])
    if lax.axis_size("rep") == 2 and sh.fits():
        return fused_body(sh, *args)
    return plain_body(*args)


def solution(mesh):
    rows = P("rep", None, "seq", None)
    owned = P(both)
    owned_rows = P(both, None)
    in_specs = (rows,) + (owned,) * 7 + (owned_rows,) * 4 + (owned,) * 4 + (owned_rows,) * 3 + (rows,)
    out_specs = (
        (rows,) * 2 + (P("rep", "seq"),) * 3 + (owned,) * 7 + (owned_rows,) * 4
        + (owned,) * 4 + (owned_rows,) * 3
    )
    return jax.shard_map(body, mesh=mesh, in_specs=in_specs, out_specs=out_specs, check_vma=False)
```

```python
import functools

import jax
import jax.numpy as jnp
from jax import lax
from jax.experimental import pallas as pl
from jax.experimental.pallas import tpu as pltpu
from jax.sharding import PartitionSpec as P

f32 = jnp.float32
bf16 = jnp.bfloat16
norm_eps = 1e-05
both = ("seq", "rep")
MESH = pl.DeviceIdType.MESH

KEY, VALUE, GATE, OUTPUT, SCREEN, FIRST_PART = 0, 1, 2, 3, 4, 5
GATHER_AT = (0, 2, 3, 5, 6)
SCATTER_AT = (0, 1, 3, 5, 7, 8)
HELD = (2, 4, 4, 4)
VECTORS = 11
(
    MIXER_G, MIXER_B, KEY_SHARE, VALUE_SHARE, GATE_SHARE, DECAY, FIRST,
    CHANNEL_G, CHANNEL_B, HIDDEN_SHARE, SCREEN_SHARE,
) = range(VECTORS)


def dot(left, right):
    return jnp.dot(left, right, preferred_element_type=f32)


def dot_nt(left, right):
    return lax.dot_general(left, right, (((1,), (1,)), ((), ())), preferred_element_type=f32)


def dot_tn(left, right):
    return lax.dot_general(left, right, (((0,), (0,)), ((), ())), preferred_element_type=f32)


def sigmoid(a):
    return 1.0 / (1.0 + jnp.exp(-a))


def normalise(values):
    centred = values - jnp.mean(values, -1, keepdims=True)
    inverse = lax.rsqrt(jnp.mean(centred * centred, -1, keepdims=True) + norm_eps)
    return centred * inverse, inverse


def norm_back(upstream, scaled, inverse, gain):
    inner = upstream * gain
    centred = inner - jnp.mean(inner, -1, keepdims=True)
    return inverse * (centred - scaled * jnp.mean(inner * scaled, -1, keepdims=True))


class Shape:
    def __init__(self, count, span, groups, stretches, width, inner):
        self.count, self.span, self.groups, self.stretches = count, span, groups, stretches
        self.width, self.inner = width, inner
        self.segs = groups * stretches
        self.rows = span * self.segs
        self.depth = count // 4
        self.chip = width // count
        self.own = self.chip // 2
        self.parts = inner // width
        self.mats = FIRST_PART + 2 * self.parts
        self.half = width // 2

    def fits(self):
        return (
            self.count % 4 == 0 and self.chip % 16 == 0 and self.own % 8 == 0 and self.own <= 32
            and self.half % 128 == 0 and self.groups == 8 and self.stretches == 2
            and self.parts == 4 and self.inner == 4 * self.width and self.rows == 1024
            and self.width // self.own == 32 and self.width // self.count <= 128
        )


class Place:
    def __init__(self, sh):
        self.sh = sh
        self.s = lax.axis_index("seq")
        self.r = lax.axis_index("rep")
        self.z = self.s // 4
        self.y = lax.rem(self.s // 2, 2)
        self.x = lax.rem(self.s, 2)

    def device(self, z, y, x, r):
        return ((z * 2 + y) * 2 + x, r)

    def sibling(self):
        return (self.s, 1 - self.r)

    def x_peer(self):
        return self.device(self.z, self.y, 1 - self.x, self.r)

    def y_peer(self):
        return self.device(self.z, 1 - self.y, self.x, self.r)

    def z_to(self, j):
        return lax.rem(self.z + 1 + j, self.sh.depth)

    def z_from(self, j):
        return lax.rem(self.z + self.sh.depth - 1 - j, self.sh.depth)

    def z_peer(self, j):
        return self.device(self.z_to(j), self.y, self.x, self.r)

    def plane_place(self, j):
        return (self.y if j == 0 else 1 - self.y, self.x if j == 1 else 1 - self.x)

    def plane_peer(self, j):
        y, x = self.plane_place(j)
        return self.device(self.z, y, x, self.r)

    def ring(self, step):
        count = self.sh.count
        return (lax.rem(self.s + count + step, count), self.r)

    def a_peer(self):
        flip_y, flip_x = 1 - self.r, self.r
        y = self.y + flip_y * (1 - 2 * self.y)
        x = self.x + flip_x * (1 - 2 * self.x)
        return self.device(self.z, y, x, self.r)

    def b_peer(self):
        flip_y, flip_x = self.r, 1 - self.r
        y = self.y + flip_y * (1 - 2 * self.y)
        x = self.x + flip_x * (1 - 2 * self.x)
        return self.device(self.z, y, x, self.r)

    def columns(self, r):
        half = self.sh.half
        return pl.ds(pl.multiple_of(r * half, half), half)


def send(src, dst, sems, index, device):
    return pltpu.make_async_remote_copy(
        src_ref=src, dst_ref=dst, send_sem=sems[0].at[index], recv_sem=sems[1].at[index],
        device_id=device, device_id_type=MESH,
    )


class Gather:
    def __init__(self, at, buf, lead, sems, group):
        self.at, self.buf, self.lead, self.sems, self.group = at, buf, lead, sems, group
        self.mine = at.columns(at.r)

    def cut(self, z, y, x):
        return self.buf.at[self.lead + (z, y, x, slice(None), self.mine)]

    def z_copy(self, j):
        at = self.at
        block = self.cut(at.z, at.y, at.x)
        return send(block, block, self.sems, (self.group, j), at.z_peer(j))

    def a_copy(self):
        at = self.at
        block = self.cut(slice(None), at.y, at.x)
        return send(block, block, self.sems, (self.group, at.sh.depth - 1), at.a_peer())

    def b_copy(self, core):
        at = self.at
        block = self.cut(slice(None), slice(None), at.x) if core == 0 else self.cut(
            slice(None), at.y, slice(None)
        )
        return send(block, block, self.sems, (self.group, at.sh.depth), at.b_peer())

    def core_copy(self):
        at = self.at
        block = self.cut(slice(None), slice(None), slice(None))
        return send(block, block, self.sems, (self.group, at.sh.depth + 1), at.sibling())

    def z_start(self):
        for j in range(self.at.sh.depth - 1):
            self.z_copy(j).start()

    def z_wait(self):
        for j in range(self.at.sh.depth - 1):
            self.z_copy(j).wait_recv()

    def a_start(self):
        self.a_copy().start()

    def a_wait(self):
        self.a_copy().wait_recv()

    def b_start(self):
        for core in range(2):
            @pl.when(self.at.r == core)
            def _():
                self.b_copy(core).start()

    def b_wait(self):
        self.b_copy(0).wait_recv()

    def core_start(self):
        self.core_copy().start()

    def core_wait(self):
        self.core_copy().wait_recv()

    def sent(self):
        for j in range(self.at.sh.depth - 1):
            self.z_copy(j).wait_send()
        self.a_copy().wait_send()
        self.b_copy(0).wait_send()
        self.core_copy().wait_send()

    def step(self, stage):
        if stage == 0:
            self.z_start()
        elif stage == 1:
            self.z_wait()
            self.a_start()
        elif stage == 2:
            self.a_wait()
            self.b_start()
        elif stage == 3:
            self.b_wait()
            self.core_start()
        else:
            self.core_wait()


def enter(at, meanwhile):
    sh = at.sh
    partners = [at.sibling(), at.ring(1), at.ring(-1)] + [at.plane_peer(j) for j in range(3)]
    partners += [at.z_peer(j) for j in range(sh.depth - 1)]
    barrier = pltpu.get_barrier_semaphore()
    for partner in partners:
        pl.semaphore_signal(barrier, inc=1, device_id=partner, device_id_type=MESH)
    meanwhile()
    pl.semaphore_wait(barrier, len(partners))


def slab(p, segs):
    return pl.ds(pl.multiple_of(p * segs, segs), segs)


def sequence_rows(sh, p, stretch):
    return pl.ds(p + stretch * sh.span, sh.groups, stride=sh.stretches * sh.span)


def to_position_major(sh, stage, lanes, dest):
    tiles = sh.width // 128
    for j in range(tiles):
        lanes[j] = stage[:, j * 128 : (j + 1) * 128].astype(f32)

    def move(p, _):
        for j in range(tiles):
            both_stretches = [
                lanes[j, sequence_rows(sh, p, st), :] for st in range(sh.stretches)
            ]
            dest[slab(p, sh.segs), j * 128 : (j + 1) * 128] = jnp.concatenate(
                both_stretches, 0
            ).astype(dest.dtype)
        return 0

    lax.fori_loop(0, sh.span, move, 0, unroll=4)


def wrap_before(sh, at, got):
    half = sh.groups
    wrapped = jnp.concatenate([jnp.zeros((half, sh.width), f32), got[:half]], 0)
    return jnp.where(at.s == 0, wrapped, got)


def wrap_after(sh, at, got):
    half = sh.groups
    wrapped = jnp.concatenate([got[half:], jnp.zeros((half, sh.width), f32)], 0)
    return jnp.where(at.s == sh.count - 1, wrapped, got)


def decay_over(rate, positions):
    return jnp.exp(-positions * rate)


class Exchange:
    def __init__(self, sh, at, onward, own, near, whole, far, sems):
        self.sh, self.at, self.onward = sh, at, onward
        self.own, self.near, self.whole, self.far, self.sems = own, near, whole, far, sems
        self.u = self.turn(2 * at.y + at.x, 4)
        self.v = self.turn(at.z, sh.depth)

    def turn(self, place, count):
        return place if self.onward else count - 1 - place

    def near_copy(self, j):
        return send(self.own, self.near.at[j], self.sems, j, self.at.plane_peer(j))

    def far_copy(self, j):
        return send(self.whole, self.far.at[j], self.sems, 3 + j, self.at.z_peer(j))

    def from_near(self, j):
        y, x = self.at.plane_place(j)
        return self.turn(2 * y + x, 4)

    def from_far(self, j):
        return self.turn(self.at.z_from(j), self.sh.depth)

    def sent(self):
        for j in range(3):
            self.near_copy(j).wait_send()
        for j in range(self.sh.depth - 1):
            self.far_copy(j).wait_send()


def fade(rate, steps, length):
    return jnp.exp(-(steps.astype(f32) * length) * rate)


class Carry(Exchange):
    def __init__(self, sh, at, onward, own, near, whole, far, sems, give, take):
        super().__init__(sh, at, onward, own, near, whole, far, sems)
        self.give, self.take = give, take

    def piece(self, y, x):
        return self.own.at[y, :, self.at.columns(x)]

    def near_copy(self, j):
        y, x = self.at.plane_place(j)
        return send(self.piece(y, x), self.near.at[j], self.sems, j, self.at.plane_peer(j))

    def give_copy(self, j):
        at = self.at
        return send(
            self.give.at[j], self.take.at[:, at.y, :, at.columns(at.x)], self.sems,
            2 + self.sh.depth + j, at.plane_peer(j),
        )

    def start(self, totals):
        for i, part in enumerate(totals):
            self.own[i] = part
        for j in range(3):
            self.near_copy(j).start()

    def after_plane(self, rates):
        sh, at = self.sh, self.at
        span = float(sh.span)
        self.rate = rates[:, at.columns(at.x)]
        for j in range(3):
            self.near_copy(j).wait_recv()
        parts = [(self.u, self.own[at.y, :, at.columns(at.x)])]
        parts += [(self.from_near(j), self.near[j]) for j in range(3)]
        self.parts = parts
        self.whole[...] = sum(fade(self.rate, 3 - u, span) * part for u, part in parts)
        for j in range(sh.depth - 1):
            self.far_copy(j).start()

    def after_z(self):
        sh, at = self.sh, self.at
        span, plane, half = float(sh.span), 4.0 * sh.span, sh.groups
        rate = self.rate
        for j in range(sh.depth - 1):
            self.far_copy(j).wait_recv()
        planes = [(self.v, self.whole[...])]
        planes += [(self.from_far(j), self.far[j]) for j in range(sh.depth - 1)]
        before, every = self.before(planes, self.v, plane), 0.0
        for v, part in planes:
            every += fade(rate, sh.depth - 1 - v, plane) * part

        def entering(u):
            state = self.before(self.parts, u, span) + fade(rate, u, span) * before
            across = fade(rate, self.v * 4 + u, span)
            if self.onward:
                earlier = across * every[:half]
                return state + jnp.concatenate([jnp.zeros_like(earlier), earlier], 0)
            later = across * every[half:]
            return state + jnp.concatenate([later, jnp.zeros_like(later)], 0)

        for j in range(3):
            self.give[j, 0] = entering(self.from_near(j))
            if self.onward:
                self.give[j, 1] = every
            self.give_copy(j).start()
        mine = at.columns(at.x)
        self.take[0, at.y, :, mine] = entering(self.u)
        if self.onward:
            self.take[1, at.y, :, mine] = every

    def before(self, parts, place, length):
        total = 0.0
        for u, part in parts:
            gap = fade(self.rate, jnp.maximum(place - 1 - u, 0), length)
            total += jnp.where(u < place, gap, 0.0) * part
        return total

    def finish(self):
        for j in range(3):
            self.give_copy(j).wait_recv()

    def sent(self):
        super().sent()
        for j in range(3):
            self.give_copy(j).wait_send()


class Tops(Exchange):
    def start(self, own):
        self.own[...] = own
        for j in range(3):
            self.near_copy(j).start()

    def after_plane(self, rate):
        span = float(self.sh.span)
        for j in range(3):
            self.near_copy(j).wait_recv()
        most = self.own[...] - (3 - self.u).astype(f32) * span * rate
        for j in range(3):
            gap = (3 - self.from_near(j)).astype(f32) * span
            most = jnp.maximum(most, self.near[j] - gap * rate)
        self.whole[...] = most
        for j in range(self.sh.depth - 1):
            self.far_copy(j).start()

    def after_z(self, rate):
        sh = self.sh
        for j in range(sh.depth - 1):
            self.far_copy(j).wait_recv()
        plane = 4.0 * sh.span
        most = self.whole[...] - (sh.depth - 1 - self.v).astype(f32) * plane * rate
        for j in range(sh.depth - 1):
            gap = (sh.depth - 1 - self.from_far(j)).astype(f32) * plane
            most = jnp.maximum(most, self.far[j] - gap * rate)
        half = sh.groups
        return jnp.maximum(most[:half] - float(sh.count * sh.span) * rate, most[half:])


class Total:
    def __init__(self, at, held, near, far, sems):
        self.at, self.held, self.near, self.far, self.sems = at, held, near, far, sems

    def core_copy(self):
        return send(self.held.at[0], self.held.at[1], self.sems, 0, self.at.sibling())

    def near_copy(self, j):
        return send(self.held.at[2], self.near.at[j], self.sems, 1 + j, self.at.plane_peer(j))

    def far_copy(self, j):
        return send(self.held.at[3], self.far.at[j], self.sems, 4 + j, self.at.z_peer(j))

    def start(self, lines):
        self.held[0] = jnp.zeros_like(self.held[0])
        for i, line in enumerate(lines):
            self.held[0, i : i + 1, :] = line
        self.core_copy().start()

    def after_core(self):
        self.core_copy().wait_recv()
        self.held[2] = self.held[0] + self.held[1]
        for j in range(3):
            self.near_copy(j).start()

    def after_plane(self):
        for j in range(3):
            self.near_copy(j).wait_recv()
        self.held[3] = self.held[2] + self.near[0] + self.near[1] + self.near[2]
        for j in range(self.at.sh.depth - 1):
            self.far_copy(j).start()

    def result(self):
        total = self.held[3]
        for j in range(self.at.sh.depth - 1):
            self.far_copy(j).wait_recv()
            total += self.far[j]
        return total

    def sent(self):
        self.core_copy().wait_send()
        for j in range(3):
            self.near_copy(j).wait_send()
        for j in range(self.at.sh.depth - 1):
            self.far_copy(j).wait_send()


class Scatter:
    def __init__(self, at, buf, m, bufs, sems, number, final, out, result):
        self.at, self.buf, self.m, self.sems, self.number = at, buf, m, sems, number
        self.core_in, self.b_in, self.a_in, self.z_in = [
            held.at[number % slots] for held, slots in zip(bufs, HELD)
        ]
        self.final, self.out, self.result = final, out, result
        self.mine, self.theirs = at.columns(at.r), at.columns(1 - at.r)
        self.age = 0

    def cut(self, z, y, x, columns):
        return self.buf.at[self.m, z, y, x, :, columns]

    def core_copy(self):
        every = slice(None)
        return send(
            self.cut(every, every, every, self.theirs), self.core_in, self.sems,
            (self.number, 0), self.at.sibling(),
        )

    def b_copy(self, core):
        at, every = self.at, slice(None)
        src = (
            self.cut(every, every, 1 - at.x, self.mine) if core == 0
            else self.cut(every, 1 - at.y, every, self.mine)
        )
        return send(src, self.b_in, self.sems, (self.number, 1), at.b_peer())

    def a_copy(self):
        at, every = self.at, slice(None)
        y = at.y + (1 - at.r) * (1 - 2 * at.y)
        x = at.x + at.r * (1 - 2 * at.x)
        return send(
            self.cut(every, y, x, self.mine), self.a_in, self.sems, (self.number, 2), at.a_peer()
        )

    def z_copy(self, j):
        at = self.at
        return send(
            self.cut(at.z_to(j), at.y, at.x, self.mine), self.z_in.at[j], self.sems,
            (self.number, 3 + j), at.z_peer(j),
        )

    def last_copy(self):
        at = self.at
        return send(
            self.final.at[self.result],
            self.out.at[self.result, :, self.mine], self.sems,
            (self.number, 2 + at.sh.depth), at.sibling(),
        )

    def add(self, z, y, x, got):
        where = (self.m, z, y, x, slice(None), self.mine)
        self.buf[where] = self.buf[where] + got

    def advance(self):
        if self.age in SCATTER_AT:
            self.step(SCATTER_AT.index(self.age))
        self.age += 1

    def done(self):
        return self.age > SCATTER_AT[-1]

    def step(self, stage):
        at, sh = self.at, self.at.sh
        if stage == 0:
            self.core_copy().start()
        elif stage == 1:
            self.core_copy().wait_recv()

            def each(z, _):
                for y in range(2):
                    for x in range(2):
                        self.add(z, y, x, self.core_in[z, y, x])
                return 0

            lax.fori_loop(0, sh.depth, each, 0, unroll=True)
            for core in range(2):
                @pl.when(at.r == core)
                def _():
                    self.b_copy(core).start()
        elif stage == 2:
            self.b_copy(0).wait_recv()

            def each(z, _):
                for q in range(2):
                    y = (1 - at.r) * q + at.r * at.y
                    x = at.r * q + (1 - at.r) * at.x
                    self.add(z, y, x, self.b_in[z, q])
                return 0

            lax.fori_loop(0, sh.depth, each, 0, unroll=True)
            self.a_copy().start()
        elif stage == 3:
            self.a_copy().wait_recv()

            def each(z, _):
                self.add(z, at.y, at.x, self.a_in[z])
                return 0

            lax.fori_loop(0, sh.depth, each, 0, unroll=True)
            for j in range(sh.depth - 1):
                self.z_copy(j).start()
        elif stage == 4:
            for j in range(sh.depth - 1):
                self.z_copy(j).wait_recv()
            total = self.buf[self.m, at.z, at.y, at.x, :, self.mine].astype(f32)
            for j in range(sh.depth - 1):
                total += self.z_in[j].astype(f32)
            above, below = total[: sh.own], total[sh.own :]
            self.final[self.result] = jnp.where(at.r == 0, below, above)
            self.out[self.result, :, self.mine] = jnp.where(at.r == 0, above, below)
            self.last_copy().start()
        else:
            self.last_copy().wait_recv()

    def sent(self):
        self.core_copy().wait_send()
        self.b_copy(0).wait_send()
        self.a_copy().wait_send()
        for j in range(self.at.sh.depth - 1):
            self.z_copy(j).wait_send()
        self.last_copy().wait_send()


def put_in_sequence_order(sh, p, block, lanes):
    for j in range(sh.width // 128):
        for st in range(sh.stretches):
            lanes[j, sequence_rows(sh, p, st), :] = block[
                st * sh.groups : (st + 1) * sh.groups, j * 128 : (j + 1) * 128
            ]


def spread_units(sh, table):
    unit = lax.broadcasted_iota(jnp.int32, (1, sh.half), 1).astype(f32)
    owner = jnp.floor((unit + 0.5) * (1.0 / sh.own))
    source = unit + owner * float(sh.own * (sh.parts - 1))
    row = lax.broadcasted_iota(jnp.int32, (sh.width, sh.half), 0).astype(f32)
    for i in range(2):
        chosen = jnp.where(row + float(i * sh.width) == source, 1.0, 0.0)
        table[: sh.width, i * sh.half : (i + 1) * sh.half] = chosen.astype(bf16)


def split_units(sh, hidden, table):
    own, block = sh.own, 2 * sh.width
    wide = hidden.astype(f32)
    pieces = []
    for c in range(sh.parts):
        turned = wide if c == 0 else pltpu.roll(wide, sh.inner - c * own, 1)
        pieces += [turned[:, t * block : (t + 1) * block] for t in range(2)]
    left = jnp.concatenate(pieces, 0).astype(bf16)
    got = dot(left[:, : sh.width], table[: sh.width, : sh.half])
    got += dot(left[:, sh.width :], table[: sh.width, sh.half :])
    return [
        jnp.concatenate([got[(2 * c + t) * own : (2 * c + t + 1) * own] for t in range(2)], 1)
        for c in range(sh.parts)
    ]


def join_units(sh, parts, table, dest):
    own, block = sh.own, 2 * sh.width
    for c, part in enumerate(parts):
        rows = jnp.concatenate([part[:, t * sh.half : (t + 1) * sh.half] for t in range(2)], 0)
        high = rows.astype(bf16)
        low = (rows - high.astype(f32)).astype(bf16)
        both_terms = jnp.concatenate([high, low], 0)
        got = jnp.concatenate(
            [
                dot_nt(both_terms, table[: sh.width, i * sh.half : (i + 1) * sh.half])
                for i in range(2)
            ],
            1,
        )
        got = got[: 2 * own] + got[2 * own :]
        if c > 0:
            got = pltpu.roll(got, c * own, 1)
        for t in range(2):
            where = (slice(None), slice(t * block, (t + 1) * block))
            value = got[t * own : (t + 1) * own]
            dest[where] = value if c == 0 else dest[where] + value


def layer_kernel(
    sh,
    tok_hbm, cot_hbm, key_ref, value_ref, gate_ref, output_ref, screen_ref, hidden_ref, return_ref,
    vg0, vg1, vg2, vg3, vg4, vg5, vg6, vg7, vg8, vg9, vg10,
    out_hbm, ig_hbm, squares_out, return_out, hidden_out, ends_out, den_park, gate_park, key_park, value_park,
    gatein_park,
    w, vall, vecs, rates, pack, got_pack,
    lanes, f1, f2, f3, f4, f5, xp, b1, b2, b3, b4, k, v, cotp, b8, b9,
    halo, halo32, st_own, st_near, st_whole, st_far, st_give, st_take,
    bk_own, bk_near, bk_whole, bk_far, bk_give, bk_take,
    top_own, top_near, top_whole, top_far, acc,
    sum_held, sum_near, sum_far, late_held, late_near, late_far, grads,
    core_in, b_in, a_in, z_in, final,
    local_sem, pack_sems, ag_send, ag_recv, st_send, st_recv, bk_send, bk_recv, top_send, top_recv,
    halo_send, halo_recv, rs_send, rs_recv, sum_send, sum_recv, late_send, late_recv, emit_sem,
):
    at = Place(sh)
    segs, span, rows, width = sh.segs, sh.span, sh.rows, sh.width
    mine, theirs = at.columns(at.r), at.columns(1 - at.r)
    gathers = [Gather(at, w, (m,), (ag_send, ag_recv), m) for m in range(sh.mats)]
    gather_v = Gather(at, vall, (), (ag_send, ag_recv), sh.mats)
    clock, began = [0], [0]

    def period():
        while began[0] < min(sh.mats, 2 * clock[0] + 1):
            gathers[began[0]].step(0)
            began[0] += 1
        for stage, after in list(enumerate(GATHER_AT))[1:]:
            m = clock[0] - after
            if 0 <= m < sh.mats:
                gathers[m].step(stage)
        clock[0] += 1

    def gathered(m):
        while clock[0] <= m + GATHER_AT[-1]:
            period()
    halo_sems = (halo_send, halo_recv)

    def local(src, dst, i):
        return pltpu.make_async_copy(src, dst, local_sem.at[i])

    def matrix(m):
        return w[m].reshape(width, width)

    def set_matrix(m, value):
        w[m] = value.astype(bf16).reshape(sh.depth, 2, 2, sh.chip, width)

    def vec(i):
        return vecs[i : i + 1, :]

    load_tok = local(tok_hbm, b1, 0)
    load_tok.start()
    turn = (2 * at.s + at.r) * sh.own

    def pack_up():
        for m, ref in enumerate((key_ref, value_ref, gate_ref, output_ref, screen_ref)):
            pack[m, : sh.own] = ref[...]
        vecs[...] = jnp.zeros_like(vecs)
        for i, ref in enumerate((vg0, vg1, vg2, vg3, vg4, vg5, vg6, vg7, vg8, vg9, vg10)):
            vecs[i : i + 1, : sh.own] = ref[...].astype(f32)
        pack[sh.mats, :16] = pltpu.roll(vecs[...], turn, 1).astype(bf16)

    enter(at, pack_up)

    def pack_copy(i, first, last):
        return send(
            pack.at[pl.ds(first, last - first), :, theirs], got_pack.at[pl.ds(first, last - first)],
            (pack_sems.at[0], pack_sems.at[1]), i, at.sibling(),
        )

    pack_vectors = pack_copy(0, sh.mats, sh.mats + 1)
    pack_squares = pack_copy(1, 0, FIRST_PART)
    pack_parts = pack_copy(2, FIRST_PART, sh.mats)
    pack_vectors.start()
    pack_squares.start()
    load_tok.wait()
    to_position_major(sh, b1, lanes, xp)
    halo_x = send(xp.at[pl.ds(rows - segs, segs)], halo.at[0], halo_sems, 0, at.ring(1))
    halo_x.start()
    load_cot = local(cot_hbm, b1, 1)
    load_cot.start()

    def assemble(first, last):
        for m in range(first, last):
            own = pack[m, : sh.own, mine].astype(f32)
            other = got_pack[m, : sh.own].astype(f32)
            above = jnp.where(at.r == 0, own, other)
            below = jnp.where(at.r == 0, other, own)
            w[m, at.z, at.y, at.x, :, mine] = jnp.concatenate([above, below], 0).astype(bf16)

    pack_vectors.wait_recv()
    vall[at.z, at.y, at.x, :, mine] = (
        pack[sh.mats, :16, mine].astype(f32) + got_pack[sh.mats, :16].astype(f32)
    ).astype(bf16)
    gather_v.step(0)
    pack_squares.wait_recv()
    assemble(0, FIRST_PART)
    period()
    period()
    spread_units(sh, b9)
    for c, part in enumerate(split_units(sh, hidden_ref[...], b9)):
        pack[FIRST_PART + 2 * c, : sh.own] = part.astype(bf16)
    back_rows = return_ref[...].astype(f32)
    for c in range(sh.parts):
        pack[FIRST_PART + 2 * c + 1, : sh.own] = back_rows[c * sh.own : (c + 1) * sh.own].astype(bf16)
    pack_parts.start()
    load_cot.wait()
    to_position_major(sh, b1, lanes, cotp)
    gather_v.step(1)
    period()
    pack_parts.wait_recv()
    assemble(FIRST_PART, sh.mats)
    gather_v.step(2)
    period()
    gather_v.step(3)
    gather_v.step(4)
    spread = jnp.zeros((16, width), f32)
    for z in range(sh.depth):
        for i in range(4):
            spread += vall[z, i // 2, i % 2].astype(f32)
    vecs[...] = spread

    key_in, value_in, gate_in = b2, b3, b4
    halo_x.wait_recv()
    got, _ = normalise(halo[0].astype(f32))
    before_one = wrap_before(sh, at, got * vec(MIXER_G) + vec(MIXER_B))

    def blend_one(p, before):
        here = slab(p, segs)
        n1, _ = normalise(xp[here, :].astype(f32))
        one = n1 * vec(MIXER_G) + vec(MIXER_B)
        step = one - before
        key_in[here, :] = (before + step * vec(KEY_SHARE)).astype(bf16)
        value_in[here, :] = (before + step * vec(VALUE_SHARE)).astype(bf16)
        gate_in[here, :] = (before + step * vec(GATE_SHARE)).astype(bf16)
        return one

    before_one = lax.fori_loop(0, span // 2, blend_one, before_one, unroll=8)
    period()
    lax.fori_loop(span // 2, span, blend_one, before_one, unroll=8)
    parks = [local(key_in, key_park, 2), local(value_in, value_park, 3), local(gate_in, gatein_park, 4)]
    for copy in parks:
        copy.start()

    gathered(KEY)
    k[...] = dot(key_in[...], matrix(KEY)).astype(bf16)
    gathered(VALUE)
    v[...] = dot(value_in[...], matrix(VALUE)).astype(bf16)

    rates[...] = jnp.exp(vec(DECAY))
    rate = rates[...]
    keep = jnp.exp(-rate)
    zero = jnp.zeros((segs, width), f32)

    def add_up(p, state):
        a, b, top = state
        here = slab(p, segs)
        key = k[here, :].astype(f32)
        grown = jnp.exp(key)
        top = jnp.maximum(top - rate, key)
        return keep * a + grown * v[here, :].astype(f32), keep * b + grown, top

    sum_num, sum_den, top = lax.fori_loop(
        0, span, add_up, (zero, zero, jnp.full((segs, width), -jnp.inf, f32)), unroll=4
    )
    states = Carry(
        sh, at, True, st_own, st_near, st_whole, st_far, (st_send, st_recv), st_give, st_take
    )
    states.start((sum_num, sum_den))
    tops = Tops(
        sh, at, True, top_own, top_near, top_whole, top_far, (top_send, top_recv)
    )
    gathered(GATE)
    gate = f1
    gate[...] = sigmoid(dot(gate_in[...], matrix(GATE)))
    gate_out = local(gate, gate_park, 5)
    gate_out.start()
    states.after_plane(rates)
    period()
    states.after_z()
    tops.start(top)
    period()
    states.finish()
    carry, total = st_take.at[0], st_take.at[1]

    num, den, res, s2 = f3, f2, f4, f5
    gated, rg, hin, sin = b8, b9, b2, b3
    boost_rate = jnp.exp(vec(FIRST))

    def recur(p, state):
        a, b = state
        here = slab(p, segs)
        grown = jnp.exp(k[here, :].astype(f32))
        value = v[here, :].astype(f32)
        boost = grown * boost_rate
        num[here, :] = a
        den[here, :] = b
        mix = ((a + boost * value) / (b + boost)).astype(bf16).astype(f32)
        gated[here, :] = (gate[here, :] * mix).astype(bf16)
        return keep * a + grown * value, keep * b + grown

    lax.fori_loop(0, span, recur, (carry[0], carry[1]), unroll=4)
    den_out = local(den, den_park, 6)
    den_out.start()
    gathered(OUTPUT)
    res[...] = xp[...].astype(f32) + dot(gated[...], matrix(OUTPUT))

    last = pl.ds(rows - segs, segs)
    n2, _ = normalise(res[last, :])
    halo32[0] = n2 * vec(CHANNEL_G) + vec(CHANNEL_B)
    halo_two = send(halo32.at[0], halo32.at[1], halo_sems, 1, at.ring(1))
    halo_two.start()
    tops.after_plane(rate)
    period()
    for copy in parks:
        copy.wait()

    def blend_two(p, before):
        here = slab(p, segs)
        n2, _ = normalise(res[here, :])
        two = n2 * vec(CHANNEL_G) + vec(CHANNEL_B)
        step = two - before
        hin[here, :] = (before + step * vec(HIDDEN_SHARE)).astype(bf16)
        sin[here, :] = (before + step * vec(SCREEN_SHARE)).astype(bf16)
        return two

    n2, _ = normalise(res[pl.ds(0, segs), :])
    first_two = n2 * vec(CHANNEL_G) + vec(CHANNEL_B)
    lax.fori_loop(1, span, blend_two, first_two, unroll=7)
    halo_two.wait_recv()
    before_two = wrap_before(sh, at, halo32[1])
    blend_two(0, before_two)
    final_top = tops.after_z(rate)
    far = decay_over(rate, float(sh.count * span))
    scale = jnp.exp(-final_top)
    ends = [(far * total[i, : sh.groups] + total[i, sh.groups :]) * scale for i in range(2)]
    lane = lax.rem(width - at.s * (width // sh.count), width)
    ends = pltpu.roll(jnp.concatenate(ends + [final_top], 0), lane, 1)
    ends_out[16:] = ends[:, :128]
    gathered(SCREEN)
    s2[...] = sigmoid(dot(sin[...], matrix(SCREEN)))
    rg[...] = (cotp[...].astype(f32) * s2[...]).astype(bf16)
    gate_out.wait()
    den_out.wait()

    bufs = (core_in, b_in, a_in, z_in)
    started, flying, landed = [], [], []

    def tick():
        period()
        for one in list(flying):
            one.advance()
            if one.done():
                flying.remove(one)
                landed.append(one)

    def scatter(m, result=None):
        number = len(started)
        one = Scatter(
            at, w, m, bufs, (rs_send, rs_recv), number, final, grads,
            m if result is None else result,
        )
        started.append(one)
        flying.append(one)
        tick()

    def all_sent(number):
        one = started[number]
        while not one.done():
            tick()
        landed.remove(one)
        one.sent()

    ret, hb, act, hg = f1, f2, b4, b1
    tiles = [(j, slice(j * 128, (j + 1) * 128)) for j in range(width // 128)]
    for c in range(sh.parts):
        into, back = FIRST_PART + 2 * c, FIRST_PART + 2 * c + 1
        gathered(into)
        up = jnp.maximum(dot(hin[...], matrix(into)), 0.0)
        for j, columns in tiles:
            lanes[j] = up[:, columns]
        act[...] = (up * up).astype(bf16)
        gathered(back)
        if c == 0:
            ret[...] = dot(act[...], matrix(back))
        else:
            ret[...] += dot(act[...], matrix(back))
        relu = jnp.concatenate([lanes[j] for j, _ in tiles], 1)
        hg[...] = (dot_nt(rg[...], matrix(back)) * (2.0 * relu)).astype(bf16)
        gathers[back].sent()
        set_matrix(back, dot_tn(act[...], rg[...]))
        scatter(back, FIRST_PART + c)
        if c == 0:
            hb[...] = dot_nt(hg[...], matrix(into))
        else:
            hb[...] += dot_nt(hg[...], matrix(into))
        gathers[into].sent()
        set_matrix(into, dot_tn(hin[...], hg[...]))
        scatter(into, FIRST_PART + sh.parts + c)

    sg, sb, og = b4, f5, b1
    first = pl.ds(0, segs)
    cot0 = cotp[first, :].astype(f32)
    sg0 = (cot0 * ret[first, :] * s2[first, :] * (1.0 - s2[first, :])).astype(bf16)
    sb0 = dot_nt(sg0, matrix(SCREEN))
    halo32[2] = hb[first, :] * (1.0 - vec(HIDDEN_SHARE)) + sb0 * (1.0 - vec(SCREEN_SHARE))
    back_two = send(halo32.at[2], halo32.at[3], halo_sems, 2, at.ring(-1))
    back_two.start()
    load_gatein = local(gatein_park, b2, 7)
    load_gatein.start()
    acc[...] = jnp.zeros_like(acc)

    def finish(p, _):
        here = slab(p, segs)
        s = s2[here, :]
        held = ret[here, :]
        put_in_sequence_order(sh, p, res[here, :] + s * held, lanes)
        sg[here, :] = (cotp[here, :].astype(f32) * held * s * (1.0 - s)).astype(bf16)
        return 0

    lax.fori_loop(0, span, finish, 0, unroll=4)
    sb[...] = dot_nt(sg[...], matrix(SCREEN))
    tick()
    for j, columns in tiles:
        b9[:, columns] = lanes[j].astype(bf16)
    out_copy = local(b9, out_hbm, 12)
    out_copy.start()

    rgrad = f1

    def back_second(p, before, ahead):
        here = slab(p, segs)
        n2, inverse = normalise(res[here, :])
        two = n2 * vec(CHANNEL_G) + vec(CHANNEL_B)
        step = two - before
        hb_here, sb_here = hb[here, :], sb[here, :]
        acc[0] += hb_here * step
        acc[1] += sb_here * step
        grad = hb_here * vec(HIDDEN_SHARE) + sb_here * vec(SCREEN_SHARE) + ahead
        acc[2] += grad * n2
        acc[3] += grad
        down = cotp[here, :].astype(f32) + norm_back(grad, n2, inverse, vec(CHANNEL_G))
        rgrad[here, :] = down
        og[here, :] = down.astype(bf16)
        return two

    def back_second_step(p, before):
        there = slab(p + 1, segs)
        ahead = hb[there, :] * (1.0 - vec(HIDDEN_SHARE)) + sb[there, :] * (1.0 - vec(SCREEN_SHARE))
        return back_second(p, before, ahead)

    before = lax.fori_loop(0, span - 1, back_second_step, before_two, unroll=7)
    back_two.wait_recv()
    back_second(span - 1, before, wrap_after(sh, at, halo32[3]))
    out_copy.wait()
    load_gate = local(gate_park, f2, 8)
    load_gate.start()
    load_den = local(den_park, f5, 9)
    load_den.start()
    tick()
    gated_grad = f4
    gated_grad[...] = dot_nt(og[...], matrix(OUTPUT))
    load_gate.wait()
    load_den.wait()

    gate, den, gate_grad, mg = f2, f5, b9, cotp

    def totals_back(i, state):
        a, b = state
        here = slab(span - 1 - i, segs)
        grown = jnp.exp(k[here, :].astype(f32))
        value = v[here, :].astype(f32)
        boost = grown * boost_rate
        over = 1.0 / (den[here, :] + boost)
        raw = (num[here, :] + boost * value) * over
        mix = raw.astype(bf16).astype(f32)
        grad, s = gated_grad[here, :], gate[here, :]
        through = (grad * s).astype(bf16)
        mg[here, :] = through
        gate_grad[here, :] = (grad * mix * s * (1.0 - s)).astype(bf16)
        num_grad = through.astype(f32) * over
        return keep * a + num_grad, keep * b - num_grad * raw

    sum_num, sum_den = lax.fori_loop(0, span, totals_back, (zero, zero), unroll=4)
    adjoints = Carry(
        sh, at, False, bk_own, bk_near, bk_whole, bk_far, (bk_send, bk_recv), bk_give, bk_take
    )
    adjoints.start((sum_num, sum_den))
    gathers[OUTPUT].sent()
    set_matrix(OUTPUT, dot_tn(gated[...], og[...]))
    scatter(OUTPUT)
    adjoints.after_plane(rates)
    gathers[SCREEN].sent()
    set_matrix(SCREEN, dot_tn(sin[...], sg[...]))
    scatter(SCREEN)
    load_keyin = local(key_park, b3, 10)
    load_keyin.start()
    load_valin = local(value_park, b4, 11)
    load_valin.start()
    adjoints.after_z()
    gate_back = f4
    gate_back[...] = dot_nt(gate_grad[...], matrix(GATE))
    load_gatein.wait()
    gathers[GATE].sent()
    set_matrix(GATE, dot_tn(b2[...], gate_grad[...]))
    scatter(GATE)
    adjoints.finish()
    carry = bk_take.at[0]

    kg, vg = b8, b1

    def recur_back(i, state):
        a, b = state
        here = slab(span - 1 - i, segs)
        grown = jnp.exp(k[here, :].astype(f32))
        value = v[here, :].astype(f32)
        boost = grown * boost_rate
        n, d = num[here, :], den[here, :]
        over = 1.0 / (d + boost)
        num_grad = mg[here, :].astype(f32) * over
        den_grad = -num_grad * ((n + boost * value) * over)
        inner = boost * (value * num_grad + den_grad)
        kg[here, :] = (grown * (value * a + b) + inner).astype(bf16)
        vg[here, :] = (grown * a + boost * num_grad).astype(bf16)
        acc[4] += inner
        acc[5] += n * a + d * b
        return keep * a + num_grad, keep * b + den_grad

    lax.fori_loop(0, span, recur_back, (carry[0], carry[1]), unroll=4)
    def line(i):
        return jnp.sum(acc[i], 0, keepdims=True)

    early = Total(at, sum_held, sum_near, sum_far, (sum_send, sum_recv))
    early.start([-rate * keep * line(5)] + [line(i) for i in (4, 2, 3, 0, 1)])
    load_keyin.wait()
    load_valin.wait()
    spare = FIRST_PART
    all_sent(1)
    set_matrix(spare, dot_tn(b3[...], kg[...]))
    scatter(spare, KEY)
    all_sent(0)
    set_matrix(spare + 1, dot_tn(b4[...], vg[...]))
    scatter(spare + 1, VALUE)

    key_back, value_back = f2, f3
    key_back[...] = dot_nt(kg[...], matrix(KEY))
    value_back[...] = dot_nt(vg[...], matrix(VALUE))

    def ahead_of(where):
        return (
            key_back[where, :] * (1.0 - vec(KEY_SHARE))
            + value_back[where, :] * (1.0 - vec(VALUE_SHARE))
            + gate_back[where, :] * (1.0 - vec(GATE_SHARE))
        )

    early.after_core()
    halo32[4] = ahead_of(first)
    back_one = send(halo32.at[4], halo32.at[5], halo_sems, 3, at.ring(-1))
    back_one.start()
    tick()
    got, _ = normalise(halo[0].astype(f32))
    before_one = wrap_before(sh, at, got * vec(MIXER_G) + vec(MIXER_B))

    def back_first(p, before, ahead):
        here = slab(p, segs)
        n1, inverse = normalise(xp[here, :].astype(f32))
        one = n1 * vec(MIXER_G) + vec(MIXER_B)
        step = one - before
        kb, vb, gb = key_back[here, :], value_back[here, :], gate_back[here, :]
        acc[6] += kb * step
        acc[7] += vb * step
        acc[8] += gb * step
        grad = kb * vec(KEY_SHARE) + vb * vec(VALUE_SHARE) + gb * vec(GATE_SHARE) + ahead
        acc[9] += grad * n1
        acc[10] += grad
        down = rgrad[here, :] + norm_back(grad, n1, inverse, vec(MIXER_G))
        put_in_sequence_order(sh, p, down, lanes)
        return one

    def back_first_step(p, before):
        return back_first(p, before, ahead_of(slab(p + 1, segs)))

    middle = (span - 1) // 3
    before = lax.fori_loop(0, middle, back_first_step, before_one, unroll=7)
    tick()
    before = lax.fori_loop(middle, 2 * middle, back_first_step, before, unroll=7)
    tick()
    before = lax.fori_loop(2 * middle, span - 1, back_first_step, before, unroll=7)
    back_one.wait_recv()
    back_first(span - 1, before, wrap_after(sh, at, halo32[5]))
    ig_copies = [
        pltpu.make_async_copy(lanes.at[j], ig_hbm.at[:, columns], emit_sem.at[j])
        for j, columns in tiles
    ]
    for copy in ig_copies:
        copy.start()

    late = Total(at, late_held, late_near, late_far, (late_send, late_recv))
    early.after_plane()
    late.start([line(i) for i in (9, 10, 6, 7, 8)])
    tick()
    spread_units(sh, b9)
    while not started[2 * sh.parts - 1].done():
        tick()
    late.after_core()
    join_units(
        sh, [grads[FIRST_PART + sh.parts + c] for c in range(sh.parts)], b9, hidden_out
    )
    for c in range(sh.parts):
        return_out[c * sh.own : (c + 1) * sh.own] = grads[FIRST_PART + c]
    late.after_plane()
    tick()

    def own_lanes(total):
        return pltpu.roll(total, lax.rem(width - turn, width), 1)[:, :128]

    ends_out[:8] = own_lanes(early.result())
    ends_out[8:16] = own_lanes(late.result())
    for copy in ig_copies:
        copy.wait()
    while flying:
        tick()
    for m in (KEY, VALUE, GATE, OUTPUT, SCREEN):
        squares_out[m] = grads[m]

    for copy in (pack_vectors, pack_squares, pack_parts):
        copy.wait_send()
    halo_x.wait_send()
    for copy in (halo_two, back_two, back_one):
        copy.wait_send()
    gather_v.sent()
    gathers[KEY].sent()
    gathers[VALUE].sent()
    for one in landed:
        one.sent()
    for exchange in (states, tops, adjoints, early, late):
        exchange.sent()


def layer(sh, tokens, cotangent, matrices, vectors):
    R, D, S, Z = sh.rows, sh.width, sh.segs, sh.depth
    shape = jax.ShapeDtypeStruct
    narrow, wide = ((R, D), bf16), ((R, D), f32)
    w_shape = (sh.mats, Z, 2, 2, sh.chip, D)
    V = pltpu.VMEM
    dma = pltpu.SemaphoreType.DMA
    anywhere, in_vmem = pl.BlockSpec(memory_space=pl.ANY), pl.BlockSpec(memory_space=pltpu.VMEM)
    outs = [
        (narrow, anywhere), (wide, anywhere), (((FIRST_PART, sh.own, D), f32), in_vmem),
        (((sh.parts * sh.own, D), f32), in_vmem), (((sh.own, sh.inner), f32), in_vmem),
        (((16 + 3 * sh.groups, 128), f32), in_vmem),
        (wide, anywhere), (wide, anywhere), (narrow, anywhere), (narrow, anywhere),
        (narrow, anywhere),
    ]
    scratch = (
        [
            V(w_shape, bf16), V((Z, 2, 2, 16, D), bf16), V((16, D), f32), V((1, D), f32),
            V((sh.mats + 1, 32, D), bf16), V((sh.mats + 1, 32, sh.half), bf16), V((D // 128, R, 128), f32),
        ]
        + [V(*wide)] * 5
        + [V(*narrow)] * 10
        + [
            V((1, S, D), bf16), V((6, S, D), f32),
            V((2, S, D), f32), V((3, S, sh.half), f32), V((S, sh.half), f32),
            V((Z - 1, S, sh.half), f32), V((3, 2, S, sh.half), f32), V((2, 2, S, D), f32),
            V((2, S, D), f32), V((3, S, sh.half), f32), V((S, sh.half), f32),
            V((Z - 1, S, sh.half), f32), V((3, 1, S, sh.half), f32), V((1, 2, S, D), f32),
            V((S, D), f32), V((3, S, D), f32), V((S, D), f32), V((Z - 1, S, D), f32),
            V((VECTORS, S, D), f32),
            V((4, 8, D), f32), V((3, 8, D), f32), V((Z - 1, 8, D), f32),
            V((4, 8, D), f32), V((3, 8, D), f32), V((Z - 1, 8, D), f32),
            V((sh.mats, sh.own, D), f32),
            V((HELD[0], Z, 2, 2, sh.chip, sh.half), bf16), V((HELD[1], Z, 2, sh.chip, sh.half), bf16),
            V((HELD[2], Z, sh.chip, sh.half), bf16), V((HELD[3], Z - 1, sh.chip, sh.half), bf16),
            V((sh.mats, sh.own, sh.half), f32),
            dma((13,)), dma((2, 3)),
        ]
        + [dma((sh.mats + 1, Z + 2))] * 2
        + [dma((Z + 5,))] * 6
        + [dma((4,))] * 2
        + [dma((sh.mats, Z + 3))] * 2
        + [dma((Z + 3,))] * 4
        + [dma((D // 128,))]
    )
    return pl.pallas_call(
        functools.partial(layer_kernel, sh),
        out_shape=[shape(s, t) for (s, t), _ in outs],
        in_specs=[anywhere, anywhere] + [in_vmem] * (len(matrices) + len(vectors)),
        out_specs=[spec for _, spec in outs],
        scratch_shapes=scratch,
        compiler_params=pltpu.CompilerParams(
            collective_id=0, has_side_effects=True, vmem_limit_bytes=63 * 2**20
        ),
    )(
        tokens.reshape(R, D), cotangent.reshape(R, D), *matrices,
        *[vector.reshape(1, sh.own) for vector in vectors],
    )


def mm(left, right):
    return jnp.dot(left, right, preferred_element_type=f32)


def mm_nt(left, right):
    return lax.dot_general(left, right, (((1,), (1,)), ((), ())), preferred_element_type=f32)


def mm_tn(left, right):
    return lax.dot_general(left, right, (((0,), (0,)), ((), ())), preferred_element_type=f32)


def ring(value, steps):
    count = lax.axis_size("seq")
    return lax.ppermute(value, "seq", [(i, (i + steps) % count) for i in range(count)])


def entering(last, spot):
    got = ring(last, 1)
    pairs = got.reshape(-1, 2, got.shape[-1])
    wrapped = jnp.concatenate([jnp.zeros_like(pairs[:, :1]), pairs[:, :1]], 1)
    return jnp.where(spot == 0, wrapped, pairs).reshape(got.shape)


def leaving(first, spot):
    count = lax.axis_size("seq")
    got = ring(first, -1)
    pairs = got.reshape(-1, 2, got.shape[-1])
    wrapped = jnp.concatenate([pairs[:, 1:], jnp.zeros_like(pairs[:, :1])], 1)
    return jnp.where(spot == count - 1, wrapped, pairs).reshape(got.shape)


def plain_scan(k_ref, v_ref, carry_ref, decay_ref, first_ref, num_ref, den_ref, mix_ref):
    keep = jnp.exp(-jnp.exp(decay_ref[...]))
    boost_rate = jnp.exp(first_ref[...])

    def step(t, state):
        num, den = state
        k = jnp.exp(k_ref[t].astype(f32))
        v = v_ref[t].astype(f32)
        boost = k * boost_rate
        num_ref[t] = num
        den_ref[t] = den
        mix_ref[t] = (num + boost * v) / (den + boost)
        return keep * num + k * v, keep * den + k

    lax.fori_loop(0, k_ref.shape[0], step, (carry_ref[0], carry_ref[1]))


def plain_scan_back(
    k_ref, v_ref, num_ref, den_ref, mix_ref, grad_ref, carry_ref, decay_ref, first_ref,
    kg_ref, vg_ref, first_grad_ref, decay_grad_ref,
):
    keep = jnp.exp(-jnp.exp(decay_ref[...]))
    boost_rate = jnp.exp(first_ref[...])
    length = k_ref.shape[0]

    def step(i, state):
        adj_num, adj_den, first_sum, decay_sum = state
        t = length - 1 - i
        k = jnp.exp(k_ref[t].astype(f32))
        v = v_ref[t].astype(f32)
        boost = k * boost_rate
        num_grad = grad_ref[t].astype(f32) / (den_ref[t] + boost)
        den_grad = -num_grad * mix_ref[t]
        inner = boost * (v * num_grad + den_grad)
        kg_ref[t] = (k * (v * adj_num + adj_den) + inner).astype(bf16)
        vg_ref[t] = (k * adj_num + boost * num_grad).astype(bf16)
        first_sum = first_sum + inner
        decay_sum = decay_sum + num_ref[t] * adj_num + den_ref[t] * adj_den
        return keep * adj_num + num_grad, keep * adj_den + den_grad, first_sum, decay_sum

    zero = jnp.zeros_like(carry_ref[0])
    out = lax.fori_loop(0, length, step, (carry_ref[0], carry_ref[1], zero, zero))
    first_grad_ref[...] = out[2]
    decay_grad_ref[...] = out[3]


def call(kernel, shapes, *operands):
    space = pl.BlockSpec(memory_space=pltpu.VMEM)
    return pl.pallas_call(
        kernel,
        out_shape=[jax.ShapeDtypeStruct(s, t) for s, t in shapes],
        in_specs=[space] * len(operands),
        out_specs=[space] * len(shapes),
        compiler_params=pltpu.CompilerParams(vmem_limit_bytes=48 * 2**20),
    )(*operands)


def plain_body(
    tokens, mixer_gain, mixer_bias, key_blend, value_blend, gate_blend, time_decay, time_first,
    key_weight, value_weight, gate_weight, output_weight, channel_gain, channel_bias,
    hidden_blend, screen_blend, hidden_weight, screen_weight, return_weight, cotangent,
):
    groups, stretches, span, width = tokens.shape
    count = lax.axis_size("seq")
    owners = count * lax.axis_size("rep")
    spot = lax.axis_index("seq")
    segs = groups * stretches
    rows = span * segs
    own = width // owners
    inner = hidden_weight.shape[1]
    parts = inner // width

    vectors = (
        mixer_gain, mixer_bias, key_blend, value_blend, gate_blend, time_decay, time_first,
        channel_gain, channel_bias, hidden_blend, screen_blend,
    )
    squares = (key_weight, value_weight, gate_weight, output_weight, screen_weight)
    packed = jnp.concatenate(
        squares + (hidden_weight.reshape(own * parts, width), return_weight), 0
    )
    packed = lax.all_gather(packed, both, axis=0)
    spread_vectors = lax.all_gather(jnp.stack(vectors), both, axis=0)
    spread_vectors = jnp.swapaxes(spread_vectors, 0, 1).reshape(len(vectors), width).astype(f32)
    (
        mixer_g, mixer_b, key_share, value_share, gate_share, decay_log, first_log,
        channel_g, channel_b, hidden_share, screen_share,
    ) = [spread_vectors[i][None] for i in range(len(vectors))]

    def piece(start, size, shape):
        return packed[:, start : start + size].reshape(shape)

    w_key, w_value, w_gate, w_output, w_screen = [
        piece(own * i, own, (width, width)) for i in range(5)
    ]
    w_hidden = piece(own * 5, own * parts, (width, inner))
    w_return = piece(own * (5 + parts), own * parts, (inner, width))

    def position_major(a):
        return jnp.transpose(a, (2, 0, 1, 3)).reshape(rows, width)

    def shifted(a, first):
        return jnp.concatenate([first, a[:-segs]], 0)

    x = position_major(tokens).astype(f32)
    n1, inv1 = normalise(x)
    one = n1 * mixer_g + mixer_b
    before = shifted(one, entering(one[-segs:], spot))
    spread_one = one - before
    key_in = (before + spread_one * key_share).astype(bf16)
    value_in = (before + spread_one * value_share).astype(bf16)
    gate_in = (before + spread_one * gate_share).astype(bf16)
    k = mm(key_in, w_key).astype(bf16)
    v = mm(value_in, w_value).astype(bf16)
    gate = jax.nn.sigmoid(mm(gate_in, w_gate))

    rate = jnp.exp(decay_log)
    cube = (span, segs, width)
    offsets = jnp.arange(span, dtype=f32)[:, None, None]
    kw = k.reshape(cube).astype(f32)
    vw = v.reshape(cube).astype(f32)
    shifted_key = kw - (span - 1.0 - offsets) * rate
    ends = jnp.exp(shifted_key)
    totals = jnp.stack([jnp.sum(ends * vw, 0), jnp.sum(ends, 0)])
    tops = jnp.max(shifted_key, 0)
    everyone = lax.all_gather(jnp.concatenate([totals, tops[None]]), "seq", axis=0)
    everyone = everyone.reshape(count, 3, groups, stretches, width)
    everyone = jnp.transpose(everyone, (3, 0, 1, 2, 4)).reshape(
        stretches * count, 3, groups, width
    )
    order = jnp.arange(stretches * count, dtype=f32)

    def weights_for(here):
        gap = here - 1.0 - order[:, None]
        return jnp.where(gap >= 0, jnp.exp(-jnp.maximum(gap, 0.0) * (span * rate)), 0.0)

    def carried(here):
        return jnp.sum(weights_for(here)[:, None, None, :] * everyone[:, :2], 0)

    carry = jnp.stack([carried(j * count + spot.astype(f32)) for j in range(stretches)], 2)
    carry = carry.reshape(2, segs, width)
    final = carried(float(stretches * count))
    far = (stretches * count - 1.0 - order)[:, None] * (span * rate)
    top = jnp.max(everyone[:, 2] - far[:, None, :], 0)
    slab = width // count

    def own_slab(a):
        return lax.dynamic_slice_in_dim(a, spot * slab, slab, 1)

    final_top = own_slab(top)
    scaling = jnp.exp(-final_top)
    final_num = own_slab(final[0]) * scaling
    final_den = own_slab(final[1]) * scaling

    num, den, mix_raw = call(
        plain_scan, [(cube, f32)] * 3, k.reshape(cube), v.reshape(cube), carry,
        decay_log, first_log,
    )
    mix = mix_raw.reshape(rows, width).astype(bf16).astype(f32)
    gated = (gate * mix).astype(bf16)
    residual = x + mm(gated, w_output)
    n2, inv2 = normalise(residual)
    two = n2 * channel_g + channel_b
    before = shifted(two, entering(two[-segs:], spot))
    spread_two = two - before
    hidden_in = (before + spread_two * hidden_share).astype(bf16)
    screen_in = (before + spread_two * screen_share).astype(bf16)
    screen = jax.nn.sigmoid(mm(screen_in, w_screen))
    cot = position_major(cotangent).astype(f32)
    returned_grad = (cot * screen).astype(bf16)
    relu = jnp.maximum(mm(hidden_in, w_hidden), 0.0)
    act = jnp.square(relu).astype(bf16)
    returned = mm(act, w_return)
    output = (residual + screen * returned).astype(bf16)

    screen_grad = (cot * returned * screen * (1.0 - screen)).astype(bf16)
    hidden_grad = (mm_nt(returned_grad, w_return) * (2.0 * relu)).astype(bf16)
    dw_return = mm_tn(act, returned_grad)
    dw_hidden = mm_tn(hidden_in, hidden_grad)
    dw_screen = mm_tn(screen_in, screen_grad)
    hidden_back = mm_nt(hidden_grad, w_hidden)
    screen_back = mm_nt(screen_grad, w_screen)
    d_hidden_blend = jnp.sum(hidden_back * spread_two, 0)
    d_screen_blend = jnp.sum(screen_back * spread_two, 0)
    ahead = hidden_back * (1.0 - hidden_share) + screen_back * (1.0 - screen_share)
    two_grad = (
        hidden_back * hidden_share
        + screen_back * screen_share
        + jnp.concatenate([ahead[segs:], leaving(ahead[:segs], spot)], 0)
    )
    d_channel_gain = jnp.sum(two_grad * n2, 0)
    d_channel_bias = jnp.sum(two_grad, 0)
    residual_grad = cot + norm_back(two_grad, n2, inv2, channel_g)
    output_grad = residual_grad.astype(bf16)
    dw_output = mm_tn(gated, output_grad)
    gated_grad = mm_nt(output_grad, w_output)
    mix_grad = (gated_grad * gate).astype(bf16)
    gate_grad = (gated_grad * mix * gate * (1.0 - gate)).astype(bf16)

    boost = jnp.exp(first_log + kw)
    num_grad = mix_grad.reshape(cube).astype(f32) / (den + boost)
    den_grad = -num_grad * mix_raw
    fade = jnp.exp(-offsets * rate)
    totals = jnp.stack([jnp.sum(fade * num_grad, 0), jnp.sum(fade * den_grad, 0)])
    everyone = lax.all_gather(totals, "seq", axis=0)
    everyone = everyone.reshape(count, 2, groups, stretches, width)
    everyone = jnp.transpose(everyone, (3, 0, 1, 2, 4)).reshape(
        stretches * count, 2, groups, width
    )

    def carried_back(here):
        gap = order[:, None] - here - 1.0
        scale = jnp.where(gap >= 0, jnp.exp(-jnp.maximum(gap, 0.0) * (span * rate)), 0.0)
        return jnp.sum(scale[:, None, None, :] * everyone, 0)

    carry = jnp.stack([carried_back(j * count + spot.astype(f32)) for j in range(stretches)], 2)
    carry = carry.reshape(2, segs, width)
    key_grad, value_grad, first_sum, decay_sum = call(
        plain_scan_back, [(cube, bf16)] * 2 + [((segs, width), f32)] * 2,
        k.reshape(cube), v.reshape(cube), num, den, mix_raw, mix_grad.reshape(cube), carry,
        decay_log, first_log,
    )
    key_grad = key_grad.reshape(rows, width)
    value_grad = value_grad.reshape(rows, width)
    d_first = jnp.sum(first_sum, 0)
    d_decay = -rate[0] * jnp.exp(-rate[0]) * jnp.sum(decay_sum, 0)
    dw_key = mm_tn(key_in, key_grad)
    dw_value = mm_tn(value_in, value_grad)
    dw_gate = mm_tn(gate_in, gate_grad)
    key_back = mm_nt(key_grad, w_key)
    value_back = mm_nt(value_grad, w_value)
    gate_back = mm_nt(gate_grad, w_gate)
    d_key_blend = jnp.sum(key_back * spread_one, 0)
    d_value_blend = jnp.sum(value_back * spread_one, 0)
    d_gate_blend = jnp.sum(gate_back * spread_one, 0)
    ahead = (
        key_back * (1.0 - key_share)
        + value_back * (1.0 - value_share)
        + gate_back * (1.0 - gate_share)
    )
    one_grad = (
        key_back * key_share
        + value_back * value_share
        + gate_back * gate_share
        + jnp.concatenate([ahead[segs:], leaving(ahead[:segs], spot)], 0)
    )
    d_mixer_gain = jnp.sum(one_grad * n1, 0)
    d_mixer_bias = jnp.sum(one_grad, 0)
    input_grad = residual_grad + norm_back(one_grad, n1, inv1, mixer_g)

    packed = jnp.concatenate(
        [d.reshape(owners, own, width).astype(bf16) for d in (dw_key, dw_value, dw_gate, dw_output, dw_screen)]
        + [
            dw_hidden.reshape(owners, own * parts, width).astype(bf16),
            dw_return.reshape(owners, own * parts, width).astype(bf16),
        ],
        1,
    )
    summed = lax.psum_scatter(packed, both, scatter_dimension=0).astype(f32)
    small = jnp.stack(
        [
            d_mixer_gain, d_mixer_bias, d_key_blend, d_value_blend, d_gate_blend, d_decay, d_first,
            d_channel_gain, d_channel_bias, d_hidden_blend, d_screen_blend,
        ]
    )
    small = lax.psum(small, both)
    place = (spot * lax.axis_size("rep") + lax.axis_index("rep")) * own
    small = lax.dynamic_slice_in_dim(small, place, own, 1)

    def batch_major(a):
        return jnp.transpose(a.reshape(span, groups, stretches, width), (1, 2, 0, 3))

    return (
        batch_major(output),
        batch_major(input_grad),
        final_num,
        final_den,
        final_top,
        *[small[i] for i in range(7)],
        *[summed[own * i : own * (i + 1)] for i in range(4)],
        *[small[i] for i in range(7, 11)],
        summed[own * 5 : own * (5 + parts)].reshape(own, inner),
        summed[own * 4 : own * 5],
        summed[own * (5 + parts) :],
    )


def fused_body(sh, *args):
    (
        tokens, mixer_gain, mixer_bias, key_blend, value_blend, gate_blend, time_decay, time_first,
        key_weight, value_weight, gate_weight, output_weight, channel_gain, channel_bias,
        hidden_blend, screen_blend, hidden_weight, screen_weight, return_weight, cotangent,
    ) = args
    vectors = (
        mixer_gain, mixer_bias, key_blend, value_blend, gate_blend, time_decay, time_first,
        channel_gain, channel_bias, hidden_blend, screen_blend,
    )
    matrices = (
        key_weight, value_weight, gate_weight, output_weight, screen_weight, hidden_weight,
        return_weight,
    )
    output, input_grad, squares, back, hidden, ends = layer(
        sh, tokens, cotangent, matrices, vectors
    )[:6]
    share, groups = sh.width // sh.count, sh.groups
    late = [ends[8 + i, : sh.own] for i in range(DECAY)]
    early = [ends[i, : sh.own] for i in range(VECTORS - DECAY)]
    return (
        output.reshape(tokens.shape),
        input_grad.reshape(tokens.shape),
        *[ends[16 + groups * i : 16 + groups * (i + 1), :share] for i in range(3)],
        *late,
        *early[:2],
        *[squares[i] for i in (KEY, VALUE, GATE, OUTPUT)],
        *early[2:],
        hidden,
        squares[SCREEN],
        back,
    )


def body(*args):
    tokens, hidden_weight = args[0], args[16]
    groups, stretches, span, width = tokens.shape
    sh = Shape(lax.axis_size("seq"), span, groups, stretches, width, hidden_weight.shape[1])
    if lax.axis_size("rep") == 2 and sh.fits():
        return fused_body(sh, *args)
    return plain_body(*args)


def solution(mesh):
    rows = P("rep", None, "seq", None)
    owned = P(both)
    owned_rows = P(both, None)
    in_specs = (rows,) + (owned,) * 7 + (owned_rows,) * 4 + (owned,) * 4 + (owned_rows,) * 3 + (rows,)
    out_specs = (
        (rows,) * 2 + (P("rep", "seq"),) * 3 + (owned,) * 7 + (owned_rows,) * 4
        + (owned,) * 4 + (owned_rows,) * 3
    )
    return jax.shard_map(body, mesh=mesh, in_specs=in_specs, out_specs=out_specs, check_vma=False)
```
